32 devices in a mesh: groups: 2 (over y), dp: 4 (over z), heads: 4 (over x, core).
Axes of the slice: x: 2, y: 2, z: 4, core: 2. Of those that a mesh axis runs over, the one named last changes fastest.
Arguments:
- queries: bfloat16 [2048, 64, 128], P(('groups', 'dp'), 'heads'), parts along dimension 0, may hold values from -41 to 41
- out_grad: bfloat16 [2048, 64, 128], P(('groups', 'dp'), 'heads'), parts along dimension 0, may hold values from -24 to 24
- self_keys: bfloat16 [2048, 8, 128], P(('groups', 'dp'), 'heads'), parts along dimension 0, may hold values from -6 to 6
- self_values: bfloat16 [2048, 8, 128], P(('groups', 'dp'), 'heads'), parts along dimension 0, may hold values from -6 to 6
- cart_keys: bfloat16 [2048, 8, 128], P('groups', 'heads'), parts along dimension 0, may hold values from -17 to 17
- cart_values: bfloat16 [2048, 8, 128], P('groups', 'heads'), parts along dimension 0, may hold values from -6 to 6
- segment_ids: int32 [8, 256], P(('groups', 'dp')), parts along dimension 0, may hold values from 0 to 1, never falling along the last dimension, each value on 1 to 192 neighbouring positions
Outputs:
- cart_grads: float32 [2048, 2, 8, 128], P(('groups', 'dp'), None, 'heads'), parts along dimension 0
- self_grads: bfloat16 [2, 2048, 8, 128], P(None, ('groups', 'dp'), 'heads'), parts along dimension 1
- query_grads: bfloat16 [2048, 8192], P(('groups', 'dp', 'heads')), parts along dimension 0
The draws below stay inside these ranges and needn't reach their ends.
There are 2 independent parts, one for each index of `groups`. The reference program is written for one: setup_inputs(seed, part) draws one part's arguments, and reference() takes and returns one part's arrays. A program takes and returns all parts, laid end to end along the dimension named above; each array names one. Nothing has to cross between parts.
Inputs may be any that keep to these rules, and one draw needn't show every extreme that they name: `segment_ids`: in each row ids never fall and both sequences occur; one sequence of a row may hold up to 192 positions.
All inputs are finite; a program needn't handle non-finite values.
Results may differ from the reference program's by a relative error of at most 0.0053.
Values may be sent and summed in bfloat16 or wider, within the bound.
No kernel may reach another device: no remote copies, remote signals or barrier semaphores. Data moves between devices by JAX's collectives and lax.ppermute only.
A program may use at most 64 MiB of HBM per device.

```python
import math
import jax
import jax.numpy as jnp
import numpy as np
from jax import lax

H = 64
KVH = 8
DH = 128
TOK = 256
P_SIZE = 1024
ROWS = 4
TOKENS = 1024


def cart_table(key):
    normal_part = jnp.clip(jax.random.normal(jax.random.fold_in(key, 11), (P_SIZE, KVH, DH), jnp.float32), -4.0, 4.0)
    return normal_part


def draw_cart_keys(key, part):
    return cart_table(key).astype(jnp.bfloat16)


def draw_queries(key, part):
    normal_part = jnp.clip(jax.random.normal(jax.random.fold_in(key, 12), (TOKENS, H, DH), jnp.float32), -4.0, 4.0)
    return normal_part.astype(jnp.bfloat16)


def steps_of(stream_key, shape, split, least, top_value):
    gain, own = 1.0, jax.random.fold_in(stream_key, 6)
    for axis_at, parts in split:
        steps = jnp.exp(jax.random.uniform(jax.random.fold_in(own, axis_at), (parts,), jnp.float32, least / len(split), top_value / len(split)))
        gain = gain * jnp.repeat(steps, shape[axis_at] // parts).reshape([-1 if axis == axis_at else 1 for axis in range(len(shape))])
    return gain


def split_up(amount, total, limit, slope):
    loads = [(1 << 20) // math.isqrt(grade ** slope) + 1 for grade in range(2, amount + 1)]
    rest, counts = total - limit - (amount - 1), [1] * (amount - 1)
    while rest > 0:
        free = [i for i in range(amount - 1) if counts[i] < limit]
        pool, remaining = sum([loads[i] for i in free]), rest
        for i in free:
            more = min(limit - counts[i], max(1, remaining * loads[i] // pool), rest)
            counts[i] = counts[i] + more
            rest = rest - more
    return np.array([limit] + counts)


def uneven(stream_key, amount, total, bound, skew):
    if amount == 2:
        one = jax.random.randint(stream_key, (), max(1, total - bound), min(bound, total - 1) + 1)
        return jnp.stack([one, total - one])
    lengths = jnp.asarray(split_up(amount, total, bound, skew), jnp.int32)
    twos = (amount - 1) // 2
    giver, sink = lengths[1:1 + 2 * twos:2], lengths[2:2 + 2 * twos:2]
    room = jnp.minimum(giver - 1, bound - sink)
    moved = jax.random.randint(jax.random.fold_in(stream_key, 1), (twos,), 0, 1 << 20) % (room + 1)
    lengths = lengths.at[1:1 + 2 * twos:2].set(giver - moved).at[2:2 + 2 * twos:2].set(sink + moved)
    return lengths[jax.random.permutation(jax.random.fold_in(stream_key, 2), amount)]


def scatter_about(own_key, shape, scale, limit, cuts=(), dtype=jnp.bfloat16):
    drawn = scale * jax.random.normal(own_key, shape, jnp.float32)
    if cuts:
        drawn = drawn * steps_of(own_key, shape, cuts, -0.22, 0.18)
    return jnp.clip(drawn, -limit, limit).astype(dtype)


def setup_inputs(seed: int = 0, part: int = 0) -> dict:
    splits = jax.random.split(jax.random.key(seed), 8)
    own_keys = jax.random.split(jax.random.fold_in(splits[7], part), 8)
    queries = draw_queries(jax.random.fold_in(jax.random.fold_in(splits[7], part), 71), part)
    out_grad = scatter_about(own_keys[1], (TOKENS, H, DH), 4.0, 24.0, ((0, 4), (1, 4)))
    self_keys = scatter_about(own_keys[2], (TOKENS, KVH, DH), 1.0, 6.0, ((0, 4), (1, 4)))
    self_values = scatter_about(own_keys[3], (TOKENS, KVH, DH), 1.0, 6.0, ((0, 4), (1, 4)))
    cart_keys = draw_cart_keys(jax.random.fold_in(jax.random.fold_in(splits[7], part), 71), part)
    cart_values = scatter_about(own_keys[5], (P_SIZE, KVH, DH), 1.0, 6.0, ((1, 4),))
    segment_ids = jax.vmap(lambda own: jnp.searchsorted(jnp.cumsum(uneven(own, 2, TOK, TOK * 3 // 4, 0)), jnp.arange(TOK), side="right"))(jax.random.split(own_keys[6], ROWS)).reshape((ROWS, TOK)).astype(jnp.int32)
    return {"queries": queries, "out_grad": out_grad, "self_keys": self_keys, "self_values": self_values, "cart_keys": cart_keys, "cart_values": cart_values, "segment_ids": segment_ids}


masked_score = -1.0e30


def block_masks(segment_row):
    positions = jnp.arange(segment_row.shape[0])
    same_doc = segment_row[:, None] == segment_row[None, :]
    return same_doc & (positions[None, :] <= positions[:, None])


def head_block(query_rows, grad_rows, visible, cart_k, cart_v, own_k, own_v):
    token_count, block_width, head_dim = query_rows.shape
    score_scale = head_dim ** -0.5
    flat_query = query_rows.reshape(token_count * block_width, head_dim)
    flat_grad = grad_rows.reshape(token_count * block_width, head_dim)
    wide_mask = jnp.repeat(visible, block_width, axis=0)
    cart_scores = jnp.dot(flat_query, cart_k.T, preferred_element_type=jnp.float32) * score_scale
    own_scores = jnp.where(wide_mask, jnp.dot(flat_query, own_k.T, preferred_element_type=jnp.float32) * score_scale, masked_score)
    row_peak = jnp.maximum(jnp.max(cart_scores, axis=1, keepdims=True), jnp.max(own_scores, axis=1, keepdims=True))
    cart_exp = jnp.exp(cart_scores - row_peak)
    own_exp = jnp.exp(own_scores - row_peak)
    row_total = jnp.sum(cart_exp, axis=1, keepdims=True) + jnp.sum(own_exp, axis=1, keepdims=True)
    cart_prob = cart_exp / row_total
    own_prob = own_exp / row_total
    cart_dprob = jnp.dot(flat_grad, cart_v.T, preferred_element_type=jnp.float32)
    own_dprob = jnp.dot(flat_grad, own_v.T, preferred_element_type=jnp.float32)
    center = jnp.sum(cart_prob * cart_dprob, axis=1, keepdims=True) + jnp.sum(own_prob * own_dprob, axis=1, keepdims=True)
    cart_ds = (cart_prob * (cart_dprob - center)).astype(jnp.bfloat16)
    own_ds = (own_prob * (own_dprob - center)).astype(jnp.bfloat16)
    query_grad = (jnp.dot(cart_ds, cart_k, preferred_element_type=jnp.float32) + jnp.dot(own_ds, own_k, preferred_element_type=jnp.float32)) * score_scale
    query_grad = query_grad.reshape(token_count, block_width, head_dim).astype(jnp.bfloat16)
    local_key = jnp.dot(own_ds.T, flat_query, preferred_element_type=jnp.float32) * score_scale
    local_value = jnp.dot(own_prob.astype(jnp.bfloat16).T, flat_grad, preferred_element_type=jnp.float32)
    cart_key = jnp.dot(cart_ds.T, flat_query, preferred_element_type=jnp.float32) * score_scale
    cart_value = jnp.dot(cart_prob.astype(jnp.bfloat16).T, flat_grad, preferred_element_type=jnp.float32)
    return query_grad, local_key, local_value, cart_key, cart_value


def reference(queries, out_grad, self_keys, self_values, cart_keys, cart_values, segment_ids):
    row_count, token_count = segment_ids.shape
    head_count, head_dim = queries.shape[1], queries.shape[2]
    kv_count = cart_keys.shape[1]
    group_width = head_count // kv_count
    query_blocks = queries.reshape(row_count, token_count, kv_count, group_width, head_dim)
    grad_blocks = out_grad.reshape(row_count, token_count, kv_count, group_width, head_dim)
    key_blocks = self_keys.reshape(row_count, token_count, kv_count, head_dim)
    value_blocks = self_values.reshape(row_count, token_count, kv_count, head_dim)

    def one_row(running, inputs):
        query_row, grad_row, key_row, value_row, segment_row = inputs
        visible = block_masks(segment_row)

        def one_group(query_group, grad_group, cart_k, cart_v, own_k, own_v):
            return head_block(query_group, grad_group, visible, cart_k, cart_v, own_k, own_v)

        query_grad, local_key, local_value, cart_key, cart_value = jax.vmap(one_group, in_axes=1)(query_row, grad_row, cart_keys, cart_values, key_row, value_row)
        running = running + jnp.stack([cart_key, cart_value], axis=0).transpose(2, 0, 1, 3)
        query_flat = query_grad.transpose(1, 0, 2, 3).reshape(token_count, head_count * head_dim)
        local_pair = jnp.stack([local_key, local_value], axis=0).transpose(0, 2, 1, 3).astype(jnp.bfloat16)
        return running, (query_flat, local_pair)

    start_sum = jnp.zeros((cart_keys.shape[0], 2, kv_count, head_dim), jnp.float32)
    cart_grads, (query_rows, local_pairs) = lax.scan(one_row, start_sum, (query_blocks, grad_blocks, key_blocks, value_blocks, segment_ids))
    query_grads = query_rows.reshape(row_count * token_count, head_count * head_dim)
    self_grads = local_pairs.transpose(1, 0, 2, 3, 4).reshape(2, row_count * token_count, kv_count, head_dim)
    return cart_grads, self_grads, query_grads
```

```python
import functools
import math

import jax
import jax.numpy as jnp
from jax import lax
from jax.experimental import pallas as pl
from jax.experimental.pallas import tpu as pltpu
from jax.sharding import PartitionSpec as P

masked_score = -1e30
vmem_bytes = 56 * 1024 * 1024
f32 = jnp.float32
bf16 = jnp.bfloat16


def dot_nt(left, right):
    return lax.dot_general(left, right, (((1,), (1,)), ((), ())), preferred_element_type=f32)


def dot_nn(left, right):
    return lax.dot_general(left, right, (((1,), (0,)), ((), ())), preferred_element_type=f32)


def fold_rows(values, op):
    rows, columns = values.shape
    return op(values.reshape(rows // 8, 8, columns), axis=0)


def head_kernel(
    kv_index, kv_local, width, block_tokens, chunk,
    q_ref, g_ref, sk_ref, sv_ref, ck_ref, cv_ref, seg_ref,
    dq_ref, cart_ref, self_ref,
    wide_ref, keys_ref, vals_ref, keys_t_ref, s_ref, d_ref, dk_ref, dv_ref, out_ref,
):
    head_dim = q_ref.shape[1]
    tokens = seg_ref.shape[1]
    cart_rows = ck_ref.shape[0] // kv_local
    all_keys = cart_rows + tokens
    rows = block_tokens * width
    scale = head_dim ** -0.5
    scale2 = scale * math.log2(math.e)

    def pick(ref, dst, at):
        count = ref.shape[0] // kv_local
        if kv_local == 1:
            dst[at : at + count, :] = ref[...]
        else:
            wide_ref[0 : ref.shape[0], :] = ref[...].astype(f32)
            dst[at : at + count, :] = wide_ref[pl.ds(kv_index, count, stride=kv_local), :].astype(bf16)

    pick(ck_ref, keys_ref, 0)
    pick(sk_ref, keys_ref, cart_rows)
    pick(cv_ref, vals_ref, 0)
    pick(sv_ref, vals_ref, cart_rows)
    keys_t_ref[...] = keys_ref[...].astype(f32).T.astype(bf16)
    first_count = jnp.sum((seg_ref[...] == 0).astype(f32), axis=1, keepdims=True).astype(jnp.int32)

    def rows_of(ref, block):
        span = block_tokens * kv_local * width
        wide = ref[block * span : (block + 1) * span, :]
        if kv_local == 1:
            return wide
        wide = wide.astype(f32).reshape(block_tokens, kv_local, width, head_dim)
        return wide[:, kv_index].reshape(rows, head_dim).astype(bf16)

    for block in range(tokens // block_tokens):
        query = rows_of(q_ref, block)
        grad = rows_of(g_ref, block)
        own_limit = (block + 1) * block_tokens
        own_limit = -(-own_limit // chunk) * chunk
        starts = list(range(0, cart_rows + own_limit, chunk))
        token = (lax.broadcasted_iota(jnp.int32, (1, rows), 1) + block * rows) // width
        begin = jnp.where(token >= first_count, first_count, 0)
        peak8 = jnp.full((8, rows), masked_score, f32)
        for start in starts:
            score = dot_nt(keys_ref[start : start + chunk, :], query)
            if start >= cart_rows:
                key_at = lax.broadcasted_iota(jnp.int32, (chunk, rows), 0) + (start - cart_rows)
                score = jnp.where((key_at >= begin) & (key_at <= token), score, masked_score)
            s_ref[start : start + chunk, :] = score
            peak8 = jnp.maximum(peak8, fold_rows(score, jnp.max))
        peak = jnp.max(peak8, axis=0, keepdims=True)
        total8 = jnp.zeros((8, rows), f32)
        center8 = jnp.zeros((8, rows), f32)
        for start in starts:
            weight = jnp.exp2((s_ref[start : start + chunk, :] - peak) * scale2)
            dprob = dot_nt(vals_ref[start : start + chunk, :], grad)
            s_ref[start : start + chunk, :] = weight
            d_ref[start : start + chunk, :] = dprob
            total8 = total8 + fold_rows(weight, jnp.sum)
            center8 = center8 + fold_rows(weight * dprob, jnp.sum)
        share = 1.0 / jnp.sum(total8, axis=0, keepdims=True)
        center = jnp.sum(center8, axis=0, keepdims=True) * share
        dq_t = jnp.zeros((head_dim, rows), f32)
        for start in starts:
            span = slice(start, start + chunk)
            prob = s_ref[span, :] * share
            dscore = (prob * (d_ref[span, :] - center)).astype(bf16)
            dv = dot_nn(prob.astype(bf16), grad)
            dk = dot_nn(dscore, query)
            first = block == 0 or start >= cart_rows + -(-block * block_tokens // chunk) * chunk
            if first:
                dv_ref[span, :] = dv
                dk_ref[span, :] = dk
            else:
                dv_ref[span, :] += dv
                dk_ref[span, :] += dk
            dq_t = dq_t + dot_nn(keys_t_ref[:, span], dscore)
        out_ref[...] = (dq_t * scale).T
        for head in range(width):
            dq_ref[block * block_tokens : (block + 1) * block_tokens, head * head_dim : (head + 1) * head_dim] = (
                out_ref[pl.ds(head, block_tokens, stride=width), :].astype(bf16)
            )
    parts, _, part_rows, _ = cart_ref.shape
    for part in range(parts):
        span = slice(part * part_rows, (part + 1) * part_rows)
        cart_ref[part, 0] = (dk_ref[span, :] * scale).astype(bf16)
        cart_ref[part, 1] = dv_ref[span, :].astype(bf16)
    self_ref[0] = (dk_ref[cart_rows:all_keys, :] * scale).astype(bf16)
    self_ref[1] = dv_ref[cart_rows:all_keys, :].astype(bf16)


def cart_kernel(kv_local, *refs):
    part_refs, out_ref = refs[:-1], refs[-1]
    count = part_refs[0].shape[0]
    part_rows = part_refs[0].shape[2]
    for kv_index, ref in enumerate(part_refs):
        for kind in range(2):
            total = ref[0, kind].astype(f32)
            for part in range(1, count):
                total = total + ref[part, kind].astype(f32)
            out_ref[pl.ds(kind * kv_local + kv_index, part_rows, stride=2 * kv_local), :] = total


def on_device(dp_size, heads_size, queries, out_grad, self_keys, self_values, cart_keys, cart_values, segment_ids):
    tokens, heads_local, head_dim = queries.shape
    kv_local = self_keys.shape[1]
    cart_rows = cart_keys.shape[0]
    width = heads_local // kv_local
    block_tokens = 64
    chunk = 128
    all_keys = cart_rows + tokens
    rows = block_tokens * width
    part_rows = cart_rows // dp_size
    flat = [array.reshape(-1, head_dim) for array in (queries, out_grad, self_keys, self_values, cart_keys, cart_values)]
    macs = tokens * width * all_keys * head_dim * 5
    query_list, cart_list, self_list = [], [], []
    for kv_index in range(kv_local):
        dq, cart, own = pl.pallas_call(
            functools.partial(head_kernel, kv_index, kv_local, width, block_tokens, chunk),
            out_shape=(
                jax.ShapeDtypeStruct((tokens, width * head_dim), bf16),
                jax.ShapeDtypeStruct((dp_size, 2, part_rows, head_dim), bf16),
                jax.ShapeDtypeStruct((2, tokens, head_dim), bf16),
            ),
            scratch_shapes=[
                pltpu.VMEM((cart_rows * kv_local, head_dim), f32),
                pltpu.VMEM((all_keys, head_dim), bf16),
                pltpu.VMEM((all_keys, head_dim), bf16),
                pltpu.VMEM((head_dim, all_keys), bf16),
                pltpu.VMEM((all_keys, rows), f32),
                pltpu.VMEM((all_keys, rows), f32),
                pltpu.VMEM((all_keys, head_dim), f32),
                pltpu.VMEM((all_keys, head_dim), f32),
                pltpu.VMEM((rows, head_dim), f32),
            ],
            compiler_params=pltpu.CompilerParams(vmem_limit_bytes=vmem_bytes),
            cost_estimate=pl.CostEstimate(flops=4 * macs, bytes_accessed=5 * 2**20, transcendentals=tokens * width * all_keys),
            name="head_grads",
        )(*flat, segment_ids)
        query_list.append(lax.all_to_all(dq, "heads", split_axis=0, concat_axis=0, tiled=True))
        cart_list.append(lax.all_to_all(cart, "dp", split_axis=0, concat_axis=0, tiled=True))
        self_list.append(own)
    own_tokens = tokens // heads_size
    query_grads = jnp.stack(
        [part.reshape(heads_size, own_tokens, width * head_dim) for part in query_list], axis=1
    ).transpose(2, 0, 1, 3).reshape(own_tokens, heads_size * heads_local * head_dim)
    self_grads = jnp.stack(self_list, axis=2)
    cart_grads = pl.pallas_call(
        functools.partial(cart_kernel, kv_local),
        out_shape=jax.ShapeDtypeStruct((part_rows * 2 * kv_local, head_dim), f32),
        compiler_params=pltpu.CompilerParams(vmem_limit_bytes=vmem_bytes),
        cost_estimate=pl.CostEstimate(flops=2**20, bytes_accessed=2 * 2**20, transcendentals=0),
        name="cart_sum",
    )(*cart_list)
    cart_grads = cart_grads.reshape(part_rows, 2, kv_local, head_dim)
    return (cart_grads, self_grads, query_grads)


def solution(mesh):
    in_specs = (
        P(("groups", "dp"), "heads", None),
        P(("groups", "dp"), "heads", None),
        P(("groups", "dp"), "heads", None),
        P(("groups", "dp"), "heads", None),
        P("groups", "heads", None),
        P("groups", "heads", None),
        P(("groups", "dp"), None),
    )
    out_specs = (
        P(("groups", "dp"), None, "heads", None),
        P(None, ("groups", "dp"), "heads", None),
        P(("groups", "dp", "heads"), None),
    )
    return jax.shard_map(
        functools.partial(on_device, mesh.shape["dp"], mesh.shape["heads"]),
        mesh=mesh, in_specs=in_specs, out_specs=out_specs, check_vma=False,
    )
```

```python
import functools
import math

import jax
import jax.numpy as jnp
from jax import lax
from jax.experimental import pallas as pl
from jax.experimental.pallas import tpu as pltpu
from jax.sharding import PartitionSpec as P

masked_score = -1e30
vmem_bytes = 56 * 1024 * 1024
f32 = jnp.float32
bf16 = jnp.bfloat16


def dot_nt(left, right):
    return lax.dot_general(left, right, (((1,), (1,)), ((), ())), preferred_element_type=f32)


def dot_nn(left, right):
    return lax.dot_general(left, right, (((1,), (0,)), ((), ())), preferred_element_type=f32)


def fold_rows(values, op):
    rows, columns = values.shape
    return op(values.reshape(rows // 8, 8, columns), axis=0)


def head_kernel(
    dp_size, heads_size, kv_index, kv_local, width, block_tokens, chunk,
    q_ref, g_ref, sk_ref, sv_ref, ck_ref, cv_ref, seg_ref,
    *rest,
):
    cart_outs, dq_outs = rest[:dp_size], rest[dp_size : dp_size + heads_size]
    self_ref = rest[dp_size + heads_size]
    (
        wide_ref, keys_ref, vals_ref, keys_t_ref, s_ref, d_ref, dk_ref, dv_ref, out_ref, dq_ref,
    ) = rest[dp_size + heads_size + 1 :]
    head_dim = q_ref.shape[1]
    tokens = seg_ref.shape[1]
    cart_rows = ck_ref.shape[0] // kv_local
    all_keys = cart_rows + tokens
    rows = block_tokens * width
    scale = head_dim ** -0.5
    scale2 = scale * math.log2(math.e)

    def pick(ref, dst, at):
        count = ref.shape[0] // kv_local
        if kv_local == 1:
            dst[at : at + count, :] = ref[...]
        else:
            wide_ref[0 : ref.shape[0], :] = ref[...].astype(f32)
            dst[at : at + count, :] = wide_ref[pl.ds(kv_index, count, stride=kv_local), :].astype(bf16)

    pick(ck_ref, keys_ref, 0)
    pick(sk_ref, keys_ref, cart_rows)
    pick(cv_ref, vals_ref, 0)
    pick(sv_ref, vals_ref, cart_rows)
    keys_t_ref[...] = keys_ref[...].astype(f32).T.astype(bf16)
    first_count = jnp.sum((seg_ref[...] == 0).astype(f32), axis=1, keepdims=True).astype(jnp.int32)

    def rows_of(ref, block):
        span = block_tokens * kv_local * width
        wide = ref[block * span : (block + 1) * span, :]
        if kv_local == 1:
            return wide
        wide = wide.astype(f32).reshape(block_tokens, kv_local, width, head_dim)
        return wide[:, kv_index].reshape(rows, head_dim).astype(bf16)

    for block in range(tokens // block_tokens):
        query = rows_of(q_ref, block)
        grad = rows_of(g_ref, block)
        own_limit = (block + 1) * block_tokens
        own_limit = -(-own_limit // chunk) * chunk
        starts = list(range(0, cart_rows + own_limit, chunk))
        token = (lax.broadcasted_iota(jnp.int32, (1, rows), 1) + block * rows) // width
        begin = jnp.where(token >= first_count, first_count, 0)
        peak8 = jnp.full((8, rows), masked_score, f32)
        for start in starts:
            score = dot_nt(keys_ref[start : start + chunk, :], query)
            if start >= cart_rows:
                key_at = lax.broadcasted_iota(jnp.int32, (chunk, rows), 0) + (start - cart_rows)
                score = jnp.where((key_at >= begin) & (key_at <= token), score, masked_score)
            s_ref[start : start + chunk, :] = score
            peak8 = jnp.maximum(peak8, fold_rows(score, jnp.max))
        peak = jnp.max(peak8, axis=0, keepdims=True)
        total8 = jnp.zeros((8, rows), f32)
        center8 = jnp.zeros((8, rows), f32)
        for start in starts:
            weight = jnp.exp2((s_ref[start : start + chunk, :] - peak) * scale2)
            dprob = dot_nt(vals_ref[start : start + chunk, :], grad)
            s_ref[start : start + chunk, :] = weight
            d_ref[start : start + chunk, :] = dprob
            total8 = total8 + fold_rows(weight, jnp.sum)
            center8 = center8 + fold_rows(weight * dprob, jnp.sum)
        share = 1.0 / jnp.sum(total8, axis=0, keepdims=True)
        center = jnp.sum(center8, axis=0, keepdims=True) * share
        dq_t = jnp.zeros((head_dim, rows), f32)
        for start in starts:
            span = slice(start, start + chunk)
            prob = s_ref[span, :] * share
            dscore = (prob * (d_ref[span, :] - center)).astype(bf16)
            dv = dot_nn(prob.astype(bf16), grad)
            dk = dot_nn(dscore, query)
            first = block == 0 or start >= cart_rows + -(-block * block_tokens // chunk) * chunk
            if first:
                dv_ref[span, :] = dv
                dk_ref[span, :] = dk
            else:
                dv_ref[span, :] += dv
                dk_ref[span, :] += dk
            dq_t = dq_t + dot_nn(keys_t_ref[:, span], dscore)
        out_ref[...] = (dq_t * scale).T
        for head in range(width):
            dq_ref[block * block_tokens : (block + 1) * block_tokens, head * head_dim : (head + 1) * head_dim] = (
                out_ref[pl.ds(head, block_tokens, stride=width), :].astype(bf16)
            )
    part_rows = cart_rows // dp_size
    me = lax.axis_index("dp")
    for step, ref in enumerate(cart_outs):
        target = lax.rem(me + step, dp_size)
        span = pl.ds(pl.multiple_of(target * part_rows, part_rows), part_rows)
        ref[0] = (dk_ref[span, :] * scale).astype(ref.dtype)
        ref[1] = dv_ref[span, :].astype(ref.dtype)
    own_tokens = tokens // heads_size
    me = lax.axis_index("heads")
    for step, ref in enumerate(dq_outs):
        target = lax.rem(me + step, heads_size)
        ref[...] = dq_ref[pl.ds(pl.multiple_of(target * own_tokens, own_tokens), own_tokens), :]
    self_ref[0] = (dk_ref[cart_rows:all_keys, :] * scale).astype(bf16)
    self_ref[1] = dv_ref[cart_rows:all_keys, :].astype(bf16)


def cart_kernel(kv_local, *refs):
    part_refs, out_ref = refs[:-1], refs[-1]
    count = len(part_refs) // kv_local
    part_rows = part_refs[0].shape[1]
    for kv_index in range(kv_local):
        for kind in range(2):
            total = part_refs[kv_index * count][kind]
            for part in range(1, count):
                total = total + part_refs[kv_index * count + part][kind].astype(f32)
            out_ref[pl.ds(kind * kv_local + kv_index, part_rows, stride=2 * kv_local), :] = total


def place_kernel(kv_local, *refs):
    part_refs, out_ref = refs[:-1], refs[-1]
    count = len(part_refs) // kv_local
    columns = part_refs[0].shape[1]
    me = lax.axis_index("heads")
    for kv_index in range(kv_local):
        for step in range(count):
            source = lax.rem(me + count - step, count)
            at = pl.multiple_of((source * kv_local + kv_index) * columns, columns)
            out_ref[:, pl.ds(at, columns)] = part_refs[kv_index * count + step][...]


def shift(values, axis, size, step):
    if step == 0:
        return values
    return lax.ppermute(values, axis, [(source, (source + step) % size) for source in range(size)])


def on_device(dp_size, heads_size, queries, out_grad, self_keys, self_values, cart_keys, cart_values, segment_ids):
    tokens, heads_local, head_dim = queries.shape
    kv_local = self_keys.shape[1]
    cart_rows = cart_keys.shape[0]
    width = heads_local // kv_local
    block_tokens = 64
    chunk = 128
    all_keys = cart_rows + tokens
    rows = block_tokens * width
    part_rows = cart_rows // dp_size
    own_tokens = tokens // heads_size
    flat = [array.reshape(-1, head_dim) for array in (queries, out_grad, self_keys, self_values, cart_keys, cart_values)]
    macs = tokens * width * all_keys * head_dim * 5
    cart_list, query_list, self_list = [], [], []
    for kv_index in range(kv_local):
        outs = pl.pallas_call(
            functools.partial(head_kernel, dp_size, heads_size, kv_index, kv_local, width, block_tokens, chunk),
            out_shape=(
                *[
                    jax.ShapeDtypeStruct((2, part_rows, head_dim), bf16 if step else f32)
                    for step in range(dp_size)
                ],
                *[jax.ShapeDtypeStruct((own_tokens, width * head_dim), bf16) for _ in range(heads_size)],
                jax.ShapeDtypeStruct((2, tokens, head_dim), bf16),
            ),
            scratch_shapes=[
                pltpu.VMEM((cart_rows * kv_local, head_dim), f32),
                pltpu.VMEM((all_keys, head_dim), bf16),
                pltpu.VMEM((all_keys, head_dim), bf16),
                pltpu.VMEM((head_dim, all_keys), bf16),
                pltpu.VMEM((all_keys, rows), f32),
                pltpu.VMEM((all_keys, rows), f32),
                pltpu.VMEM((all_keys, head_dim), f32),
                pltpu.VMEM((all_keys, head_dim), f32),
                pltpu.VMEM((rows, head_dim), f32),
                pltpu.VMEM((tokens, width * head_dim), bf16),
            ],
            compiler_params=pltpu.CompilerParams(vmem_limit_bytes=vmem_bytes),
            cost_estimate=pl.CostEstimate(flops=4 * macs, bytes_accessed=5 * 2**20, transcendentals=tokens * width * all_keys),
            name="head_grads",
        )(*flat, segment_ids)
        cart_list += [shift(outs[step], "dp", dp_size, step) for step in range(dp_size)]
        query_list += [shift(outs[dp_size + step], "heads", heads_size, step) for step in range(heads_size)]
        self_list.append(outs[-1])
    query_grads = pl.pallas_call(
        functools.partial(place_kernel, kv_local),
        out_shape=jax.ShapeDtypeStruct((own_tokens, heads_size * heads_local * head_dim), bf16),
        compiler_params=pltpu.CompilerParams(vmem_limit_bytes=vmem_bytes),
        cost_estimate=pl.CostEstimate(flops=2**20, bytes_accessed=2 * 2**20, transcendentals=0),
        name="place_queries",
    )(*query_list)
    self_grads = jnp.stack(self_list, axis=2)
    cart_grads = pl.pallas_call(
        functools.partial(cart_kernel, kv_local),
        out_shape=jax.ShapeDtypeStruct((part_rows * 2 * kv_local, head_dim), f32),
        compiler_params=pltpu.CompilerParams(vmem_limit_bytes=vmem_bytes),
        cost_estimate=pl.CostEstimate(flops=2**20, bytes_accessed=2 * 2**20, transcendentals=0),
        name="cart_sum",
    )(*cart_list)
    cart_grads = cart_grads.reshape(part_rows, 2, kv_local, head_dim)
    return (cart_grads, self_grads, query_grads)


def solution(mesh):
    in_specs = (
        P(("groups", "dp"), "heads", None),
        P(("groups", "dp"), "heads", None),
        P(("groups", "dp"), "heads", None),
        P(("groups", "dp"), "heads", None),
        P("groups", "heads", None),
        P("groups", "heads", None),
        P(("groups", "dp"), None),
    )
    out_specs = (
        P(("groups", "dp"), None, "heads", None),
        P(None, ("groups", "dp"), "heads", None),
        P(("groups", "dp", "heads"), None),
    )
    return jax.shard_map(
        functools.partial(on_device, mesh.shape["dp"], mesh.shape["heads"]),
        mesh=mesh, in_specs=in_specs, out_specs=out_specs, check_vma=False,
    )
```

```python
import functools
import math

import jax
import jax.numpy as jnp
from jax import lax
from jax.experimental import pallas as pl
from jax.experimental.pallas import tpu as pltpu
from jax.sharding import PartitionSpec as P

masked_score = -1e30
vmem_bytes = 56 * 1024 * 1024
f32 = jnp.float32
bf16 = jnp.bfloat16


def dot_nt(left, right):
    return lax.dot_general(left, right, (((1,), (1,)), ((), ())), preferred_element_type=f32)


def dot_nn(left, right):
    return lax.dot_general(left, right, (((1,), (0,)), ((), ())), preferred_element_type=f32)


def fold_rows(values, op):
    rows, columns = values.shape
    return op(values.reshape(rows // 8, 8, columns), axis=0)


def head_kernel(dp_size, heads_size, kv_index, kv_local, width, block_tokens, chunk, *refs):
    last = kv_index == kv_local - 1
    q_ref, g_ref, sk_ref, sv_ref, ck_ref, cv_ref, seg_ref = refs[:7]
    refs = refs[7:]
    held = kv_index if last else 0
    dq_before, self_before, refs = refs[:held], refs[held : 2 * held], refs[2 * held :]
    cart_outs, refs = refs[:dp_size], refs[dp_size:]
    dq_count = heads_size if last else 1
    dq_outs, self_ref, refs = refs[:dq_count], refs[dq_count], refs[dq_count + 1 :]
    (
        wide_ref, keys_ref, vals_ref, keys_t_ref, s_ref, w_ref, d_ref, dk_ref, dv_ref, out_ref, dq_ref,
        q_in, g_in, sk_in, sv_in, ck_in, cv_in, sems,
    ) = refs
    head_dim = q_ref.shape[1]
    tokens = seg_ref.shape[1]
    cart_rows = ck_ref.shape[0] // kv_local
    all_keys = cart_rows + tokens
    rows = block_tokens * width
    scale = head_dim ** -0.5
    scale2 = scale * math.log2(math.e)
    span = block_tokens * kv_local * width
    blocks = tokens // block_tokens

    def block_copy(source, target, block, sem):
        at = slice(block * span, (block + 1) * span)
        return pltpu.make_async_copy(source.at[at, :], target.at[at, :], sems.at[sem])

    copies = {
        name: pltpu.make_async_copy(source, target, sems.at[at])
        for at, (name, source, target) in enumerate(
            [("ck", ck_ref, ck_in), ("sk", sk_ref, sk_in), ("cv", cv_ref, cv_in), ("sv", sv_ref, sv_in)]
        )
    }
    for block in range(blocks):
        copies["q", block] = block_copy(q_ref, q_in, block, 4 + block)
        copies["g", block] = block_copy(g_ref, g_in, block, 4 + blocks + block)
    order = ["ck", "sk", ("q", 0), "cv", "sv", ("g", 0)]
    order += [(kind, block) for block in range(1, blocks) for kind in ("q", "g")]
    for name in order:
        copies[name].start()

    def pick(name, ref, dst, at):
        copies[name].wait()
        count = ref.shape[0] // kv_local
        if kv_local == 1:
            dst[at : at + count, :] = ref[...]
        else:
            wide_ref[0 : ref.shape[0], :] = ref[...].astype(f32)
            dst[at : at + count, :] = wide_ref[pl.ds(kv_index, count, stride=kv_local), :].astype(bf16)

    def rows_of(name, ref, block):
        copies[name, block].wait()
        wide = ref[block * span : (block + 1) * span, :]
        if kv_local == 1:
            return wide
        wide = wide.astype(f32).reshape(block_tokens, kv_local, width, head_dim)
        return wide[:, kv_index].reshape(rows, head_dim).astype(bf16)

    first_count = jnp.sum((seg_ref[...] == 0).astype(f32), axis=1, keepdims=True).astype(jnp.int32)

    def limit(block):
        return -(-(block + 1) * block_tokens // chunk) * chunk

    def starts_of(block):
        return range(0, cart_rows + limit(block), chunk)

    queries, grads, peaks, stats = {}, {}, {}, {}
    acc = {}

    def open_scores(block):
        queries[block] = rows_of("q", q_in, block)
        token = (lax.broadcasted_iota(jnp.int32, (1, rows), 1) + block * rows) // width
        begin = jnp.where(token >= first_count, first_count, 0)
        acc["peak"] = jnp.full((8, rows), masked_score, f32)
        acc["token"], acc["begin"] = token, begin

    def step_scores(block, start):
        score = dot_nt(keys_ref[start : start + chunk, :], queries[block])
        if start >= cart_rows:
            key_at = lax.broadcasted_iota(jnp.int32, (chunk, rows), 0) + (start - cart_rows)
            score = jnp.where((key_at >= acc["begin"]) & (key_at <= acc["token"]), score, masked_score)
        s_ref[block % 2, start : start + chunk, :] = score
        acc["peak"] = jnp.maximum(acc["peak"], fold_rows(score, jnp.max))

    def close_scores(block):
        peaks[block] = jnp.max(acc["peak"], axis=0, keepdims=True)

    def open_weights(block):
        grads[block] = rows_of("g", g_in, block)
        acc["total"] = jnp.zeros((8, rows), f32)
        acc["center"] = jnp.zeros((8, rows), f32)

    def step_weights(block, start):
        at = slice(start, start + chunk)
        weight = jnp.exp2((s_ref[block % 2, at, :] - peaks[block]) * scale2)
        dprob = dot_nt(vals_ref[at, :], grads[block])
        w_ref[block % 2, at, :] = weight
        d_ref[block % 2, at, :] = dprob
        acc["total"] = acc["total"] + fold_rows(weight, jnp.sum)
        acc["center"] = acc["center"] + fold_rows(weight * dprob, jnp.sum)

    def close_weights(block):
        share = 1.0 / jnp.sum(acc["total"], axis=0, keepdims=True)
        stats[block] = share, jnp.sum(acc["center"], axis=0, keepdims=True) * share

    def open_grads(block):
        acc["dq"] = jnp.zeros((head_dim, rows), f32)

    def step_grads(block, start):
        at = slice(start, start + chunk)
        share, center = stats[block]
        prob = w_ref[block % 2, at, :] * share
        dscore = (prob * (d_ref[block % 2, at, :] - center)).astype(bf16)
        dv = dot_nn(prob.astype(bf16), grads[block])
        dk = dot_nn(dscore, queries[block])
        if block == 0 or start >= cart_rows + limit(block - 1):
            dv_ref[at, :] = dv
            dk_ref[at, :] = dk
        else:
            dv_ref[at, :] += dv
            dk_ref[at, :] += dk
        acc["dq"] = acc["dq"] + dot_nn(keys_t_ref[:, at], dscore)

    def close_grads(block):
        out_ref[...] = (acc["dq"] * scale).T
        for head in range(width):
            dq_ref[block * block_tokens : (block + 1) * block_tokens, head * head_dim : (head + 1) * head_dim] = (
                out_ref[pl.ds(head, block_tokens, stride=width), :].astype(bf16)
            )

    pick("ck", ck_in, keys_ref, 0)
    pick("sk", sk_in, keys_ref, cart_rows)
    stages = (
        (2, open_grads, step_grads, close_grads),
        (1, open_weights, step_weights, close_weights),
        (0, open_scores, step_scores, close_scores),
    )
    for turn in range(blocks + 2):
        live = [(turn - lag, *calls) for lag, *calls in stages if 0 <= turn - lag < blocks]
        if turn == 1:
            pick("cv", cv_in, vals_ref, 0)
            pick("sv", sv_in, vals_ref, cart_rows)
            keys_t_ref[...] = keys_ref[...].astype(f32).T.astype(bf16)
        for block, begin_call, _, _ in live:
            begin_call(block)
        for start in range(0, all_keys, chunk):
            for block, _, step_call, _ in live:
                if start in starts_of(block):
                    step_call(block, start)
        for block, _, _, end_call in live:
            end_call(block)

    part_rows = cart_rows // dp_size
    me = lax.axis_index("dp")
    for step, ref in enumerate(cart_outs):
        target = lax.rem(me + step, dp_size)
        at = pl.ds(pl.multiple_of(target * part_rows, part_rows), part_rows)
        ref[0] = (dk_ref[at, :] * scale).astype(ref.dtype)
        ref[1] = dv_ref[at, :].astype(ref.dtype)
    own = dk_ref[cart_rows:all_keys, :] * scale, dv_ref[cart_rows:all_keys, :]
    if not last:
        dq_outs[0][...] = dq_ref[...]
        self_ref[0], self_ref[1] = own
        return
    own_tokens = tokens // heads_size
    columns = width * head_dim
    me = lax.axis_index("heads")
    for step, ref in enumerate(dq_outs):
        target = lax.rem(me + step, heads_size)
        at = pl.ds(pl.multiple_of(target * own_tokens, own_tokens), own_tokens)
        for index, before in enumerate((*dq_before, dq_ref)):
            ref[:, index * columns : (index + 1) * columns] = before[at, :]
    count = tokens * kv_local
    for kind in range(2):
        for index, before in enumerate(self_before):
            wide_ref[pl.ds(index, tokens, stride=kv_local), :] = before[kind]
        wide_ref[pl.ds(kv_index, tokens, stride=kv_local), :] = own[kind]
        self_ref[kind * count : (kind + 1) * count, :] = wide_ref[0:count, :].astype(bf16)


def cart_kernel(kv_local, *refs):
    part_refs, out_ref = refs[:-2], refs[-1]
    count = len(part_refs) // kv_local
    part_rows = part_refs[0].shape[1]
    for kv_index in range(kv_local):
        for kind in range(2):
            total = part_refs[kv_index * count][kind]
            for part in range(1, count):
                total = total + part_refs[kv_index * count + part][kind].astype(f32)
            out_ref[pl.ds(kind * kv_local + kv_index, part_rows, stride=2 * kv_local), :] = total


def place_kernel(*refs):
    part_refs, out_ref = refs[:-1], refs[-1]
    count = len(part_refs)
    columns = part_refs[0].shape[1]
    me = lax.axis_index("heads")
    for step, ref in enumerate(part_refs):
        source = lax.rem(me + count - step, count)
        out_ref[:, pl.ds(pl.multiple_of(source * columns, columns), columns)] = ref[...]


def shift(values, axis, size, step):
    if step == 0:
        return values
    return lax.ppermute(values, axis, [(source, (source + step) % size) for source in range(size)])


def on_device(dp_size, heads_size, queries, out_grad, self_keys, self_values, cart_keys, cart_values, segment_ids):
    tokens, heads_local, head_dim = queries.shape
    kv_local = self_keys.shape[1]
    cart_rows = cart_keys.shape[0]
    width = heads_local // kv_local
    block_tokens = 64
    chunk = 128
    all_keys = cart_rows + tokens
    rows = block_tokens * width
    part_rows = cart_rows // dp_size
    own_tokens = tokens // heads_size
    flat = [array.reshape(-1, head_dim) for array in (queries, out_grad, self_keys, self_values, cart_keys, cart_values)]
    macs = tokens * width * all_keys * head_dim * 5
    blocks = tokens // block_tokens
    columns = width * head_dim
    count = tokens * kv_local
    cart_list, query_list, self_list = [], [], []
    for kv_index in range(kv_local):
        last = kv_index == kv_local - 1
        if last:
            other_shapes = [jax.ShapeDtypeStruct((own_tokens, kv_local * columns), bf16) for _ in range(heads_size)]
            other_shapes.append(jax.ShapeDtypeStruct((2 * count, head_dim), bf16))
        else:
            other_shapes = [
                jax.ShapeDtypeStruct((tokens, columns), bf16),
                jax.ShapeDtypeStruct((2, tokens, head_dim), f32),
            ]
        before = query_list + self_list
        outs = pl.pallas_call(
            functools.partial(head_kernel, dp_size, heads_size, kv_index, kv_local, width, block_tokens, chunk),
            out_shape=(
                *[
                    jax.ShapeDtypeStruct((2, part_rows, head_dim), bf16 if step else f32)
                    for step in range(dp_size)
                ],
                *other_shapes,
            ),
            in_specs=[pl.BlockSpec(memory_space=pl.ANY)] * 6
            + [pl.BlockSpec(memory_space=pltpu.VMEM)] * (1 + (len(before) if last else 0)),
            scratch_shapes=[
                pltpu.VMEM((cart_rows * kv_local, head_dim), f32),
                pltpu.VMEM((all_keys, head_dim), bf16),
                pltpu.VMEM((all_keys, head_dim), bf16),
                pltpu.VMEM((head_dim, all_keys), bf16),
                pltpu.VMEM((2, all_keys, rows), f32),
                pltpu.VMEM((2, all_keys, rows), f32),
                pltpu.VMEM((2, all_keys, rows), f32),
                pltpu.VMEM((all_keys, head_dim), f32),
                pltpu.VMEM((all_keys, head_dim), f32),
                pltpu.VMEM((rows, head_dim), f32),
                pltpu.VMEM((tokens, columns), bf16),
                *[pltpu.VMEM(array.shape, bf16) for array in flat],
                pltpu.SemaphoreType.DMA((4 + 2 * blocks,)),
            ],
            compiler_params=pltpu.CompilerParams(vmem_limit_bytes=vmem_bytes),
            cost_estimate=pl.CostEstimate(flops=4 * macs, bytes_accessed=5 * 2**20, transcendentals=tokens * width * all_keys),
            name="head_grads",
        )(*flat, segment_ids, *(before if last else []))
        cart_list += [shift(outs[step], "dp", dp_size, step) for step in range(dp_size)]
        if last:
            query_list, self_grads = outs[dp_size:-1], outs[-1]
        else:
            query_list.append(outs[-2])
            self_list.append(outs[-1])
    query_list = [shift(part, "heads", heads_size, step) for step, part in enumerate(query_list)]
    query_grads = pl.pallas_call(
        place_kernel,
        out_shape=jax.ShapeDtypeStruct((own_tokens, heads_size * heads_local * head_dim), bf16),
        compiler_params=pltpu.CompilerParams(vmem_limit_bytes=vmem_bytes),
        cost_estimate=pl.CostEstimate(flops=2**20, bytes_accessed=2 * 2**20, transcendentals=0),
        name="place_queries",
    )(*query_list)
    cart_grads = pl.pallas_call(
        functools.partial(cart_kernel, kv_local),
        out_shape=jax.ShapeDtypeStruct((part_rows * 2 * kv_local, head_dim), f32),
        in_specs=[pl.BlockSpec(memory_space=pltpu.VMEM)] * len(cart_list) + [pl.BlockSpec(memory_space=pl.ANY)],
        compiler_params=pltpu.CompilerParams(vmem_limit_bytes=vmem_bytes),
        cost_estimate=pl.CostEstimate(flops=2**20, bytes_accessed=2 * 2**20, transcendentals=0),
        name="cart_sum",
    )(*cart_list, query_grads)
    cart_grads = cart_grads.reshape(part_rows, 2, kv_local, head_dim)
    self_grads = self_grads.reshape(2, tokens, kv_local, head_dim)
    return (cart_grads, self_grads, query_grads)


def solution(mesh):
    in_specs = (
        P(("groups", "dp"), "heads", None),
        P(("groups", "dp"), "heads", None),
        P(("groups", "dp"), "heads", None),
        P(("groups", "dp"), "heads", None),
        P("groups", "heads", None),
        P("groups", "heads", None),
        P(("groups", "dp"), None),
    )
    out_specs = (
        P(("groups", "dp"), None, "heads", None),
        P(None, ("groups", "dp"), "heads", None),
        P(("groups", "dp", "heads"), None),
    )
    return jax.shard_map(
        functools.partial(on_device, mesh.shape["dp"], mesh.shape["heads"]),
        mesh=mesh, in_specs=in_specs, out_specs=out_specs, check_vma=False,
    )
```

```python
import functools
import math

import jax
import jax.numpy as jnp
from jax import lax
from jax.experimental import pallas as pl
from jax.experimental.pallas import tpu as pltpu
from jax.sharding import PartitionSpec as P

masked_score = -1e30
vmem_bytes = 56 * 1024 * 1024
f32 = jnp.float32
bf16 = jnp.bfloat16


def dot_nt(left, right):
    return lax.dot_general(left, right, (((1,), (1,)), ((), ())), preferred_element_type=f32)


def dot_nn(left, right):
    return lax.dot_general(left, right, (((1,), (0,)), ((), ())), preferred_element_type=f32)


def dot_tn(left, right):
    return lax.dot_general(left, right, (((0,), (0,)), ((), ())), preferred_element_type=f32)


def fold_rows(values, op):
    rows, columns = values.shape
    return op(values.reshape(rows // 8, 8, columns), axis=0)


def head_kernel(dp_size, heads_size, kv_index, kv_local, width, block_tokens, chunk, fine, *refs):
    last = kv_index == kv_local - 1
    q_ref, g_ref, sk_ref, sv_ref, ck_ref, cv_ref, seg_ref = refs[:7]
    refs = refs[7:]
    held = kv_index if last else 0
    dq_before, self_before, refs = refs[:held], refs[held : 2 * held], refs[2 * held :]
    cart_outs, refs = refs[:dp_size], refs[dp_size:]
    dq_count = heads_size if last else 1
    dq_outs, self_ref, refs = refs[:dq_count], refs[dq_count], refs[dq_count + 1 :]
    (
        wide_ref, keys_ref, vals_ref, s_ref, w_ref, d_ref, dk_ref, dv_ref, out_ref, dq_ref,
        q_in, g_in, sk_in, sv_in, ck_in, cv_in, sems,
    ) = refs
    head_dim = q_ref.shape[1]
    tokens = seg_ref.shape[1]
    cart_rows = ck_ref.shape[0] // kv_local
    all_keys = cart_rows + tokens
    rows = block_tokens * width
    scale = head_dim ** -0.5
    scale2 = scale * math.log2(math.e)
    span = block_tokens * kv_local * width
    blocks = tokens // block_tokens

    def block_copy(source, target, block, sem):
        at = slice(block * span, (block + 1) * span)
        return pltpu.make_async_copy(source.at[at, :], target.at[at, :], sems.at[sem])

    copies = {
        name: pltpu.make_async_copy(source, target, sems.at[at])
        for at, (name, source, target) in enumerate(
            [("ck", ck_ref, ck_in), ("sk", sk_ref, sk_in), ("cv", cv_ref, cv_in), ("sv", sv_ref, sv_in)]
        )
    }
    for block in range(blocks):
        copies["q", block] = block_copy(q_ref, q_in, block, 4 + block)
        copies["g", block] = block_copy(g_ref, g_in, block, 4 + blocks + block)
    order = ["ck", "sk", ("q", 0), "cv", "sv", ("g", 0)]
    order += [(kind, block) for block in range(1, blocks) for kind in ("q", "g")]
    for name in order:
        copies[name].start()

    def pick(name, ref, dst, at):
        copies[name].wait()
        count = ref.shape[0] // kv_local
        if kv_local == 1:
            dst[at : at + count, :] = ref[...]
        else:
            wide_ref[0 : ref.shape[0], :] = ref[...].astype(f32)
            dst[at : at + count, :] = wide_ref[pl.ds(kv_index, count, stride=kv_local), :].astype(bf16)

    def rows_of(name, ref, block):
        copies[name, block].wait()
        wide = ref[block * span : (block + 1) * span, :]
        if kv_local == 1:
            return wide
        wide = wide.astype(f32).reshape(block_tokens, kv_local, width, head_dim)
        return wide[:, kv_index].reshape(rows, head_dim).astype(bf16)

    first_count = jnp.sum((seg_ref[...] == 0).astype(f32), axis=1, keepdims=True).astype(jnp.int32)

    def limit(block):
        return -(-(block + 1) * block_tokens // fine) * fine

    def pieces(block):
        cart = [(start, chunk) for start in range(0, cart_rows, chunk)]
        return cart + [(cart_rows, limit(block))]

    queries, grads, peaks, stats = {}, {}, {}, {}
    acc = {}

    def open_scores(block):
        queries[block] = rows_of("q", q_in, block)
        token = (lax.broadcasted_iota(jnp.int32, (1, rows), 1) + block * rows) // width
        begin = jnp.where(token >= first_count, first_count, 0)
        acc["peak"] = jnp.full((8, rows), masked_score, f32)
        acc["token"], acc["begin"] = token, begin

    def step_scores(block, start, size):
        score = dot_nt(keys_ref[start : start + size, :], queries[block])
        if start >= cart_rows:
            key_at = lax.broadcasted_iota(jnp.int32, (size, rows), 0)
            score = jnp.where((key_at >= acc["begin"]) & (key_at <= acc["token"]), score, masked_score)
        s_ref[block % 2, start : start + size, :] = score
        acc["peak"] = jnp.maximum(acc["peak"], fold_rows(score, jnp.max))

    def close_scores(block):
        peaks[block] = jnp.max(acc["peak"], axis=0, keepdims=True)

    def open_weights(block):
        grads[block] = rows_of("g", g_in, block)
        acc["total"] = jnp.zeros((8, rows), f32)
        acc["center"] = jnp.zeros((8, rows), f32)

    def step_weights(block, start, size):
        at = slice(start, start + size)
        weight = jnp.exp2((s_ref[block % 2, at, :] - peaks[block]) * scale2)
        dprob = dot_nt(vals_ref[at, :], grads[block])
        w_ref[block % 2, at, :] = weight
        d_ref[block % 2, at, :] = dprob
        acc["total"] = acc["total"] + fold_rows(weight, jnp.sum)
        acc["center"] = acc["center"] + fold_rows(weight * dprob, jnp.sum)

    def close_weights(block):
        share = 1.0 / jnp.sum(acc["total"], axis=0, keepdims=True)
        stats[block] = share, jnp.sum(acc["center"], axis=0, keepdims=True) * share

    def open_grads(block):
        acc["dq"] = jnp.zeros((rows, head_dim), f32)

    def step_grads(block, start, size):
        at = slice(start, start + size)
        share, center = stats[block]
        prob = w_ref[block % 2, at, :] * share
        dscore = (prob * (d_ref[block % 2, at, :] - center)).astype(bf16)
        dv = dot_nn(prob.astype(bf16), grads[block])
        dk = dot_nn(dscore, queries[block])
        old = size if start < cart_rows else (limit(block - 1) if block else 0)
        old = old if block else 0
        for ref, part in ((dv_ref, dv), (dk_ref, dk)):
            if old:
                ref[start : start + old, :] += part[:old]
            if old < size:
                ref[start + old : start + size, :] = part[old:]
        acc["dq"] = acc["dq"] + dot_tn(dscore, keys_ref[at, :])

    def close_grads(block):
        out_ref[...] = acc["dq"] * scale
        for head in range(width):
            dq_ref[block * block_tokens : (block + 1) * block_tokens, head * head_dim : (head + 1) * head_dim] = (
                out_ref[pl.ds(head, block_tokens, stride=width), :].astype(bf16)
            )

    pick("ck", ck_in, keys_ref, 0)
    pick("sk", sk_in, keys_ref, cart_rows)
    stages = (
        (2, open_grads, step_grads, close_grads),
        (1, open_weights, step_weights, close_weights),
        (0, open_scores, step_scores, close_scores),
    )
    for turn in range(blocks + 2):
        live = [(turn - lag, *calls) for lag, *calls in stages if 0 <= turn - lag < blocks]
        if turn == 1:
            pick("cv", cv_in, vals_ref, 0)
            pick("sv", sv_in, vals_ref, cart_rows)
        for block, begin_call, _, _ in live:
            begin_call(block)
        for index in range(len(pieces(0))):
            for block, _, step_call, _ in live:
                step_call(block, *pieces(block)[index])
        for block, _, _, end_call in live:
            end_call(block)

    part_rows = cart_rows // dp_size
    me = lax.axis_index("dp")
    for step, ref in enumerate(cart_outs):
        target = lax.rem(me + step, dp_size)
        at = pl.ds(pl.multiple_of(target * part_rows, part_rows), part_rows)
        ref[0] = (dk_ref[at, :] * scale).astype(ref.dtype)
        ref[1] = dv_ref[at, :].astype(ref.dtype)
    own = dk_ref[cart_rows:all_keys, :] * scale, dv_ref[cart_rows:all_keys, :]
    if not last:
        dq_outs[0][...] = dq_ref[...]
        self_ref[0], self_ref[1] = own
        return
    own_tokens = tokens // heads_size
    columns = width * head_dim
    me = lax.axis_index("heads")
    for step, ref in enumerate(dq_outs):
        target = lax.rem(me + step, heads_size)
        at = pl.ds(pl.multiple_of(target * own_tokens, own_tokens), own_tokens)
        for index, before in enumerate((*dq_before, dq_ref)):
            ref[:, index * columns : (index + 1) * columns] = before[at, :]
    count = tokens * kv_local
    for kind in range(2):
        for index, before in enumerate(self_before):
            wide_ref[pl.ds(index, tokens, stride=kv_local), :] = before[kind]
        wide_ref[pl.ds(kv_index, tokens, stride=kv_local), :] = own[kind]
        self_ref[kind * count : (kind + 1) * count, :] = wide_ref[0:count, :].astype(bf16)


def order_kernel(*refs):
    pass


def sum_kernel(*refs):
    part_refs, out_ref = refs[:-1], refs[-1]
    total = part_refs[0][...]
    for ref in part_refs[1:]:
        total = total + ref[...].astype(f32)
    out_ref[...] = total


def cart_kernel(kv_local, *refs):
    done_refs, part_refs, out_ref = refs[: kv_local - 1], refs[kv_local - 1 : -2], refs[-1]
    part_rows = part_refs[0].shape[1]
    for kind in range(2):
        total = part_refs[0][kind]
        for ref in part_refs[1:]:
            total = total + ref[kind].astype(f32)
        for kv_index, part in enumerate((*[ref[kind] for ref in done_refs], total)):
            out_ref[pl.ds(kind * kv_local + kv_index, part_rows, stride=2 * kv_local), :] = part


def place_kernel(count, *refs):
    part_refs, out_ref = refs[:count], refs[-1]
    columns = part_refs[0].shape[1]
    me = lax.axis_index("heads")
    for step, ref in enumerate(part_refs):
        source = lax.rem(me + count - step, count)
        out_ref[:, pl.ds(pl.multiple_of(source * columns, columns), columns)] = ref[...]


def shift(values, axis, size, step):
    if step == 0:
        return values
    return lax.ppermute(values, axis, [(source, (source + step) % size) for source in range(size)])


def on_device(dp_size, heads_size, queries, out_grad, self_keys, self_values, cart_keys, cart_values, segment_ids):
    tokens, heads_local, head_dim = queries.shape
    kv_local = self_keys.shape[1]
    cart_rows = cart_keys.shape[0]
    width = heads_local // kv_local
    block_tokens = 64
    chunk = 512
    fine = 128
    all_keys = cart_rows + tokens
    rows = block_tokens * width
    part_rows = cart_rows // dp_size
    own_tokens = tokens // heads_size
    flat = [array.reshape(-1, head_dim) for array in (queries, out_grad, self_keys, self_values, cart_keys, cart_values)]
    macs = tokens * width * all_keys * head_dim * 5
    blocks = tokens // block_tokens
    columns = width * head_dim
    count = tokens * kv_local
    cart_list, query_list, self_list = [], [], []
    for kv_index in range(kv_local):
        last = kv_index == kv_local - 1
        if last:
            other_shapes = [jax.ShapeDtypeStruct((own_tokens, kv_local * columns), bf16) for _ in range(heads_size)]
            other_shapes.append(jax.ShapeDtypeStruct((2 * count, head_dim), bf16))
        else:
            other_shapes = [
                jax.ShapeDtypeStruct((tokens, columns), bf16),
                jax.ShapeDtypeStruct((2, tokens, head_dim), f32),
            ]
        before = query_list + self_list
        outs = pl.pallas_call(
            functools.partial(head_kernel, dp_size, heads_size, kv_index, kv_local, width, block_tokens, chunk, fine),
            out_shape=(
                *[
                    jax.ShapeDtypeStruct((2, part_rows, head_dim), bf16 if step else f32)
                    for step in range(dp_size)
                ],
                *other_shapes,
            ),
            in_specs=[pl.BlockSpec(memory_space=pltpu.HBM)] * 6
            + [pl.BlockSpec(memory_space=pltpu.VMEM)] * (1 + (len(before) if last else 0)),
            scratch_shapes=[
                pltpu.VMEM((cart_rows * kv_local, head_dim), f32),
                pltpu.VMEM((all_keys, head_dim), bf16),
                pltpu.VMEM((all_keys, head_dim), bf16),
                pltpu.VMEM((2, all_keys, rows), f32),
                pltpu.VMEM((2, all_keys, rows), f32),
                pltpu.VMEM((2, all_keys, rows), f32),
                pltpu.VMEM((all_keys, head_dim), f32),
                pltpu.VMEM((all_keys, head_dim), f32),
                pltpu.VMEM((rows, head_dim), f32),
                pltpu.VMEM((tokens, columns), bf16),
                *[pltpu.VMEM(array.shape, bf16) for array in flat],
                pltpu.SemaphoreType.DMA((4 + 2 * blocks,)),
            ],
            compiler_params=pltpu.CompilerParams(vmem_limit_bytes=vmem_bytes),
            cost_estimate=pl.CostEstimate(flops=4 * macs, bytes_accessed=5 * 2**20, transcendentals=tokens * width * all_keys),
            name="head_grads",
        )(*flat, segment_ids, *(before if last else []))
        sends = list(outs[1:dp_size])
        if last and cart_list:
            anywhere = pl.BlockSpec(memory_space=pl.ANY)
            sends = pl.pallas_call(
                order_kernel,
                out_shape=tuple(jax.ShapeDtypeStruct(array.shape, array.dtype) for array in sends),
                in_specs=[anywhere] * (len(sends) + len(cart_parts) - 1),
                out_specs=(anywhere,) * len(sends),
                input_output_aliases={index: index for index in range(len(sends))},
                cost_estimate=pl.CostEstimate(flops=32 * macs, bytes_accessed=0, transcendentals=0),
                name="order_sends",
            )(*sends, *cart_parts[1:])
        cart_parts = [outs[0]] + [shift(array, "dp", dp_size, step + 1) for step, array in enumerate(sends)]
        if last:
            query_list, self_grads = outs[dp_size:-1], outs[-1]
        else:
            query_list.append(outs[-2])
            self_list.append(outs[-1])
            cart_list.append(
                pl.pallas_call(
                    sum_kernel,
                    out_shape=jax.ShapeDtypeStruct((2, part_rows, head_dim), f32),
                    compiler_params=pltpu.CompilerParams(vmem_limit_bytes=vmem_bytes),
                    cost_estimate=pl.CostEstimate(flops=2**20, bytes_accessed=2**20, transcendentals=0),
                    name="cart_sum",
                )(*cart_parts)
            )
    query_list = [shift(part, "heads", heads_size, step) for step, part in enumerate(query_list)]
    query_grads = pl.pallas_call(
        functools.partial(place_kernel, heads_size),
        out_shape=jax.ShapeDtypeStruct((own_tokens, heads_size * heads_local * head_dim), bf16),
        in_specs=[pl.BlockSpec(memory_space=pltpu.VMEM)] * heads_size
        + [pl.BlockSpec(memory_space=pl.ANY)] * len(cart_list),
        compiler_params=pltpu.CompilerParams(vmem_limit_bytes=vmem_bytes),
        cost_estimate=pl.CostEstimate(flops=2**20, bytes_accessed=2 * 2**20, transcendentals=0),
        name="place_queries",
    )(*query_list, *cart_list)
    cart_grads = pl.pallas_call(
        functools.partial(cart_kernel, kv_local),
        out_shape=jax.ShapeDtypeStruct((part_rows * 2 * kv_local, head_dim), f32),
        in_specs=[pl.BlockSpec(memory_space=pltpu.VMEM)] * (len(cart_list) + dp_size)
        + [pl.BlockSpec(memory_space=pl.ANY)],
        compiler_params=pltpu.CompilerParams(vmem_limit_bytes=vmem_bytes),
        cost_estimate=pl.CostEstimate(flops=2**20, bytes_accessed=2 * 2**20, transcendentals=0),
        name="cart_grads",
    )(*cart_list, *cart_parts, query_grads)
    cart_grads = cart_grads.reshape(part_rows, 2, kv_local, head_dim)
    self_grads = self_grads.reshape(2, tokens, kv_local, head_dim)
    return (cart_grads, self_grads, query_grads)


def solution(mesh):
    in_specs = (
        P(("groups", "dp"), "heads", None),
        P(("groups", "dp"), "heads", None),
        P(("groups", "dp"), "heads", None),
        P(("groups", "dp"), "heads", None),
        P("groups", "heads", None),
        P("groups", "heads", None),
        P(("groups", "dp"), None),
    )
    out_specs = (
        P(("groups", "dp"), None, "heads", None),
        P(None, ("groups", "dp"), "heads", None),
        P(("groups", "dp", "heads"), None),
    )
    return jax.shard_map(
        functools.partial(on_device, mesh.shape["dp"], mesh.shape["heads"]),
        mesh=mesh, in_specs=in_specs, out_specs=out_specs, check_vma=False,
    )
```

```python
import functools
import math

import jax
import jax.numpy as jnp
from jax import lax
from jax.experimental import pallas as pl
from jax.experimental.pallas import tpu as pltpu
from jax.sharding import PartitionSpec as P

masked_score = -1e30
vmem_bytes = 56 * 1024 * 1024
f32 = jnp.float32
bf16 = jnp.bfloat16


def dot_nt(left, right):
    return lax.dot_general(left, right, (((1,), (1,)), ((), ())), preferred_element_type=f32)


def dot_nn(left, right):
    return lax.dot_general(left, right, (((1,), (0,)), ((), ())), preferred_element_type=f32)


def fold_rows(values, op):
    rows, columns = values.shape
    return op(values.reshape(rows // 8, 8, columns), axis=0)


def head_kernel(dp_size, heads_size, kv_index, kv_local, width, block_tokens, chunk, fine, *refs):
    last = kv_index == kv_local - 1
    q_ref, g_ref, sk_ref, sv_ref, ck_ref, cv_ref, seg_ref = refs[:7]
    refs = refs[7:]
    held = kv_index if last else 0
    dq_before, self_before, refs = refs[:held], refs[held : 2 * held], refs[2 * held :]
    cart_outs, refs = refs[:dp_size], refs[dp_size:]
    dq_count = heads_size if last else 1
    dq_outs, self_ref, refs = refs[:dq_count], refs[dq_count], refs[dq_count + 1 :]
    (
        wide_ref, keys_ref, vals_ref, keys_t_ref, s_ref, w_ref, d_ref, dk_t_ref, dv_t_ref, dk_ref, dv_ref, out_ref, dq_ref,
        q_in, g_in, sk_in, sv_in, ck_in, cv_in, sems,
    ) = refs
    head_dim = q_ref.shape[1]
    tokens = seg_ref.shape[1]
    cart_rows = ck_ref.shape[0] // kv_local
    all_keys = cart_rows + tokens
    rows = block_tokens * width
    scale = head_dim ** -0.5
    scale2 = scale * math.log2(math.e)
    span = block_tokens * kv_local * width
    blocks = tokens // block_tokens

    def block_copy(source, target, block, sem):
        at = slice(block * span, (block + 1) * span)
        return pltpu.make_async_copy(source.at[at, :], target.at[at, :], sems.at[sem])

    copies = {
        name: pltpu.make_async_copy(source, target, sems.at[at])
        for at, (name, source, target) in enumerate(
            [("ck", ck_ref, ck_in), ("sk", sk_ref, sk_in), ("cv", cv_ref, cv_in), ("sv", sv_ref, sv_in)]
        )
    }
    for block in range(blocks):
        copies["q", block] = block_copy(q_ref, q_in, block, 4 + block)
        copies["g", block] = block_copy(g_ref, g_in, block, 4 + blocks + block)
    order = ["ck", "sk", ("q", 0), "cv", "sv", ("g", 0)]
    order += [(kind, block) for block in range(1, blocks) for kind in ("q", "g")]
    for name in order:
        copies[name].start()

    def pick(name, ref, dst, at):
        copies[name].wait()
        count = ref.shape[0] // kv_local
        if kv_local == 1:
            dst[at : at + count, :] = ref[...]
        else:
            wide_ref[0 : ref.shape[0], :] = ref[...].astype(f32)
            dst[at : at + count, :] = wide_ref[pl.ds(kv_index, count, stride=kv_local), :].astype(bf16)

    def rows_of(name, ref, block):
        copies[name, block].wait()
        wide = ref[block * span : (block + 1) * span, :]
        if kv_local == 1:
            return wide
        wide = wide.astype(f32).reshape(block_tokens, kv_local, width, head_dim)
        return wide[:, kv_index].reshape(rows, head_dim).astype(bf16)

    first_count = jnp.sum((seg_ref[...] == 0).astype(f32), axis=1, keepdims=True).astype(jnp.int32)

    def limit(block):
        return -(-(block + 1) * block_tokens // fine) * fine

    def pieces(block):
        cart = [(start, chunk) for start in range(0, cart_rows, chunk)]
        return cart + [(cart_rows, limit(block))]

    queries, grads, peaks, stats = {}, {}, {}, {}
    acc, turned = {}, {}

    def turn_values(values):
        return values.astype(f32).T.astype(bf16)

    def open_scores(block):
        queries[block] = rows_of("q", q_in, block)
        token = (lax.broadcasted_iota(jnp.int32, (1, rows), 1) + block * rows) // width
        begin = jnp.where(token >= first_count, first_count, 0)
        acc["peak"] = jnp.full((8, rows), masked_score, f32)
        acc["token"], acc["begin"] = token, begin

    def step_scores(block, start, size):
        score = dot_nt(keys_ref[start : start + size, :], queries[block])
        if start >= cart_rows:
            key_at = lax.broadcasted_iota(jnp.int32, (size, rows), 0)
            score = jnp.where((key_at >= acc["begin"]) & (key_at <= acc["token"]), score, masked_score)
        s_ref[block % 2, start : start + size, :] = score
        acc["peak"] = jnp.maximum(acc["peak"], fold_rows(score, jnp.max))

    def close_scores(block):
        peaks[block] = jnp.max(acc["peak"], axis=0, keepdims=True)

    def open_weights(block):
        grads[block] = rows_of("g", g_in, block)
        acc["total"] = jnp.zeros((8, rows), f32)
        acc["center"] = jnp.zeros((8, rows), f32)

    def step_weights(block, start, size):
        at = slice(start, start + size)
        weight = jnp.exp2((s_ref[block % 2, at, :] - peaks[block]) * scale2)
        dprob = dot_nt(vals_ref[at, :], grads[block])
        w_ref[block % 2, at, :] = weight
        d_ref[block % 2, at, :] = dprob
        acc["total"] = acc["total"] + fold_rows(weight, jnp.sum)
        acc["center"] = acc["center"] + fold_rows(weight * dprob, jnp.sum)

    def close_weights(block):
        share = 1.0 / jnp.sum(acc["total"], axis=0, keepdims=True)
        stats[block] = share, jnp.sum(acc["center"], axis=0, keepdims=True) * share

    def open_grads(block):
        acc["dq"] = jnp.zeros((head_dim, rows), f32)
        turned["q", block] = turn_values(queries[block])
        turned["g", block] = turn_values(grads[block])

    def step_grads(block, start, size):
        at = slice(start, start + size)
        share, center = stats[block]
        prob = w_ref[block % 2, at, :] * share
        dscore = (prob * (d_ref[block % 2, at, :] - center)).astype(bf16)
        dv = dot_nt(turned["g", block], prob.astype(bf16))
        dk = dot_nt(turned["q", block], dscore)
        old = size if start < cart_rows else (limit(block - 1) if block else 0)
        old = old if block else 0
        for ref, part in ((dv_t_ref, dv), (dk_t_ref, dk)):
            if old:
                ref[:, start : start + old] += part[:, :old]
            if old < size:
                ref[:, start + old : start + size] = part[:, old:]
        acc["dq"] = acc["dq"] + dot_nn(keys_t_ref[:, at], dscore)

    def close_grads(block):
        out_ref[...] = (acc["dq"] * scale).T
        for head in range(width):
            dq_ref[block * block_tokens : (block + 1) * block_tokens, head * head_dim : (head + 1) * head_dim] = (
                out_ref[pl.ds(head, block_tokens, stride=width), :].astype(bf16)
            )

    pick("ck", ck_in, keys_ref, 0)
    pick("sk", sk_in, keys_ref, cart_rows)
    stages = (
        (2, open_grads, step_grads, close_grads),
        (1, open_weights, step_weights, close_weights),
        (0, open_scores, step_scores, close_scores),
    )
    for turn in range(blocks + 2):
        live = [(turn - lag, *calls) for lag, *calls in stages if 0 <= turn - lag < blocks]
        if turn == 1:
            pick("cv", cv_in, vals_ref, 0)
            pick("sv", sv_in, vals_ref, cart_rows)
            keys_t_ref[...] = turn_values(keys_ref[...])
        for block, begin_call, _, _ in live:
            begin_call(block)
        for index in range(len(pieces(0))):
            for block, _, step_call, _ in live:
                step_call(block, *pieces(block)[index])
        for block, _, _, end_call in live:
            end_call(block)

    dk_ref[...] = dk_t_ref[...].T
    dv_ref[...] = dv_t_ref[...].T
    part_rows = cart_rows // dp_size
    me = lax.axis_index("dp")
    for step, ref in enumerate(cart_outs):
        target = lax.rem(me + step, dp_size)
        at = pl.ds(pl.multiple_of(target * part_rows, part_rows), part_rows)
        ref[0] = (dk_ref[at, :] * scale).astype(ref.dtype)
        ref[1] = dv_ref[at, :].astype(ref.dtype)
    own = dk_ref[cart_rows:all_keys, :] * scale, dv_ref[cart_rows:all_keys, :]
    if not last:
        dq_outs[0][...] = dq_ref[...]
        self_ref[0], self_ref[1] = own
        return
    own_tokens = tokens // heads_size
    columns = width * head_dim
    me = lax.axis_index("heads")
    for step, ref in enumerate(dq_outs):
        target = lax.rem(me + step, heads_size)
        at = pl.ds(pl.multiple_of(target * own_tokens, own_tokens), own_tokens)
        for index, before in enumerate((*dq_before, dq_ref)):
            ref[:, index * columns : (index + 1) * columns] = before[at, :]
    count = tokens * kv_local
    for kind in range(2):
        for index, before in enumerate(self_before):
            wide_ref[pl.ds(index, tokens, stride=kv_local), :] = before[kind]
        wide_ref[pl.ds(kv_index, tokens, stride=kv_local), :] = own[kind]
        self_ref[kind * count : (kind + 1) * count, :] = wide_ref[0:count, :].astype(bf16)


def order_kernel(*refs):
    pass


def sum_kernel(*refs):
    part_refs, out_ref = refs[:-1], refs[-1]
    total = part_refs[0][...]
    for ref in part_refs[1:]:
        total = total + ref[...].astype(f32)
    out_ref[...] = total


def cart_kernel(kv_local, *refs):
    done_refs, part_refs, out_ref = refs[: kv_local - 1], refs[kv_local - 1 : -2], refs[-1]
    part_rows = part_refs[0].shape[1]
    for kind in range(2):
        total = part_refs[0][kind]
        for ref in part_refs[1:]:
            total = total + ref[kind].astype(f32)
        for kv_index, part in enumerate((*[ref[kind] for ref in done_refs], total)):
            out_ref[pl.ds(kind * kv_local + kv_index, part_rows, stride=2 * kv_local), :] = part


def place_kernel(count, *refs):
    part_refs, out_ref = refs[:count], refs[-1]
    columns = part_refs[0].shape[1]
    me = lax.axis_index("heads")
    for step, ref in enumerate(part_refs):
        source = lax.rem(me + count - step, count)
        out_ref[:, pl.ds(pl.multiple_of(source * columns, columns), columns)] = ref[...]


def shift(values, axis, size, step):
    if step == 0:
        return values
    return lax.ppermute(values, axis, [(source, (source + step) % size) for source in range(size)])


def on_device(dp_size, heads_size, queries, out_grad, self_keys, self_values, cart_keys, cart_values, segment_ids):
    tokens, heads_local, head_dim = queries.shape
    kv_local = self_keys.shape[1]
    cart_rows = cart_keys.shape[0]
    width = heads_local // kv_local
    block_tokens = 64
    chunk = 512
    fine = 128
    all_keys = cart_rows + tokens
    rows = block_tokens * width
    part_rows = cart_rows // dp_size
    own_tokens = tokens // heads_size
    flat = [array.reshape(-1, head_dim) for array in (queries, out_grad, self_keys, self_values, cart_keys, cart_values)]
    macs = tokens * width * all_keys * head_dim * 5
    blocks = tokens // block_tokens
    columns = width * head_dim
    count = tokens * kv_local
    cart_list, query_list, self_list = [], [], []
    for kv_index in range(kv_local):
        last = kv_index == kv_local - 1
        if last:
            other_shapes = [jax.ShapeDtypeStruct((own_tokens, kv_local * columns), bf16) for _ in range(heads_size)]
            other_shapes.append(jax.ShapeDtypeStruct((2 * count, head_dim), bf16))
        else:
            other_shapes = [
                jax.ShapeDtypeStruct((tokens, columns), bf16),
                jax.ShapeDtypeStruct((2, tokens, head_dim), f32),
            ]
        before = query_list + self_list
        outs = pl.pallas_call(
            functools.partial(head_kernel, dp_size, heads_size, kv_index, kv_local, width, block_tokens, chunk, fine),
            out_shape=(
                *[
                    jax.ShapeDtypeStruct((2, part_rows, head_dim), bf16 if step else f32)
                    for step in range(dp_size)
                ],
                *other_shapes,
            ),
            in_specs=[pl.BlockSpec(memory_space=pltpu.HBM)] * 6
            + [pl.BlockSpec(memory_space=pltpu.VMEM)] * (1 + (len(before) if last else 0)),
            scratch_shapes=[
                pltpu.VMEM((cart_rows * kv_local, head_dim), f32),
                pltpu.VMEM((all_keys, head_dim), bf16),
                pltpu.VMEM((all_keys, head_dim), bf16),
                pltpu.VMEM((head_dim, all_keys), bf16),
                pltpu.VMEM((2, all_keys, rows), f32),
                pltpu.VMEM((2, all_keys, rows), f32),
                pltpu.VMEM((2, all_keys, rows), f32),
                pltpu.VMEM((head_dim, all_keys), f32),
                pltpu.VMEM((head_dim, all_keys), f32),
                pltpu.VMEM((all_keys, head_dim), f32),
                pltpu.VMEM((all_keys, head_dim), f32),
                pltpu.VMEM((rows, head_dim), f32),
                pltpu.VMEM((tokens, columns), bf16),
                *[pltpu.VMEM(array.shape, bf16) for array in flat],
                pltpu.SemaphoreType.DMA((4 + 2 * blocks,)),
            ],
            compiler_params=pltpu.CompilerParams(vmem_limit_bytes=vmem_bytes),
            cost_estimate=pl.CostEstimate(flops=4 * macs, bytes_accessed=5 * 2**20, transcendentals=tokens * width * all_keys),
            name="head_grads",
        )(*flat, segment_ids, *(before if last else []))
        sends = list(outs[1:dp_size])
        if last and cart_list:
            anywhere = pl.BlockSpec(memory_space=pl.ANY)
            sends = pl.pallas_call(
                order_kernel,
                out_shape=tuple(jax.ShapeDtypeStruct(array.shape, array.dtype) for array in sends),
                in_specs=[anywhere] * (len(sends) + len(cart_parts) - 1),
                out_specs=(anywhere,) * len(sends),
                input_output_aliases={index: index for index in range(len(sends))},
                cost_estimate=pl.CostEstimate(flops=32 * macs, bytes_accessed=0, transcendentals=0),
                name="order_sends",
            )(*sends, *cart_parts[1:])
        cart_parts = [outs[0]] + [shift(array, "dp", dp_size, step + 1) for step, array in enumerate(sends)]
        if last:
            query_list, self_grads = outs[dp_size:-1], outs[-1]
        else:
            query_list.append(outs[-2])
            self_list.append(outs[-1])
            cart_list.append(
                pl.pallas_call(
                    sum_kernel,
                    out_shape=jax.ShapeDtypeStruct((2, part_rows, head_dim), f32),
                    compiler_params=pltpu.CompilerParams(vmem_limit_bytes=vmem_bytes),
                    cost_estimate=pl.CostEstimate(flops=2**20, bytes_accessed=2**20, transcendentals=0),
                    name="cart_sum",
                )(*cart_parts)
            )
    query_list = [shift(part, "heads", heads_size, step) for step, part in enumerate(query_list)]
    query_grads = pl.pallas_call(
        functools.partial(place_kernel, heads_size),
        out_shape=jax.ShapeDtypeStruct((own_tokens, heads_size * heads_local * head_dim), bf16),
        in_specs=[pl.BlockSpec(memory_space=pltpu.VMEM)] * heads_size
        + [pl.BlockSpec(memory_space=pl.ANY)] * len(cart_list),
        compiler_params=pltpu.CompilerParams(vmem_limit_bytes=vmem_bytes),
        cost_estimate=pl.CostEstimate(flops=2**20, bytes_accessed=2 * 2**20, transcendentals=0),
        name="place_queries",
    )(*query_list, *cart_list)
    cart_grads = pl.pallas_call(
        functools.partial(cart_kernel, kv_local),
        out_shape=jax.ShapeDtypeStruct((part_rows * 2 * kv_local, head_dim), f32),
        in_specs=[pl.BlockSpec(memory_space=pltpu.VMEM)] * (len(cart_list) + dp_size)
        + [pl.BlockSpec(memory_space=pl.ANY)],
        compiler_params=pltpu.CompilerParams(vmem_limit_bytes=vmem_bytes),
        cost_estimate=pl.CostEstimate(flops=2**20, bytes_accessed=2 * 2**20, transcendentals=0),
        name="cart_grads",
    )(*cart_list, *cart_parts, query_grads)
    cart_grads = cart_grads.reshape(part_rows, 2, kv_local, head_dim)
    self_grads = self_grads.reshape(2, tokens, kv_local, head_dim)
    return (cart_grads, self_grads, query_grads)


def solution(mesh):
    in_specs = (
        P(("groups", "dp"), "heads", None),
        P(("groups", "dp"), "heads", None),
        P(("groups", "dp"), "heads", None),
        P(("groups", "dp"), "heads", None),
        P("groups", "heads", None),
        P("groups", "heads", None),
        P(("groups", "dp"), None),
    )
    out_specs = (
        P(("groups", "dp"), None, "heads", None),
        P(None, ("groups", "dp"), "heads", None),
        P(("groups", "dp", "heads"), None),
    )
    return jax.shard_map(
        functools.partial(on_device, mesh.shape["dp"], mesh.shape["heads"]),
        mesh=mesh, in_specs=in_specs, out_specs=out_specs, check_vma=False,
    )
```

```python
import functools
import math

import jax
import jax.numpy as jnp
from jax import lax
from jax.experimental import pallas as pl
from jax.experimental.pallas import tpu as pltpu
from jax.sharding import PartitionSpec as P

masked_score = -1e30
vmem_bytes = 56 * 1024 * 1024
f32 = jnp.float32
bf16 = jnp.bfloat16


def dot_nt(left, right):
    return lax.dot_general(left, right, (((1,), (1,)), ((), ())), preferred_element_type=f32)


def dot_nn(left, right):
    return lax.dot_general(left, right, (((1,), (0,)), ((), ())), preferred_element_type=f32)


def fold_rows(values, op):
    rows, columns = values.shape
    return op(values.reshape(rows // 8, 8, columns), axis=0)


def head_kernel(dp_size, heads_size, kv_index, kv_local, width, block_tokens, chunk, fine, sub, *refs):
    last = kv_index == kv_local - 1
    q_ref, g_ref, sk_ref, sv_ref, ck_ref, cv_ref, seg_ref = refs[:7]
    refs = refs[7:]
    held = kv_index if last else 0
    dq_before, self_before, refs = refs[:held], refs[held : 2 * held], refs[2 * held :]
    cart_outs, refs = refs[:dp_size], refs[dp_size:]
    dq_count = heads_size if last else 1
    dq_outs, self_ref, refs = refs[:dq_count], refs[dq_count], refs[dq_count + 1 :]
    (
        wide_ref, keys_ref, vals_ref, keys_t_ref, s_ref, w_ref, d_ref, p_ref, ds_ref, dk_ref, dv_ref, out_ref, dq_ref,
        q_in, g_in, sk_in, sv_in, ck_in, cv_in, sems,
    ) = refs
    head_dim = q_ref.shape[1]
    tokens = seg_ref.shape[1]
    cart_rows = ck_ref.shape[0] // kv_local
    all_keys = cart_rows + tokens
    rows = block_tokens * width
    scale = head_dim ** -0.5
    scale2 = scale * math.log2(math.e)
    span = block_tokens * kv_local * width
    blocks = tokens // block_tokens

    def block_copy(source, target, block, sem):
        at = slice(block * span, (block + 1) * span)
        return pltpu.make_async_copy(source.at[at, :], target.at[at, :], sems.at[sem])

    copies = {
        name: pltpu.make_async_copy(source, target, sems.at[at])
        for at, (name, source, target) in enumerate(
            [("ck", ck_ref, ck_in), ("sk", sk_ref, sk_in), ("cv", cv_ref, cv_in), ("sv", sv_ref, sv_in)]
        )
    }
    for block in range(blocks):
        copies["q", block] = block_copy(q_ref, q_in, block, 4 + block)
        copies["g", block] = block_copy(g_ref, g_in, block, 4 + blocks + block)
    order = ["ck", "sk", ("q", 0), "cv", "sv", ("g", 0)]
    order += [(kind, block) for block in range(1, blocks) for kind in ("q", "g")]
    for name in order:
        copies[name].start()

    def pick(name, ref, dst, at):
        copies[name].wait()
        count = ref.shape[0] // kv_local
        if kv_local == 1:
            dst[at : at + count, :] = ref[...]
        else:
            wide_ref[0 : ref.shape[0], :] = ref[...].astype(f32)
            dst[at : at + count, :] = wide_ref[pl.ds(kv_index, count, stride=kv_local), :].astype(bf16)

    def rows_of(name, ref, block):
        copies[name, block].wait()
        wide = ref[block * span : (block + 1) * span, :]
        if kv_local == 1:
            return wide
        wide = wide.astype(f32).reshape(block_tokens, kv_local, width, head_dim)
        return wide[:, kv_index].reshape(rows, head_dim).astype(bf16)

    first_count = jnp.sum((seg_ref[...] == 0).astype(f32), axis=1, keepdims=True).astype(jnp.int32)

    def limit(block):
        return -(-(block + 1) * block_tokens // fine) * fine

    def pieces(block):
        cart = [(start, chunk) for start in range(0, cart_rows, chunk)]
        return cart + [(cart_rows, limit(block))]

    queries, grads, peaks, stats = {}, {}, {}, {}
    acc = {}

    def subs(start, size):
        return [slice(at, at + sub) for at in range(start, start + size, sub)]

    def open_scores(block):
        queries[block] = rows_of("q", q_in, block)
        token = (lax.broadcasted_iota(jnp.int32, (1, rows), 1) + block * rows) // width
        begin = jnp.where(token >= first_count, first_count, 0)
        acc["peak"] = jnp.full((8, rows), masked_score, f32)
        acc["token"], acc["begin"] = token, begin

    def step_scores(block, start, size):
        s_ref[block % 2, start : start + size, :] = dot_nt(keys_ref[start : start + size, :], queries[block])
        for at in subs(start, size):
            score = s_ref[block % 2, at, :]
            if start >= cart_rows:
                key_at = lax.broadcasted_iota(jnp.int32, (sub, rows), 0) + (at.start - cart_rows)
                score = jnp.where((key_at >= acc["begin"]) & (key_at <= acc["token"]), score, masked_score)
                s_ref[block % 2, at, :] = score
            acc["peak"] = jnp.maximum(acc["peak"], fold_rows(score, jnp.max))

    def close_scores(block):
        peaks[block] = jnp.max(acc["peak"], axis=0, keepdims=True)

    def open_weights(block):
        grads[block] = rows_of("g", g_in, block)
        acc["total"] = jnp.zeros((8, rows), f32)
        acc["center"] = jnp.zeros((8, rows), f32)

    def step_weights(block, start, size):
        d_ref[block % 2, start : start + size, :] = dot_nt(vals_ref[start : start + size, :], grads[block])
        for at in subs(start, size):
            weight = jnp.exp2((s_ref[block % 2, at, :] - peaks[block]) * scale2)
            w_ref[block % 2, at, :] = weight
            acc["total"] = acc["total"] + fold_rows(weight, jnp.sum)
            acc["center"] = acc["center"] + fold_rows(weight * d_ref[block % 2, at, :], jnp.sum)

    def close_weights(block):
        share = 1.0 / jnp.sum(acc["total"], axis=0, keepdims=True)
        stats[block] = share, jnp.sum(acc["center"], axis=0, keepdims=True) * share

    def open_grads(block):
        acc["dq"] = jnp.zeros((head_dim, rows), f32)

    def step_grads(block, start, size):
        share, center = stats[block]
        for at in subs(start, size):
            prob = w_ref[block % 2, at, :] * share
            p_ref[at, :] = prob.astype(bf16)
            ds_ref[at, :] = (prob * (d_ref[block % 2, at, :] - center)).astype(bf16)
        at = slice(start, start + size)
        old = size if start < cart_rows else (limit(block - 1) if block else 0)
        old = old if block else 0
        for ref, left, right in ((dv_ref, p_ref, grads[block]), (dk_ref, ds_ref, queries[block])):
            part = dot_nn(left[at, :], right)
            if old:
                ref[start : start + old, :] += part[:old]
            if old < size:
                ref[start + old : start + size, :] = part[old:]
        acc["dq"] = acc["dq"] + dot_nn(keys_t_ref[:, at], ds_ref[at, :])

    def close_grads(block):
        out_ref[...] = (acc["dq"] * scale).T
        for head in range(width):
            dq_ref[block * block_tokens : (block + 1) * block_tokens, head * head_dim : (head + 1) * head_dim] = (
                out_ref[pl.ds(head, block_tokens, stride=width), :].astype(bf16)
            )

    pick("ck", ck_in, keys_ref, 0)
    pick("sk", sk_in, keys_ref, cart_rows)
    stages = (
        (2, open_grads, step_grads, close_grads),
        (1, open_weights, step_weights, close_weights),
        (0, open_scores, step_scores, close_scores),
    )
    for turn in range(blocks + 2):
        live = [(turn - lag, *calls) for lag, *calls in stages if 0 <= turn - lag < blocks]
        if turn == 1:
            pick("cv", cv_in, vals_ref, 0)
            pick("sv", sv_in, vals_ref, cart_rows)
            keys_t_ref[...] = keys_ref[...].astype(f32).T.astype(bf16)
        for block, begin_call, _, _ in live:
            begin_call(block)
        for index in range(len(pieces(0))):
            for block, _, step_call, _ in live:
                step_call(block, *pieces(block)[index])
        for block, _, _, end_call in live:
            end_call(block)

    part_rows = cart_rows // dp_size
    me = lax.axis_index("dp")
    for step, ref in enumerate(cart_outs):
        target = lax.rem(me + step, dp_size)
        at = pl.ds(pl.multiple_of(target * part_rows, part_rows), part_rows)
        ref[0] = (dk_ref[at, :] * scale).astype(ref.dtype)
        ref[1] = dv_ref[at, :].astype(ref.dtype)
    own = dk_ref[cart_rows:all_keys, :] * scale, dv_ref[cart_rows:all_keys, :]
    if not last:
        dq_outs[0][...] = dq_ref[...]
        self_ref[0], self_ref[1] = own
        return
    own_tokens = tokens // heads_size
    columns = width * head_dim
    me = lax.axis_index("heads")
    for step, ref in enumerate(dq_outs):
        target = lax.rem(me + step, heads_size)
        at = pl.ds(pl.multiple_of(target * own_tokens, own_tokens), own_tokens)
        for index, before in enumerate((*dq_before, dq_ref)):
            ref[:, index * columns : (index + 1) * columns] = before[at, :]
    count = tokens * kv_local
    for kind in range(2):
        for index, before in enumerate(self_before):
            wide_ref[pl.ds(index, tokens, stride=kv_local), :] = before[kind]
        wide_ref[pl.ds(kv_index, tokens, stride=kv_local), :] = own[kind]
        self_ref[kind * count : (kind + 1) * count, :] = wide_ref[0:count, :].astype(bf16)


def order_kernel(*refs):
    pass


def sum_kernel(*refs):
    part_refs, out_ref = refs[:-1], refs[-1]
    total = part_refs[0][...]
    for ref in part_refs[1:]:
        total = total + ref[...].astype(f32)
    out_ref[...] = total


def cart_kernel(kv_local, *refs):
    done_refs, part_refs, out_ref = refs[: kv_local - 1], refs[kv_local - 1 : -2], refs[-1]
    part_rows = part_refs[0].shape[1]
    for kind in range(2):
        total = part_refs[0][kind]
        for ref in part_refs[1:]:
            total = total + ref[kind].astype(f32)
        for kv_index, part in enumerate((*[ref[kind] for ref in done_refs], total)):
            out_ref[pl.ds(kind * kv_local + kv_index, part_rows, stride=2 * kv_local), :] = part


def place_kernel(count, *refs):
    part_refs, out_ref = refs[:count], refs[-1]
    columns = part_refs[0].shape[1]
    me = lax.axis_index("heads")
    for step, ref in enumerate(part_refs):
        source = lax.rem(me + count - step, count)
        out_ref[:, pl.ds(pl.multiple_of(source * columns, columns), columns)] = ref[...]


def shift(values, axis, size, step):
    if step == 0:
        return values
    return lax.ppermute(values, axis, [(source, (source + step) % size) for source in range(size)])


def on_device(dp_size, heads_size, queries, out_grad, self_keys, self_values, cart_keys, cart_values, segment_ids):
    tokens, heads_local, head_dim = queries.shape
    kv_local = self_keys.shape[1]
    cart_rows = cart_keys.shape[0]
    width = heads_local // kv_local
    block_tokens = 64
    chunk = 256
    fine = 128
    sub = 16
    all_keys = cart_rows + tokens
    rows = block_tokens * width
    part_rows = cart_rows // dp_size
    own_tokens = tokens // heads_size
    flat = [array.reshape(-1, head_dim) for array in (queries, out_grad, self_keys, self_values, cart_keys, cart_values)]
    macs = tokens * width * all_keys * head_dim * 5
    blocks = tokens // block_tokens
    columns = width * head_dim
    count = tokens * kv_local
    cart_list, query_list, self_list = [], [], []
    for kv_index in range(kv_local):
        last = kv_index == kv_local - 1
        if last:
            other_shapes = [jax.ShapeDtypeStruct((own_tokens, kv_local * columns), bf16) for _ in range(heads_size)]
            other_shapes.append(jax.ShapeDtypeStruct((2 * count, head_dim), bf16))
        else:
            other_shapes = [
                jax.ShapeDtypeStruct((tokens, columns), bf16),
                jax.ShapeDtypeStruct((2, tokens, head_dim), f32),
            ]
        before = query_list + self_list
        outs = pl.pallas_call(
            functools.partial(head_kernel, dp_size, heads_size, kv_index, kv_local, width, block_tokens, chunk, fine, sub),
            out_shape=(
                *[
                    jax.ShapeDtypeStruct((2, part_rows, head_dim), bf16 if step else f32)
                    for step in range(dp_size)
                ],
                *other_shapes,
            ),
            in_specs=[pl.BlockSpec(memory_space=pltpu.HBM)] * 6
            + [pl.BlockSpec(memory_space=pltpu.VMEM)] * (1 + (len(before) if last else 0)),
            scratch_shapes=[
                pltpu.VMEM((cart_rows * kv_local, head_dim), f32),
                pltpu.VMEM((all_keys, head_dim), bf16),
                pltpu.VMEM((all_keys, head_dim), bf16),
                pltpu.VMEM((head_dim, all_keys), bf16),
                pltpu.VMEM((2, all_keys, rows), f32),
                pltpu.VMEM((2, all_keys, rows), f32),
                pltpu.VMEM((2, all_keys, rows), f32),
                pltpu.VMEM((all_keys, rows), bf16),
                pltpu.VMEM((all_keys, rows), bf16),
                pltpu.VMEM((all_keys, head_dim), f32),
                pltpu.VMEM((all_keys, head_dim), f32),
                pltpu.VMEM((rows, head_dim), f32),
                pltpu.VMEM((tokens, columns), bf16),
                *[pltpu.VMEM(array.shape, bf16) for array in flat],
                pltpu.SemaphoreType.DMA((4 + 2 * blocks,)),
            ],
            compiler_params=pltpu.CompilerParams(vmem_limit_bytes=vmem_bytes),
            cost_estimate=pl.CostEstimate(flops=4 * macs, bytes_accessed=5 * 2**20, transcendentals=tokens * width * all_keys),
            name="head_grads",
        )(*flat, segment_ids, *(before if last else []))
        sends = list(outs[1:dp_size])
        if last and cart_list:
            anywhere = pl.BlockSpec(memory_space=pl.ANY)
            sends = pl.pallas_call(
                order_kernel,
                out_shape=tuple(jax.ShapeDtypeStruct(array.shape, array.dtype) for array in sends),
                in_specs=[anywhere] * (len(sends) + len(cart_parts) - 1),
                out_specs=(anywhere,) * len(sends),
                input_output_aliases={index: index for index in range(len(sends))},
                cost_estimate=pl.CostEstimate(flops=32 * macs, bytes_accessed=0, transcendentals=0),
                name="order_sends",
            )(*sends, *cart_parts[1:])
        cart_parts = [outs[0]] + [shift(array, "dp", dp_size, step + 1) for step, array in enumerate(sends)]
        if last:
            query_list, self_grads = outs[dp_size:-1], outs[-1]
        else:
            query_list.append(outs[-2])
            self_list.append(outs[-1])
            cart_list.append(
                pl.pallas_call(
                    sum_kernel,
                    out_shape=jax.ShapeDtypeStruct((2, part_rows, head_dim), f32),
                    compiler_params=pltpu.CompilerParams(vmem_limit_bytes=vmem_bytes),
                    cost_estimate=pl.CostEstimate(flops=2**20, bytes_accessed=2**20, transcendentals=0),
                    name="cart_sum",
                )(*cart_parts)
            )
    query_list = [shift(part, "heads", heads_size, step) for step, part in enumerate(query_list)]
    query_grads = pl.pallas_call(
        functools.partial(place_kernel, heads_size),
        out_shape=jax.ShapeDtypeStruct((own_tokens, heads_size * heads_local * head_dim), bf16),
        in_specs=[pl.BlockSpec(memory_space=pltpu.VMEM)] * heads_size
        + [pl.BlockSpec(memory_space=pl.ANY)] * len(cart_list),
        compiler_params=pltpu.CompilerParams(vmem_limit_bytes=vmem_bytes),
        cost_estimate=pl.CostEstimate(flops=2**20, bytes_accessed=2 * 2**20, transcendentals=0),
        name="place_queries",
    )(*query_list, *cart_list)
    cart_grads = pl.pallas_call(
        functools.partial(cart_kernel, kv_local),
        out_shape=jax.ShapeDtypeStruct((part_rows * 2 * kv_local, head_dim), f32),
        in_specs=[pl.BlockSpec(memory_space=pltpu.VMEM)] * (len(cart_list) + dp_size)
        + [pl.BlockSpec(memory_space=pl.ANY)],
        compiler_params=pltpu.CompilerParams(vmem_limit_bytes=vmem_bytes),
        cost_estimate=pl.CostEstimate(flops=2**20, bytes_accessed=2 * 2**20, transcendentals=0),
        name="cart_grads",
    )(*cart_list, *cart_parts, query_grads)
    cart_grads = cart_grads.reshape(part_rows, 2, kv_local, head_dim)
    self_grads = self_grads.reshape(2, tokens, kv_local, head_dim)
    return (cart_grads, self_grads, query_grads)


def solution(mesh):
    in_specs = (
        P(("groups", "dp"), "heads", None),
        P(("groups", "dp"), "heads", None),
        P(("groups", "dp"), "heads", None),
        P(("groups", "dp"), "heads", None),
        P("groups", "heads", None),
        P("groups", "heads", None),
        P(("groups", "dp"), None),
    )
    out_specs = (
        P(("groups", "dp"), None, "heads", None),
        P(None, ("groups", "dp"), "heads", None),
        P(("groups", "dp", "heads"), None),
    )
    return jax.shard_map(
        functools.partial(on_device, mesh.shape["dp"], mesh.shape["heads"]),
        mesh=mesh, in_specs=in_specs, out_specs=out_specs, check_vma=False,
    )
```

```python
import functools
import math

import jax
import jax.numpy as jnp
from jax import lax
from jax.experimental import pallas as pl
from jax.experimental.pallas import tpu as pltpu
from jax.sharding import PartitionSpec as P

masked_score = -1e30
vmem_bytes = 56 * 1024 * 1024
f32 = jnp.float32
bf16 = jnp.bfloat16


def dot_nt(left, right):
    return lax.dot_general(left, right, (((1,), (1,)), ((), ())), preferred_element_type=f32)


def dot_nn(left, right):
    return lax.dot_general(left, right, (((1,), (0,)), ((), ())), preferred_element_type=f32)


def fold_rows(values, op):
    rows, columns = values.shape
    return op(values.reshape(rows // 8, 8, columns), axis=0)


def head_kernel(dp_size, heads_size, kv_index, kv_local, width, block_tokens, chunk, sub, *refs):
    last = kv_index == kv_local - 1
    q_ref, g_ref, sk_ref, sv_ref, ck_ref, cv_ref, seg_ref = refs[:7]
    refs = refs[7:]
    held = kv_index if last else 0
    dq_before, self_before, refs = refs[:held], refs[held : 2 * held], refs[2 * held :]
    cart_outs, refs = refs[:dp_size], refs[dp_size:]
    dq_count = heads_size if last else 1
    dq_outs, self_ref, refs = refs[:dq_count], refs[dq_count], refs[dq_count + 1 :]
    (
        wide_ref, keys_ref, vals_ref, keys_t_ref, s_even, s_odd, w_even, w_odd, d_even, d_odd, p_ref, ds_ref, dk_ref, dv_ref, out_ref, dq_ref,
        q_rows, g_rows, q_in, g_in, sk_in, sv_in, ck_in, cv_in, sems,
    ) = refs
    head_dim = q_ref.shape[1]
    tokens = seg_ref.shape[1]
    cart_rows = ck_ref.shape[0] // kv_local
    all_keys = cart_rows + tokens
    rows = block_tokens * width
    scale = head_dim ** -0.5
    scale2 = scale * math.log2(math.e)
    span = block_tokens * kv_local * width
    blocks = tokens // block_tokens

    def block_copy(source, target, block, sem):
        at = slice(block * span, (block + 1) * span)
        return pltpu.make_async_copy(source.at[at, :], target.at[at, :], sems.at[sem])

    copies = {
        name: pltpu.make_async_copy(source, target, sems.at[at])
        for at, (name, source, target) in enumerate(
            [("ck", ck_ref, ck_in), ("sk", sk_ref, sk_in), ("cv", cv_ref, cv_in), ("sv", sv_ref, sv_in)]
        )
    }
    for block in range(blocks):
        copies["q", block] = block_copy(q_ref, q_in, block, 4 + block)
        copies["g", block] = block_copy(g_ref, g_in, block, 4 + blocks + block)
    order = ["ck", "sk", ("q", 0), "cv", "sv", ("g", 0)]
    order += [(kind, block) for block in range(1, blocks) for kind in ("q", "g")]
    for name in order:
        copies[name].start()

    def pick(name, ref, dst, at):
        copies[name].wait()
        count = ref.shape[0] // kv_local
        if kv_local == 1:
            dst[at : at + count, :] = ref[...]
        else:
            wide_ref[0 : ref.shape[0], :] = ref[...].astype(f32)
            dst[at : at + count, :] = wide_ref[pl.ds(kv_index, count, stride=kv_local), :].astype(bf16)

    def fill_rows(ref, dst, block):
        wide = ref[block * span : (block + 1) * span, :]
        if kv_local > 1:
            wide = wide.astype(f32).reshape(block_tokens, kv_local, width, head_dim)
            wide = wide[:, kv_index].reshape(rows, head_dim).astype(bf16)
        dst[block] = wide

    first_count = jnp.sum((seg_ref[...] == 0).astype(f32), axis=1, keepdims=True).astype(jnp.int32)

    s_refs, w_refs, d_refs = (s_even, s_odd), (w_even, w_odd), (d_even, d_odd)

    def chunk_step(turn, live, carry, start, size, own):
        peak, peak8, total8, center8, share, center = carry
        scoring, weighing, grading = live
        whole = pl.ds(start, size)
        if grading:
            block, slot = turn - 2, (turn - 2) % 2
            for at in range(0, size, sub):
                here = pl.ds(start + at, sub)
                prob = w_refs[slot][here, :] * share
                p_ref[here, :] = prob.astype(bf16)
                ds_ref[here, :] = (prob * (d_refs[slot][here, :] - center)).astype(bf16)
        if scoring:
            s_refs[turn % 2][whole, :] = dot_nt(keys_ref[whole, :], q_rows[turn])
        if weighing:
            d_refs[(turn - 1) % 2][whole, :] = dot_nt(vals_ref[whole, :], g_rows[turn - 1])
        if grading:
            dv_ref[whole, :] += dot_nn(p_ref[whole, :], g_rows[block])
            dk_ref[whole, :] += dot_nn(ds_ref[whole, :], q_rows[block])
        if weighing:
            slot = (turn - 1) % 2
            for at in range(0, size, sub):
                here = pl.ds(start + at, sub)
                weight = jnp.exp2((s_refs[slot][here, :] - peak) * scale2)
                w_refs[slot][here, :] = weight
                total8 = total8 + fold_rows(weight, jnp.sum)
                center8 = center8 + fold_rows(weight * d_refs[slot][here, :], jnp.sum)
        if scoring:
            slot = turn % 2
            if own:
                token = (lax.broadcasted_iota(jnp.int32, (1, rows), 1) + turn * rows) // width
                begin = jnp.where(token >= first_count, first_count, 0)
            for at in range(0, size, sub):
                here = pl.ds(start + at, sub)
                score = s_refs[slot][here, :]
                if own:
                    key_at = lax.broadcasted_iota(jnp.int32, (sub, rows), 0) + at
                    score = jnp.where((key_at >= begin) & (key_at <= token), score, masked_score)
                    s_refs[slot][here, :] = score
                peak8 = jnp.maximum(peak8, fold_rows(score, jnp.max))
        return peak, peak8, total8, center8, share, center

    def run_turn(turn, live, peak, share, center):
        if live[0]:
            fill_rows(q_in, q_rows, turn)
        if live[1]:
            fill_rows(g_in, g_rows, turn - 1)
        carry = (
            peak, jnp.full((8, rows), masked_score, f32), jnp.zeros((8, rows), f32), jnp.zeros((8, rows), f32),
            share, center,
        )

        def step(index, carry):
            return chunk_step(turn, live, carry, pl.multiple_of(index * chunk, chunk), chunk, False)

        carry = lax.fori_loop(0, cart_rows // chunk, step, carry)
        carry = chunk_step(turn, live, carry, cart_rows, tokens, True)
        _, peak8, total8, center8, _, _ = carry
        if live[2]:
            out_ref[...] = (dot_nn(keys_t_ref[...], ds_ref[...]) * scale).T
            at = slice((turn - 2) * block_tokens, (turn - 1) * block_tokens)
            for head in range(width):
                dq_ref[at, head * head_dim : (head + 1) * head_dim] = (
                    out_ref[pl.ds(head, block_tokens, stride=width), :].astype(bf16)
                )
        peak = jnp.max(peak8, axis=0, keepdims=True)
        if live[1]:
            share = 1.0 / jnp.sum(total8, axis=0, keepdims=True)
            center = jnp.sum(center8, axis=0, keepdims=True) * share
        return peak, share, center

    dk_ref[...] = jnp.zeros_like(dk_ref)
    dv_ref[...] = jnp.zeros_like(dv_ref)
    pick("ck", ck_in, keys_ref, 0)
    pick("sk", sk_in, keys_ref, cart_rows)
    copies["q", 0].wait()
    empty = jnp.zeros((1, rows), f32)
    state = run_turn(0, (True, False, False), empty, empty, empty)
    pick("cv", cv_in, vals_ref, 0)
    pick("sv", sv_in, vals_ref, cart_rows)
    keys_t_ref[...] = keys_ref[...].astype(f32).T.astype(bf16)
    for turn in range(1, blocks + 2):
        live = turn < blocks, turn <= blocks, turn > 1
        if live[0]:
            copies["q", turn].wait()
        if live[1]:
            copies["g", turn - 1].wait()
        state = run_turn(turn, live, *state)

    part_rows = cart_rows // dp_size
    me = lax.axis_index("dp")
    for step, ref in enumerate(cart_outs):
        target = lax.rem(me + step, dp_size)
        at = pl.ds(pl.multiple_of(target * part_rows, part_rows), part_rows)
        ref[0] = (dk_ref[at, :] * scale).astype(ref.dtype)
        ref[1] = dv_ref[at, :].astype(ref.dtype)
    own = dk_ref[cart_rows:all_keys, :] * scale, dv_ref[cart_rows:all_keys, :]
    if not last:
        dq_outs[0][...] = dq_ref[...]
        self_ref[0], self_ref[1] = own
        return
    own_tokens = tokens // heads_size
    columns = width * head_dim
    me = lax.axis_index("heads")
    for step, ref in enumerate(dq_outs):
        target = lax.rem(me + step, heads_size)
        at = pl.ds(pl.multiple_of(target * own_tokens, own_tokens), own_tokens)
        for index, before in enumerate((*dq_before, dq_ref)):
            ref[:, index * columns : (index + 1) * columns] = before[at, :]
    count = tokens * kv_local
    for kind in range(2):
        for index, before in enumerate(self_before):
            wide_ref[pl.ds(index, tokens, stride=kv_local), :] = before[kind]
        wide_ref[pl.ds(kv_index, tokens, stride=kv_local), :] = own[kind]
        self_ref[kind * count : (kind + 1) * count, :] = wide_ref[0:count, :].astype(bf16)


def order_kernel(*refs):
    pass


def sum_kernel(*refs):
    part_refs, out_ref = refs[:-1], refs[-1]
    total = part_refs[0][...]
    for ref in part_refs[1:]:
        total = total + ref[...].astype(f32)
    out_ref[...] = total


def cart_kernel(kv_local, *refs):
    done_refs, part_refs, out_ref = refs[: kv_local - 1], refs[kv_local - 1 : -2], refs[-1]
    part_rows = part_refs[0].shape[1]
    for kind in range(2):
        total = part_refs[0][kind]
        for ref in part_refs[1:]:
            total = total + ref[kind].astype(f32)
        for kv_index, part in enumerate((*[ref[kind] for ref in done_refs], total)):
            out_ref[pl.ds(kind * kv_local + kv_index, part_rows, stride=2 * kv_local), :] = part


def place_kernel(count, *refs):
    part_refs, out_ref = refs[:count], refs[-1]
    columns = part_refs[0].shape[1]
    me = lax.axis_index("heads")
    for step, ref in enumerate(part_refs):
        source = lax.rem(me + count - step, count)
        out_ref[:, pl.ds(pl.multiple_of(source * columns, columns), columns)] = ref[...]


def shift(values, axis, size, step):
    if step == 0:
        return values
    return lax.ppermute(values, axis, [(source, (source + step) % size) for source in range(size)])


def on_device(dp_size, heads_size, queries, out_grad, self_keys, self_values, cart_keys, cart_values, segment_ids):
    tokens, heads_local, head_dim = queries.shape
    kv_local = self_keys.shape[1]
    cart_rows = cart_keys.shape[0]
    width = heads_local // kv_local
    block_tokens = 64
    chunk = 256
    sub = 16
    all_keys = cart_rows + tokens
    rows = block_tokens * width
    part_rows = cart_rows // dp_size
    own_tokens = tokens // heads_size
    flat = [array.reshape(-1, head_dim) for array in (queries, out_grad, self_keys, self_values, cart_keys, cart_values)]
    macs = tokens * width * all_keys * head_dim * 5
    blocks = tokens // block_tokens
    columns = width * head_dim
    count = tokens * kv_local
    cart_list, query_list, self_list = [], [], []
    for kv_index in range(kv_local):
        last = kv_index == kv_local - 1
        if last:
            other_shapes = [jax.ShapeDtypeStruct((own_tokens, kv_local * columns), bf16) for _ in range(heads_size)]
            other_shapes.append(jax.ShapeDtypeStruct((2 * count, head_dim), bf16))
        else:
            other_shapes = [
                jax.ShapeDtypeStruct((tokens, columns), bf16),
                jax.ShapeDtypeStruct((2, tokens, head_dim), f32),
            ]
        before = query_list + self_list
        outs = pl.pallas_call(
            functools.partial(head_kernel, dp_size, heads_size, kv_index, kv_local, width, block_tokens, chunk, sub),
            out_shape=(
                *[
                    jax.ShapeDtypeStruct((2, part_rows, head_dim), bf16 if step else f32)
                    for step in range(dp_size)
                ],
                *other_shapes,
            ),
            in_specs=[pl.BlockSpec(memory_space=pltpu.HBM)] * 6
            + [pl.BlockSpec(memory_space=pltpu.VMEM)] * (1 + (len(before) if last else 0)),
            scratch_shapes=[
                pltpu.VMEM((cart_rows * kv_local, head_dim), f32),
                pltpu.VMEM((all_keys, head_dim), bf16),
                pltpu.VMEM((all_keys, head_dim), bf16),
                pltpu.VMEM((head_dim, all_keys), bf16),
                *[pltpu.VMEM((all_keys, rows), f32) for _ in range(6)],
                pltpu.VMEM((all_keys, rows), bf16),
                pltpu.VMEM((all_keys, rows), bf16),
                pltpu.VMEM((all_keys, head_dim), f32),
                pltpu.VMEM((all_keys, head_dim), f32),
                pltpu.VMEM((rows, head_dim), f32),
                pltpu.VMEM((tokens, columns), bf16),
                pltpu.VMEM((blocks, rows, head_dim), bf16),
                pltpu.VMEM((blocks, rows, head_dim), bf16),
                *[pltpu.VMEM(array.shape, bf16) for array in flat],
                pltpu.SemaphoreType.DMA((4 + 2 * blocks,)),
            ],
            compiler_params=pltpu.CompilerParams(vmem_limit_bytes=vmem_bytes),
            cost_estimate=pl.CostEstimate(flops=4 * macs, bytes_accessed=5 * 2**20, transcendentals=tokens * width * all_keys),
            name="head_grads",
        )(*flat, segment_ids, *(before if last else []))
        sends = list(outs[1:dp_size])
        if last and cart_list:
            anywhere = pl.BlockSpec(memory_space=pl.ANY)
            sends = pl.pallas_call(
                order_kernel,
                out_shape=tuple(jax.ShapeDtypeStruct(array.shape, array.dtype) for array in sends),
                in_specs=[anywhere] * (len(sends) + len(cart_parts) - 1),
                out_specs=(anywhere,) * len(sends),
                input_output_aliases={index: index for index in range(len(sends))},
                cost_estimate=pl.CostEstimate(flops=32 * macs, bytes_accessed=0, transcendentals=0),
                name="order_sends",
            )(*sends, *cart_parts[1:])
        cart_parts = [outs[0]] + [shift(array, "dp", dp_size, step + 1) for step, array in enumerate(sends)]
        if last:
            query_list, self_grads = outs[dp_size:-1], outs[-1]
        else:
            query_list.append(outs[-2])
            self_list.append(outs[-1])
            cart_list.append(
                pl.pallas_call(
                    sum_kernel,
                    out_shape=jax.ShapeDtypeStruct((2, part_rows, head_dim), f32),
                    compiler_params=pltpu.CompilerParams(vmem_limit_bytes=vmem_bytes),
                    cost_estimate=pl.CostEstimate(flops=2**20, bytes_accessed=2**20, transcendentals=0),
                    name="cart_sum",
                )(*cart_parts)
            )
    query_list = [shift(part, "heads", heads_size, step) for step, part in enumerate(query_list)]
    query_grads = pl.pallas_call(
        functools.partial(place_kernel, heads_size),
        out_shape=jax.ShapeDtypeStruct((own_tokens, heads_size * heads_local * head_dim), bf16),
        in_specs=[pl.BlockSpec(memory_space=pltpu.VMEM)] * heads_size
        + [pl.BlockSpec(memory_space=pl.ANY)] * len(cart_list),
        compiler_params=pltpu.CompilerParams(vmem_limit_bytes=vmem_bytes),
        cost_estimate=pl.CostEstimate(flops=2**20, bytes_accessed=2 * 2**20, transcendentals=0),
        name="place_queries",
    )(*query_list, *cart_list)
    cart_grads = pl.pallas_call(
        functools.partial(cart_kernel, kv_local),
        out_shape=jax.ShapeDtypeStruct((part_rows * 2 * kv_local, head_dim), f32),
        in_specs=[pl.BlockSpec(memory_space=pltpu.VMEM)] * (len(cart_list) + dp_size)
        + [pl.BlockSpec(memory_space=pl.ANY)],
        compiler_params=pltpu.CompilerParams(vmem_limit_bytes=vmem_bytes),
        cost_estimate=pl.CostEstimate(flops=2**20, bytes_accessed=2 * 2**20, transcendentals=0),
        name="cart_grads",
    )(*cart_list, *cart_parts, query_grads)
    cart_grads = cart_grads.reshape(part_rows, 2, kv_local, head_dim)
    self_grads = self_grads.reshape(2, tokens, kv_local, head_dim)
    return (cart_grads, self_grads, query_grads)


def solution(mesh):
    in_specs = (
        P(("groups", "dp"), "heads", None),
        P(("groups", "dp"), "heads", None),
        P(("groups", "dp"), "heads", None),
        P(("groups", "dp"), "heads", None),
        P("groups", "heads", None),
        P("groups", "heads", None),
        P(("groups", "dp"), None),
    )
    out_specs = (
        P(("groups", "dp"), None, "heads", None),
        P(None, ("groups", "dp"), "heads", None),
        P(("groups", "dp", "heads"), None),
    )
    return jax.shard_map(
        functools.partial(on_device, mesh.shape["dp"], mesh.shape["heads"]),
        mesh=mesh, in_specs=in_specs, out_specs=out_specs, check_vma=False,
    )
```

```python
import functools
import math

import jax
import jax.numpy as jnp
from jax import lax
from jax.experimental import pallas as pl
from jax.experimental.pallas import tpu as pltpu
from jax.sharding import PartitionSpec as P

masked_score = -1e30
vmem_bytes = 56 * 1024 * 1024
small_vmem_bytes = 8 * 1024 * 1024
f32 = jnp.float32
bf16 = jnp.bfloat16


def dot_nt(left, right):
    return lax.dot_general(left, right, (((1,), (1,)), ((), ())), preferred_element_type=f32)


def dot_nn(left, right):
    return lax.dot_general(left, right, (((1,), (0,)), ((), ())), preferred_element_type=f32)


def fold_rows(values, op):
    rows, columns = values.shape
    return op(values.reshape(rows // 8, 8, columns), axis=0)


def head_kernel(dp_size, heads_size, kv_index, kv_local, width, block_tokens, chunk, fine, sub, *refs):
    last = kv_index == kv_local - 1
    q_ref, g_ref, sk_ref, sv_ref, ck_ref, cv_ref, seg_ref = refs[:7]
    refs = refs[7:]
    held = kv_index if last else 0
    dq_before, self_before, refs = refs[:held], refs[held : 2 * held], refs[2 * held :]
    cart_outs, refs = refs[:dp_size], refs[dp_size:]
    dq_count = heads_size if last else 1
    dq_outs, self_ref, refs = refs[:dq_count], refs[dq_count], refs[dq_count + 1 :]
    (
        wide_ref, keys_ref, vals_ref, keys_t_ref, s_ref, w_ref, d_ref, p_ref, ds_ref, dk_ref, dv_ref, out_ref, dq_ref,
        q_in, g_in, sk_in, sv_in, ck_in, cv_in, sems,
    ) = refs
    head_dim = q_ref.shape[1]
    tokens = seg_ref.shape[1]
    cart_rows = ck_ref.shape[0] // kv_local
    all_keys = cart_rows + tokens
    rows = block_tokens * width
    scale = head_dim ** -0.5
    scale2 = scale * math.log2(math.e)
    span = block_tokens * kv_local * width
    blocks = tokens // block_tokens

    def block_copy(source, target, block, sem):
        at = slice(block * span, (block + 1) * span)
        return pltpu.make_async_copy(source.at[at, :], target.at[at, :], sems.at[sem])

    copies = {
        name: pltpu.make_async_copy(source, target, sems.at[at])
        for at, (name, source, target) in enumerate(
            [("ck", ck_ref, ck_in), ("sk", sk_ref, sk_in), ("cv", cv_ref, cv_in), ("sv", sv_ref, sv_in)]
        )
    }
    for block in range(blocks):
        copies["q", block] = block_copy(q_ref, q_in, block, 4 + block)
        copies["g", block] = block_copy(g_ref, g_in, block, 4 + blocks + block)
    order = ["ck", "sk", ("q", 0), "cv", "sv", ("g", 0)]
    order += [(kind, block) for block in range(1, blocks) for kind in ("q", "g")]
    for name in order:
        copies[name].start()

    def pick(name, ref, dst, at):
        copies[name].wait()
        count = ref.shape[0] // kv_local
        if kv_local == 1:
            dst[at : at + count, :] = ref[...]
        else:
            wide_ref[0 : ref.shape[0], :] = ref[...].astype(f32)
            dst[at : at + count, :] = wide_ref[pl.ds(kv_index, count, stride=kv_local), :].astype(bf16)

    def rows_of(name, ref, block):
        copies[name, block].wait()
        wide = ref[block * span : (block + 1) * span, :]
        if kv_local == 1:
            return wide
        wide = wide.astype(f32).reshape(block_tokens, kv_local, width, head_dim)
        return wide[:, kv_index].reshape(rows, head_dim).astype(bf16)

    first_count = jnp.sum((seg_ref[...] == 0).astype(f32), axis=1, keepdims=True).astype(jnp.int32)

    def limit(block):
        return -(-(block + 1) * block_tokens // fine) * fine

    def pieces(block):
        cart = [(start, chunk) for start in range(0, cart_rows, chunk)]
        return cart + [(cart_rows, limit(block))]

    queries, grads, peaks, stats = {}, {}, {}, {}
    acc = {}

    def subs(start, size):
        return [slice(at, at + sub) for at in range(start, start + size, sub)]

    def open_scores(block):
        queries[block] = rows_of("q", q_in, block)
        token = (lax.broadcasted_iota(jnp.int32, (1, rows), 1) + block * rows) // width
        begin = jnp.where(token >= first_count, first_count, 0)
        acc["peak"] = jnp.full((8, rows), masked_score, f32)
        acc["token"], acc["begin"] = token, begin

    def step_scores(block, start, size):
        s_ref[block % 2, start : start + size, :] = dot_nt(keys_ref[start : start + size, :], queries[block])
        for at in subs(start, size):
            score = s_ref[block % 2, at, :]
            if start >= cart_rows:
                key_at = lax.broadcasted_iota(jnp.int32, (sub, rows), 0) + (at.start - cart_rows)
                score = jnp.where((key_at >= acc["begin"]) & (key_at <= acc["token"]), score, masked_score)
                s_ref[block % 2, at, :] = score
            acc["peak"] = jnp.maximum(acc["peak"], fold_rows(score, jnp.max))

    def close_scores(block):
        peaks[block] = jnp.max(acc["peak"], axis=0, keepdims=True)

    def open_weights(block):
        grads[block] = rows_of("g", g_in, block)
        acc["total"] = jnp.zeros((8, rows), f32)
        acc["center"] = jnp.zeros((8, rows), f32)

    def step_weights(block, start, size):
        d_ref[block % 2, start : start + size, :] = dot_nt(vals_ref[start : start + size, :], grads[block])
        for at in subs(start, size):
            weight = jnp.exp2((s_ref[block % 2, at, :] - peaks[block]) * scale2)
            w_ref[block % 2, at, :] = weight
            acc["total"] = acc["total"] + fold_rows(weight, jnp.sum)
            acc["center"] = acc["center"] + fold_rows(weight * d_ref[block % 2, at, :], jnp.sum)

    def close_weights(block):
        share = 1.0 / jnp.sum(acc["total"], axis=0, keepdims=True)
        stats[block] = share, jnp.sum(acc["center"], axis=0, keepdims=True) * share

    def open_grads(block):
        acc["dq"] = jnp.zeros((head_dim, rows), f32)

    def step_grads(block, start, size):
        share, center = stats[block]
        for at in subs(start, size):
            prob = w_ref[block % 2, at, :] * share
            p_ref[at, :] = prob.astype(bf16)
            ds_ref[at, :] = (prob * (d_ref[block % 2, at, :] - center)).astype(bf16)
        at = slice(start, start + size)
        old = size if start < cart_rows else (limit(block - 1) if block else 0)
        old = old if block else 0
        for ref, left, right in ((dv_ref, p_ref, grads[block]), (dk_ref, ds_ref, queries[block])):
            part = dot_nn(left[at, :], right)
            if old:
                ref[start : start + old, :] += part[:old]
            if old < size:
                ref[start + old : start + size, :] = part[old:]
        acc["dq"] = acc["dq"] + dot_nn(keys_t_ref[:, at], ds_ref[at, :])

    def close_grads(block):
        out_ref[...] = (acc["dq"] * scale).T
        for head in range(width):
            dq_ref[block * block_tokens : (block + 1) * block_tokens, head * head_dim : (head + 1) * head_dim] = (
                out_ref[pl.ds(head, block_tokens, stride=width), :].astype(bf16)
            )

    pick("ck", ck_in, keys_ref, 0)
    pick("sk", sk_in, keys_ref, cart_rows)
    stages = (
        (2, open_grads, step_grads, close_grads),
        (1, open_weights, step_weights, close_weights),
        (0, open_scores, step_scores, close_scores),
    )
    for turn in range(blocks + 2):
        live = [(turn - lag, *calls) for lag, *calls in stages if 0 <= turn - lag < blocks]
        if turn == 1:
            pick("cv", cv_in, vals_ref, 0)
            pick("sv", sv_in, vals_ref, cart_rows)
            keys_t_ref[...] = keys_ref[...].astype(f32).T.astype(bf16)
        for block, begin_call, _, _ in live:
            begin_call(block)
        for index in range(len(pieces(0))):
            for block, _, step_call, _ in live:
                step_call(block, *pieces(block)[index])
        for block, _, _, end_call in live:
            end_call(block)

    part_rows = cart_rows // dp_size
    me = lax.axis_index("dp")
    for step, ref in enumerate(cart_outs):
        target = target_of(me, step, dp_size)
        at = pl.ds(pl.multiple_of(target * part_rows, part_rows), part_rows)
        ref[0] = (dk_ref[at, :] * scale).astype(ref.dtype)
        ref[1] = dv_ref[at, :].astype(ref.dtype)
    own = dk_ref[cart_rows:all_keys, :] * scale, dv_ref[cart_rows:all_keys, :]
    if not last:
        dq_outs[0][...] = dq_ref[...]
        self_ref[0], self_ref[1] = own
        return
    own_tokens = tokens // heads_size
    columns = width * head_dim
    me = lax.axis_index("heads")
    for step, ref in enumerate(dq_outs):
        target = target_of(me, step, heads_size)
        at = pl.ds(pl.multiple_of(target * own_tokens, own_tokens), own_tokens)
        for index, before in enumerate((*dq_before, dq_ref)):
            ref[:, index * columns : (index + 1) * columns] = before[at, :]
    count = tokens * kv_local
    for kind in range(2):
        for index, before in enumerate(self_before):
            wide_ref[pl.ds(index, tokens, stride=kv_local), :] = before[kind]
        wide_ref[pl.ds(kv_index, tokens, stride=kv_local), :] = own[kind]
        self_ref[kind * count : (kind + 1) * count, :] = wide_ref[0:count, :].astype(bf16)


def sum_kernel(*refs):
    part_refs, out_ref = refs[:-1], refs[-1]
    total = part_refs[0][...]
    for ref in part_refs[1:]:
        total = total + ref[...].astype(f32)
    out_ref[...] = total


def cart_kernel(kv_local, *refs):
    done_refs, part_refs, out_ref = refs[: kv_local - 1], refs[kv_local - 1 : -1], refs[-1]
    part_rows = part_refs[0].shape[1]
    for kind in range(2):
        total = part_refs[0][kind]
        for ref in part_refs[1:]:
            total = total + ref[kind].astype(f32)
        for kv_index, part in enumerate((*[ref[kind] for ref in done_refs], total)):
            out_ref[pl.ds(kind * kv_local + kv_index, part_rows, stride=2 * kv_local), :] = part


def place_kernel(count, *refs):
    part_refs, out_ref, sems = refs[:count], *refs[-2:]
    columns = part_refs[0].shape[1]
    me = lax.axis_index("heads")
    copies = []
    for step, ref in enumerate(part_refs):
        source = source_of(me, step, count)
        at = pl.ds(pl.multiple_of(source * columns, columns), columns)
        copies.append(pltpu.make_async_copy(ref, out_ref.at[:, at], sems.at[step]))
    for copy in copies:
        copy.start()
    for copy in copies:
        copy.wait()


def paired(size):
    return size & (size - 1) == 0


def target_of(me, step, size):
    return me ^ step if paired(size) else (me + step) % size


def source_of(me, step, size):
    return me ^ step if paired(size) else (me + size - step) % size


def shift(values, axis, size, step):
    if step == 0:
        return values
    return lax.ppermute(values, axis, [(source, target_of(source, step, size)) for source in range(size)])


def on_device(dp_size, heads_size, queries, out_grad, self_keys, self_values, cart_keys, cart_values, segment_ids):
    tokens, heads_local, head_dim = queries.shape
    kv_local = self_keys.shape[1]
    cart_rows = cart_keys.shape[0]
    width = heads_local // kv_local
    block_tokens = 64
    chunk = 256
    fine = 128
    sub = 16
    all_keys = cart_rows + tokens
    rows = block_tokens * width
    part_rows = cart_rows // dp_size
    own_tokens = tokens // heads_size
    flat = [array.reshape(-1, head_dim) for array in (queries, out_grad, self_keys, self_values, cart_keys, cart_values)]
    macs = tokens * width * all_keys * head_dim * 5
    blocks = tokens // block_tokens
    columns = width * head_dim
    count = tokens * kv_local
    cart_list, query_list, self_list = [], [], []
    anywhere = pl.BlockSpec(memory_space=pl.ANY)
    for kv_index in range(kv_local):
        last = kv_index == kv_local - 1
        if last:
            other_shapes = [jax.ShapeDtypeStruct((own_tokens, kv_local * columns), bf16) for _ in range(heads_size)]
            other_shapes.append(jax.ShapeDtypeStruct((2 * count, head_dim), bf16))
        else:
            other_shapes = [
                jax.ShapeDtypeStruct((tokens, columns), bf16),
                jax.ShapeDtypeStruct((2, tokens, head_dim), f32),
            ]
        before = query_list + self_list
        outs = pl.pallas_call(
            functools.partial(head_kernel, dp_size, heads_size, kv_index, kv_local, width, block_tokens, chunk, fine, sub),
            out_shape=(
                *[
                    jax.ShapeDtypeStruct((2, part_rows, head_dim), bf16 if step else f32)
                    for step in range(dp_size)
                ],
                *other_shapes,
            ),
            in_specs=[pl.BlockSpec(memory_space=pltpu.HBM)] * 6
            + [pl.BlockSpec(memory_space=pltpu.VMEM)] * (1 + (len(before) if last else 0)),
            scratch_shapes=[
                pltpu.VMEM((cart_rows * kv_local, head_dim), f32),
                pltpu.VMEM((all_keys, head_dim), bf16),
                pltpu.VMEM((all_keys, head_dim), bf16),
                pltpu.VMEM((head_dim, all_keys), bf16),
                pltpu.VMEM((2, all_keys, rows), f32),
                pltpu.VMEM((2, all_keys, rows), f32),
                pltpu.VMEM((2, all_keys, rows), f32),
                pltpu.VMEM((all_keys, rows), bf16),
                pltpu.VMEM((all_keys, rows), bf16),
                pltpu.VMEM((all_keys, head_dim), f32),
                pltpu.VMEM((all_keys, head_dim), f32),
                pltpu.VMEM((rows, head_dim), f32),
                pltpu.VMEM((tokens, columns), bf16),
                *[pltpu.VMEM(array.shape, bf16) for array in flat],
                pltpu.SemaphoreType.DMA((4 + 2 * blocks,)),
            ],
            compiler_params=pltpu.CompilerParams(vmem_limit_bytes=vmem_bytes),
            cost_estimate=pl.CostEstimate(flops=4 * macs, bytes_accessed=5 * 2**20, transcendentals=tokens * width * all_keys),
            name="head_grads",
        )(*flat, segment_ids, *(before if last else []))
        sends = list(outs[1:dp_size])
        if last:
            sends += outs[dp_size + 1 : -1]
        if last and cart_list:
            received = cart_parts[1:]
            sends, received = lax.optimization_barrier((sends, received))
        cart_parts = [outs[0]] + [shift(array, "dp", dp_size, step + 1) for step, array in enumerate(sends[: dp_size - 1])]
        if last:
            query_list, self_grads = [outs[dp_size], *sends[dp_size - 1 :]], outs[-1]
        else:
            query_list.append(outs[-2])
            self_list.append(outs[-1])
            cart_list.append(
                pl.pallas_call(
                    sum_kernel,
                    out_shape=jax.ShapeDtypeStruct((2, part_rows, head_dim), f32),
                    compiler_params=pltpu.CompilerParams(vmem_limit_bytes=small_vmem_bytes),
                    cost_estimate=pl.CostEstimate(flops=2**20, bytes_accessed=2**20, transcendentals=0),
                    name="cart_sum",
                )(*cart_parts)
            )
    query_list = [shift(part, "heads", heads_size, step) for step, part in enumerate(query_list)]
    query_grads = pl.pallas_call(
        functools.partial(place_kernel, heads_size),
        out_shape=jax.ShapeDtypeStruct((own_tokens, heads_size * heads_local * head_dim), bf16),
        in_specs=[anywhere] * heads_size,
        out_specs=anywhere,
        scratch_shapes=[pltpu.SemaphoreType.DMA((heads_size,))],
        compiler_params=pltpu.CompilerParams(vmem_limit_bytes=small_vmem_bytes),
        cost_estimate=pl.CostEstimate(flops=2**20, bytes_accessed=2 * 2**20, transcendentals=0),
        name="place_queries",
    )(*query_list)
    query_grads, cart_list, cart_parts = lax.optimization_barrier((query_grads, cart_list, cart_parts))
    cart_grads = pl.pallas_call(
        functools.partial(cart_kernel, kv_local),
        out_shape=jax.ShapeDtypeStruct((part_rows * 2 * kv_local, head_dim), f32),
        compiler_params=pltpu.CompilerParams(vmem_limit_bytes=small_vmem_bytes),
        cost_estimate=pl.CostEstimate(flops=2**20, bytes_accessed=2 * 2**20, transcendentals=0),
        name="cart_grads",
    )(*cart_list, *cart_parts)
    cart_grads = cart_grads.reshape(part_rows, 2, kv_local, head_dim)
    self_grads = self_grads.reshape(2, tokens, kv_local, head_dim)
    return (cart_grads, self_grads, query_grads)


def solution(mesh):
    in_specs = (
        P(("groups", "dp"), "heads", None),
        P(("groups", "dp"), "heads", None),
        P(("groups", "dp"), "heads", None),
        P(("groups", "dp"), "heads", None),
        P("groups", "heads", None),
        P("groups", "heads", None),
        P(("groups", "dp"), None),
    )
    out_specs = (
        P(("groups", "dp"), None, "heads", None),
        P(None, ("groups", "dp"), "heads", None),
        P(("groups", "dp", "heads"), None),
    )
    return jax.shard_map(
        functools.partial(on_device, mesh.shape["dp"], mesh.shape["heads"]),
        mesh=mesh, in_specs=in_specs, out_specs=out_specs, check_vma=False,
    )
```

```python
import functools
import math

import jax
import jax.numpy as jnp
from jax import lax
from jax.experimental import pallas as pl
from jax.experimental.pallas import tpu as pltpu
from jax.sharding import PartitionSpec as P

masked_score = -1e30
vmem_bytes = 56 * 1024 * 1024
small_vmem_bytes = 8 * 1024 * 1024
kept_steps = 2
f32 = jnp.float32
bf16 = jnp.bfloat16


def dot_nt(left, right):
    return lax.dot_general(left, right, (((1,), (1,)), ((), ())), preferred_element_type=f32)


def dot_nn(left, right):
    return lax.dot_general(left, right, (((1,), (0,)), ((), ())), preferred_element_type=f32)


def fold_rows(values, op):
    rows, columns = values.shape
    return op(values.reshape(rows // 8, 8, columns), axis=0)


def head_kernel(dp_size, heads_size, kv_index, kv_local, width, block_tokens, chunk, fine, sub, *refs):
    last = kv_index == kv_local - 1
    q_ref, g_ref, sk_ref, sv_ref, ck_ref, cv_ref, seg_ref = refs[:7]
    refs = refs[7:]
    held = kv_index if last else 0
    kept = min(kept_steps, heads_size)
    dq_before, refs = refs[: held * kept], refs[held * kept :]
    self_before, refs = refs[:held], refs[held:]
    cart_outs, refs = refs[:dp_size], refs[dp_size:]
    dq_outs, self_ref, refs = refs[:heads_size], refs[heads_size], refs[heads_size + 1 :]
    (
        wide_ref, keys_ref, vals_ref, keys_t_ref, s_ref, w_ref, d_ref, p_ref, ds_ref, dk_ref, dv_ref, out_ref, dq_ref,
        q_in, g_in, sk_in, sv_in, ck_in, cv_in, sems,
    ) = refs
    head_dim = q_ref.shape[1]
    tokens = seg_ref.shape[1]
    cart_rows = ck_ref.shape[0] // kv_local
    all_keys = cart_rows + tokens
    rows = block_tokens * width
    scale = head_dim ** -0.5
    scale2 = scale * math.log2(math.e)
    span = block_tokens * kv_local * width
    blocks = tokens // block_tokens

    def block_copy(source, target, block, sem):
        at = slice(block * span, (block + 1) * span)
        return pltpu.make_async_copy(source.at[at, :], target.at[at, :], sems.at[sem])

    copies = {
        name: pltpu.make_async_copy(source, target, sems.at[at])
        for at, (name, source, target) in enumerate(
            [("ck", ck_ref, ck_in), ("sk", sk_ref, sk_in), ("cv", cv_ref, cv_in), ("sv", sv_ref, sv_in)]
        )
    }
    for block in range(blocks):
        copies["q", block] = block_copy(q_ref, q_in, block, 4 + block)
        copies["g", block] = block_copy(g_ref, g_in, block, 4 + blocks + block)
    order = ["ck", "sk", ("q", 0), "cv", "sv", ("g", 0)]
    order += [(kind, block) for block in range(1, blocks) for kind in ("q", "g")]
    for name in order:
        copies[name].start()

    def pick(name, ref, dst, at):
        copies[name].wait()
        count = ref.shape[0] // kv_local
        if kv_local == 1:
            dst[at : at + count, :] = ref[...]
        else:
            wide_ref[0 : ref.shape[0], :] = ref[...].astype(f32)
            dst[at : at + count, :] = wide_ref[pl.ds(kv_index, count, stride=kv_local), :].astype(bf16)

    def rows_of(name, ref, block):
        copies[name, block].wait()
        wide = ref[block * span : (block + 1) * span, :]
        if kv_local == 1:
            return wide
        wide = wide.astype(f32).reshape(block_tokens, kv_local, width, head_dim)
        return wide[:, kv_index].reshape(rows, head_dim).astype(bf16)

    first_count = jnp.sum((seg_ref[...] == 0).astype(f32), axis=1, keepdims=True).astype(jnp.int32)

    def limit(block):
        return -(-(block + 1) * block_tokens // fine) * fine

    def pieces(block):
        cart = [(start, chunk) for start in range(0, cart_rows, chunk)]
        return cart + [(cart_rows, limit(block))]

    queries, grads, peaks, stats = {}, {}, {}, {}
    acc = {}

    def spread(values):
        return jnp.concatenate([values] * (sub // 8), axis=0)

    def subs(start, size):
        return [slice(at, at + sub) for at in range(start, start + size, sub)]

    def open_scores(block):
        queries[block] = rows_of("q", q_in, block)
        token = (lax.broadcasted_iota(jnp.int32, (1, rows), 1) + block * rows) // width
        begin = jnp.where(token >= first_count, first_count, 0)
        acc["peak"] = jnp.full((8, rows), masked_score, f32)
        acc["token"], acc["begin"] = token, begin

    def step_scores(block, start, size):
        s_ref[block % 2, start : start + size, :] = dot_nt(keys_ref[start : start + size, :], queries[block])
        for at in subs(start, size):
            score = s_ref[block % 2, at, :]
            if start >= cart_rows:
                key_at = lax.broadcasted_iota(jnp.int32, (sub, rows), 0) + (at.start - cart_rows)
                score = jnp.where((key_at >= acc["begin"]) & (key_at <= acc["token"]), score, masked_score)
                s_ref[block % 2, at, :] = score
            acc["peak"] = jnp.maximum(acc["peak"], fold_rows(score, jnp.max))

    def close_scores(block):
        peaks[block] = jnp.broadcast_to(jnp.max(acc["peak"], axis=0, keepdims=True), (8, rows))

    def open_weights(block):
        grads[block] = rows_of("g", g_in, block)
        acc["total"] = jnp.zeros((8, rows), f32)
        acc["center"] = jnp.zeros((8, rows), f32)

    def step_weights(block, start, size):
        d_ref[block % 2, start : start + size, :] = dot_nt(vals_ref[start : start + size, :], grads[block])
        for at in subs(start, size):
            weight = jnp.exp2((s_ref[block % 2, at, :] - spread(peaks[block])) * scale2)
            w_ref[block % 2, at, :] = weight
            acc["total"] = acc["total"] + fold_rows(weight, jnp.sum)
            acc["center"] = acc["center"] + fold_rows(weight * d_ref[block % 2, at, :], jnp.sum)

    def close_weights(block):
        share = 1.0 / jnp.sum(acc["total"], axis=0, keepdims=True)
        center = jnp.sum(acc["center"], axis=0, keepdims=True) * share
        stats[block] = jnp.broadcast_to(share, (8, rows)), jnp.broadcast_to(center, (8, rows))

    def open_grads(block):
        acc["dq"] = jnp.zeros((head_dim, rows), f32)

    def step_grads(block, start, size):
        share, center = stats[block]
        for at in subs(start, size):
            prob = w_ref[block % 2, at, :] * spread(share)
            p_ref[at, :] = prob.astype(bf16)
            ds_ref[at, :] = (prob * (d_ref[block % 2, at, :] - spread(center))).astype(bf16)
        at = slice(start, start + size)
        old = size if start < cart_rows else (limit(block - 1) if block else 0)
        old = old if block else 0
        for ref, left, right in ((dv_ref, p_ref, grads[block]), (dk_ref, ds_ref, queries[block])):
            part = dot_nn(left[at, :], right)
            if old:
                ref[start : start + old, :] += part[:old]
            if old < size:
                ref[start + old : start + size, :] = part[old:]
        acc["dq"] = acc["dq"] + dot_nn(keys_t_ref[:, at], ds_ref[at, :])

    def close_grads(block):
        out_ref[...] = (acc["dq"] * scale).T
        for head in range(width):
            dq_ref[block * block_tokens : (block + 1) * block_tokens, head * head_dim : (head + 1) * head_dim] = (
                out_ref[pl.ds(head, block_tokens, stride=width), :].astype(bf16)
            )

    pick("ck", ck_in, keys_ref, 0)
    pick("sk", sk_in, keys_ref, cart_rows)
    stages = (
        (2, open_grads, step_grads, close_grads),
        (1, open_weights, step_weights, close_weights),
        (0, open_scores, step_scores, close_scores),
    )
    for turn in range(blocks + 2):
        live = [(turn - lag, *calls) for lag, *calls in stages if 0 <= turn - lag < blocks]
        if turn == 1:
            pick("cv", cv_in, vals_ref, 0)
            pick("sv", sv_in, vals_ref, cart_rows)
            keys_t_ref[...] = keys_ref[...].astype(f32).T.astype(bf16)
        for block, begin_call, _, _ in live:
            begin_call(block)
        for index in range(len(pieces(0))):
            for block, _, step_call, _ in live:
                step_call(block, *pieces(block)[index])
        for block, _, _, end_call in live:
            end_call(block)

    part_rows = cart_rows // dp_size
    me = lax.axis_index("dp")
    for step, ref in enumerate(cart_outs):
        target = target_of(me, step, dp_size)
        at = pl.ds(pl.multiple_of(target * part_rows, part_rows), part_rows)
        ref[0] = (dk_ref[at, :] * scale).astype(ref.dtype)
        ref[1] = dv_ref[at, :].astype(ref.dtype)
    own = dk_ref[cart_rows:all_keys, :] * scale, dv_ref[cart_rows:all_keys, :]
    own_tokens = tokens // heads_size
    columns = width * head_dim
    me = lax.axis_index("heads")
    for step, ref in enumerate(dq_outs):
        target = target_of(me, step, heads_size)
        at = pl.ds(pl.multiple_of(target * own_tokens, own_tokens), own_tokens)
        if last and step < kept:
            for index in range(held):
                ref[:, index * columns : (index + 1) * columns] = dq_before[index * kept + step][...]
            ref[:, held * columns :] = dq_ref[at, :]
        else:
            ref[...] = dq_ref[at, :]
    if not last:
        self_ref[0], self_ref[1] = own
        return
    count = tokens * kv_local
    for kind in range(2):
        for index, before in enumerate(self_before):
            wide_ref[pl.ds(index, tokens, stride=kv_local), :] = before[kind]
        wide_ref[pl.ds(kv_index, tokens, stride=kv_local), :] = own[kind]
        self_ref[kind * count : (kind + 1) * count, :] = wide_ref[0:count, :].astype(bf16)


def sum_kernel(*refs):
    part_refs, out_ref = refs[:-1], refs[-1]
    total = part_refs[0][...]
    for ref in part_refs[1:]:
        total = total + ref[...].astype(f32)
    out_ref[...] = total


def cart_kernel(kv_local, *refs):
    done_refs, part_refs, out_ref = refs[: kv_local - 1], refs[kv_local - 1 : -1], refs[-1]
    part_rows = part_refs[0].shape[1]
    for kind in range(2):
        total = part_refs[0][kind]
        for ref in part_refs[1:]:
            total = total + ref[kind].astype(f32)
        for kv_index, part in enumerate((*[ref[kind] for ref in done_refs], total)):
            out_ref[pl.ds(kind * kv_local + kv_index, part_rows, stride=2 * kv_local), :] = part


def place_kernel(heads_size, kv_local, *refs):
    part_refs, out_ref, sems = refs[:-2], refs[-2], refs[-1]
    kept = min(kept_steps, heads_size)
    columns = out_ref.shape[1] // (heads_size * kv_local)
    me = lax.axis_index("heads")
    places = [(step, 0) for step in range(kept)]
    places += [(step, kv_index) for kv_index in range(kv_local) for step in range(kept, heads_size)]
    copies = []
    for index, ((step, kv_index), ref) in enumerate(zip(places, part_refs)):
        source = source_of(me, step, heads_size)
        at = pl.multiple_of((source * kv_local + kv_index) * columns, columns)
        copies.append(pltpu.make_async_copy(ref, out_ref.at[:, pl.ds(at, ref.shape[1])], sems.at[index]))
    for copy in copies:
        copy.start()
    for copy in copies:
        copy.wait()


def paired(size):
    return size & (size - 1) == 0


def target_of(me, step, size):
    return me ^ step if paired(size) else (me + step) % size


def source_of(me, step, size):
    return me ^ step if paired(size) else (me + size - step) % size


def shift(values, axis, size, step):
    if step == 0:
        return values
    return lax.ppermute(values, axis, [(source, target_of(source, step, size)) for source in range(size)])


def on_device(dp_size, heads_size, queries, out_grad, self_keys, self_values, cart_keys, cart_values, segment_ids):
    tokens, heads_local, head_dim = queries.shape
    kv_local = self_keys.shape[1]
    cart_rows = cart_keys.shape[0]
    width = heads_local // kv_local
    block_tokens = 64
    chunk = 256
    fine = 128
    sub = 16
    all_keys = cart_rows + tokens
    rows = block_tokens * width
    part_rows = cart_rows // dp_size
    own_tokens = tokens // heads_size
    flat = [array.reshape(-1, head_dim) for array in (queries, out_grad, self_keys, self_values, cart_keys, cart_values)]
    macs = tokens * width * all_keys * head_dim * 5
    blocks = tokens // block_tokens
    columns = width * head_dim
    count = tokens * kv_local
    kept = min(kept_steps, heads_size)
    anywhere = pl.BlockSpec(memory_space=pl.ANY)
    cart_list, kept_list, far_list, self_list, received = [], [], [], [], []
    for kv_index in range(kv_local):
        last = kv_index == kv_local - 1
        near = jax.ShapeDtypeStruct((own_tokens, kv_local * columns if last else columns), bf16)
        far = jax.ShapeDtypeStruct((own_tokens, columns), bf16)
        own_shape = (2 * count, head_dim) if last else (2, tokens, head_dim)
        other_shapes = [near] * kept + [far] * (heads_size - kept)
        other_shapes.append(jax.ShapeDtypeStruct(own_shape, bf16 if last else f32))
        before = kept_list + self_list
        outs = pl.pallas_call(
            functools.partial(head_kernel, dp_size, heads_size, kv_index, kv_local, width, block_tokens, chunk, fine, sub),
            out_shape=(
                *[
                    jax.ShapeDtypeStruct((2, part_rows, head_dim), bf16 if step else f32)
                    for step in range(dp_size)
                ],
                *other_shapes,
            ),
            in_specs=[pl.BlockSpec(memory_space=pltpu.HBM)] * 6
            + [pl.BlockSpec(memory_space=pltpu.VMEM)] * (1 + (len(before) if last else 0)),
            scratch_shapes=[
                pltpu.VMEM((cart_rows * kv_local, head_dim), f32),
                pltpu.VMEM((all_keys, head_dim), bf16),
                pltpu.VMEM((all_keys, head_dim), bf16),
                pltpu.VMEM((head_dim, all_keys), bf16),
                pltpu.VMEM((2, all_keys, rows), f32),
                pltpu.VMEM((2, all_keys, rows), f32),
                pltpu.VMEM((2, all_keys, rows), f32),
                pltpu.VMEM((all_keys, rows), bf16),
                pltpu.VMEM((all_keys, rows), bf16),
                pltpu.VMEM((all_keys, head_dim), f32),
                pltpu.VMEM((all_keys, head_dim), f32),
                pltpu.VMEM((rows, head_dim), f32),
                pltpu.VMEM((tokens, columns), bf16),
                *[pltpu.VMEM(array.shape, bf16) for array in flat],
                pltpu.SemaphoreType.DMA((4 + 2 * blocks,)),
            ],
            compiler_params=pltpu.CompilerParams(vmem_limit_bytes=vmem_bytes),
            cost_estimate=pl.CostEstimate(flops=4 * macs, bytes_accessed=5 * 2**20, transcendentals=tokens * width * all_keys),
            name="head_grads",
        )(*flat, segment_ids, *(before if last else []))
        cart_sends, near, far = outs[1:dp_size], outs[dp_size : dp_size + kept], outs[dp_size + kept : -1]
        if last:
            cart_sends, near, far, received = lax.optimization_barrier((cart_sends, near, far, received))
        else:
            kept_list += near
            self_list.append(outs[-1])
        cart_parts = [outs[0], *[shift(part, "dp", dp_size, step + 1) for step, part in enumerate(cart_sends)]]
        far_parts = [shift(part, "heads", heads_size, kept + step) for step, part in enumerate(far)]
        if not last:
            received.append((cart_parts, far_parts))
    for early_cart, early_far in received:
        cart_list.append(
            pl.pallas_call(
                sum_kernel,
                out_shape=jax.ShapeDtypeStruct((2, part_rows, head_dim), f32),
                compiler_params=pltpu.CompilerParams(vmem_limit_bytes=small_vmem_bytes),
                cost_estimate=pl.CostEstimate(flops=2**20, bytes_accessed=2**20, transcendentals=0),
                name="cart_sum",
            )(*early_cart)
        )
        far_list += early_far
    query_list = [shift(part, "heads", heads_size, step) for step, part in enumerate(near)] + far_list + far_parts
    query_grads = pl.pallas_call(
        functools.partial(place_kernel, heads_size, kv_local),
        out_shape=jax.ShapeDtypeStruct((own_tokens, heads_size * heads_local * head_dim), bf16),
        in_specs=[anywhere] * len(query_list),
        out_specs=anywhere,
        scratch_shapes=[pltpu.SemaphoreType.DMA((len(query_list),))],
        compiler_params=pltpu.CompilerParams(vmem_limit_bytes=small_vmem_bytes),
        cost_estimate=pl.CostEstimate(flops=2**20, bytes_accessed=2 * 2**20, transcendentals=0),
        name="place_queries",
    )(*query_list)
    cart_grads = pl.pallas_call(
        functools.partial(cart_kernel, kv_local),
        out_shape=jax.ShapeDtypeStruct((part_rows * 2 * kv_local, head_dim), f32),
        compiler_params=pltpu.CompilerParams(vmem_limit_bytes=small_vmem_bytes),
        cost_estimate=pl.CostEstimate(flops=2**20, bytes_accessed=2 * 2**20, transcendentals=0),
        name="cart_grads",
    )(*cart_list, *cart_parts)
    cart_grads = cart_grads.reshape(part_rows, 2, kv_local, head_dim)
    self_grads = outs[-1].reshape(2, tokens, kv_local, head_dim)
    return (cart_grads, self_grads, query_grads)


def solution(mesh):
    in_specs = (
        P(("groups", "dp"), "heads", None),
        P(("groups", "dp"), "heads", None),
        P(("groups", "dp"), "heads", None),
        P(("groups", "dp"), "heads", None),
        P("groups", "heads", None),
        P("groups", "heads", None),
        P(("groups", "dp"), None),
    )
    out_specs = (
        P(("groups", "dp"), None, "heads", None),
        P(None, ("groups", "dp"), "heads", None),
        P(("groups", "dp", "heads"), None),
    )
    return jax.shard_map(
        functools.partial(on_device, mesh.shape["dp"], mesh.shape["heads"]),
        mesh=mesh, in_specs=in_specs, out_specs=out_specs, check_vma=False,
    )
```

```python
import functools
import math

import jax
import jax.numpy as jnp
from jax import lax
from jax.experimental import pallas as pl
from jax.experimental.pallas import tpu as pltpu
from jax.sharding import PartitionSpec as P

masked_score = -1e30
vmem_bytes = 56 * 1024 * 1024
small_vmem_bytes = 8 * 1024 * 1024
early_steps = (2,)
f32 = jnp.float32
bf16 = jnp.bfloat16


def dot_nt(left, right):
    return lax.dot_general(left, right, (((1,), (1,)), ((), ())), preferred_element_type=f32)


def dot_nn(left, right):
    return lax.dot_general(left, right, (((1,), (0,)), ((), ())), preferred_element_type=f32)


def fold_rows(values, op):
    rows, columns = values.shape
    return op(values.reshape(rows // 8, 8, columns), axis=0)


def head_kernel(dp_size, heads_size, kv_index, kv_local, width, block_tokens, chunk, fine, sub, *refs):
    last = kv_index == kv_local - 1
    q_ref, g_ref, sk_ref, sv_ref, ck_ref, cv_ref, seg_ref = refs[:7]
    refs = refs[7:]
    held = kv_index if last else 0
    near_steps, far_steps = split_steps(heads_size)
    kept = len(near_steps)
    dq_before, refs = refs[: held * kept], refs[held * kept :]
    self_before, refs = refs[:held], refs[held:]
    cart_outs, refs = refs[:dp_size], refs[dp_size:]
    dq_outs, self_ref, refs = refs[:heads_size], refs[heads_size], refs[heads_size + 1 :]
    (
        wide_ref, keys_ref, vals_ref, keys_t_ref, s_ref, w_ref, d_ref, p_ref, ds_ref, dk_ref, dv_ref, out_ref, dq_ref,
        q_in, g_in, sk_in, sv_in, ck_in, cv_in, sems,
    ) = refs
    head_dim = q_ref.shape[1]
    tokens = seg_ref.shape[1]
    cart_rows = ck_ref.shape[0] // kv_local
    all_keys = cart_rows + tokens
    rows = block_tokens * width
    scale = head_dim ** -0.5
    scale2 = scale * math.log2(math.e)
    span = block_tokens * kv_local * width
    blocks = tokens // block_tokens

    def block_copy(source, target, block, sem):
        at = slice(block * span, (block + 1) * span)
        return pltpu.make_async_copy(source.at[at, :], target.at[at, :], sems.at[sem])

    copies = {
        name: pltpu.make_async_copy(source, target, sems.at[at])
        for at, (name, source, target) in enumerate(
            [("ck", ck_ref, ck_in), ("sk", sk_ref, sk_in), ("cv", cv_ref, cv_in), ("sv", sv_ref, sv_in)]
        )
    }
    for block in range(blocks):
        copies["q", block] = block_copy(q_ref, q_in, block, 4 + block)
        copies["g", block] = block_copy(g_ref, g_in, block, 4 + blocks + block)
    order = ["ck", "sk", ("q", 0), "cv", "sv", ("g", 0)]
    order += [(kind, block) for block in range(1, blocks) for kind in ("q", "g")]
    for name in order:
        copies[name].start()

    def pick(name, ref, dst, at):
        copies[name].wait()
        count = ref.shape[0] // kv_local
        if kv_local == 1:
            dst[at : at + count, :] = ref[...]
        else:
            wide_ref[0 : ref.shape[0], :] = ref[...].astype(f32)
            dst[at : at + count, :] = wide_ref[pl.ds(kv_index, count, stride=kv_local), :].astype(bf16)

    def rows_of(name, ref, block):
        copies[name, block].wait()
        wide = ref[block * span : (block + 1) * span, :]
        if kv_local == 1:
            return wide
        wide = wide.astype(f32).reshape(block_tokens, kv_local, width, head_dim)
        return wide[:, kv_index].reshape(rows, head_dim).astype(bf16)

    first_count = jnp.sum((seg_ref[...] == 0).astype(f32), axis=1, keepdims=True).astype(jnp.int32)

    def limit(block):
        return -(-(block + 1) * block_tokens // fine) * fine

    def pieces(block):
        cart = [(start, chunk) for start in range(0, cart_rows, chunk)]
        return cart + [(cart_rows, limit(block))]

    queries, grads, peaks, stats = {}, {}, {}, {}
    acc = {}

    def spread(values):
        return jnp.concatenate([values] * (sub // 8), axis=0)

    def subs(start, size):
        return [slice(at, at + sub) for at in range(start, start + size, sub)]

    def open_scores(block):
        queries[block] = rows_of("q", q_in, block)
        token = (lax.broadcasted_iota(jnp.int32, (1, rows), 1) + block * rows) // width
        begin = jnp.where(token >= first_count, first_count, 0)
        acc["peak"] = jnp.full((8, rows), masked_score, f32)
        acc["token"], acc["begin"] = token, begin

    def step_scores(block, start, size):
        s_ref[block % 2, start : start + size, :] = dot_nt(keys_ref[start : start + size, :], queries[block])
        for at in subs(start, size):
            score = s_ref[block % 2, at, :]
            if start >= cart_rows:
                key_at = lax.broadcasted_iota(jnp.int32, (sub, rows), 0) + (at.start - cart_rows)
                score = jnp.where((key_at >= acc["begin"]) & (key_at <= acc["token"]), score, masked_score)
                s_ref[block % 2, at, :] = score
            acc["peak"] = jnp.maximum(acc["peak"], fold_rows(score, jnp.max))

    def close_scores(block):
        peaks[block] = jnp.broadcast_to(jnp.max(acc["peak"], axis=0, keepdims=True), (8, rows))

    def open_weights(block):
        grads[block] = rows_of("g", g_in, block)
        acc["total"] = jnp.zeros((8, rows), f32)
        acc["center"] = jnp.zeros((8, rows), f32)

    def step_weights(block, start, size):
        d_ref[block % 2, start : start + size, :] = dot_nt(vals_ref[start : start + size, :], grads[block])
        for at in subs(start, size):
            weight = jnp.exp2((s_ref[block % 2, at, :] - spread(peaks[block])) * scale2)
            w_ref[block % 2, at, :] = weight
            acc["total"] = acc["total"] + fold_rows(weight, jnp.sum)
            acc["center"] = acc["center"] + fold_rows(weight * d_ref[block % 2, at, :], jnp.sum)

    def close_weights(block):
        share = 1.0 / jnp.sum(acc["total"], axis=0, keepdims=True)
        center = jnp.sum(acc["center"], axis=0, keepdims=True) * share
        stats[block] = jnp.broadcast_to(share, (8, rows)), jnp.broadcast_to(center, (8, rows))

    def open_grads(block):
        acc["dq"] = jnp.zeros((head_dim, rows), f32)

    def step_grads(block, start, size):
        share, center = stats[block]
        for at in subs(start, size):
            prob = w_ref[block % 2, at, :] * spread(share)
            p_ref[at, :] = prob.astype(bf16)
            ds_ref[at, :] = (prob * (d_ref[block % 2, at, :] - spread(center))).astype(bf16)
        at = slice(start, start + size)
        old = size if start < cart_rows else (limit(block - 1) if block else 0)
        old = old if block else 0
        for ref, left, right in ((dv_ref, p_ref, grads[block]), (dk_ref, ds_ref, queries[block])):
            part = dot_nn(left[at, :], right)
            if old:
                ref[start : start + old, :] += part[:old]
            if old < size:
                ref[start + old : start + size, :] = part[old:]
        acc["dq"] = acc["dq"] + dot_nn(keys_t_ref[:, at], ds_ref[at, :])

    def close_grads(block):
        out_ref[...] = (acc["dq"] * scale).T
        for head in range(width):
            dq_ref[block * block_tokens : (block + 1) * block_tokens, head * head_dim : (head + 1) * head_dim] = (
                out_ref[pl.ds(head, block_tokens, stride=width), :].astype(bf16)
            )

    pick("ck", ck_in, keys_ref, 0)
    pick("sk", sk_in, keys_ref, cart_rows)
    stages = (
        (2, open_grads, step_grads, close_grads),
        (1, open_weights, step_weights, close_weights),
        (0, open_scores, step_scores, close_scores),
    )
    for turn in range(blocks + 2):
        live = [(turn - lag, *calls) for lag, *calls in stages if 0 <= turn - lag < blocks]
        if turn == 1:
            pick("cv", cv_in, vals_ref, 0)
            pick("sv", sv_in, vals_ref, cart_rows)
            keys_t_ref[...] = keys_ref[...].astype(f32).T.astype(bf16)
        for block, begin_call, _, _ in live:
            begin_call(block)
        for index in range(len(pieces(0))):
            for block, _, step_call, _ in live:
                step_call(block, *pieces(block)[index])
        for block, _, _, end_call in live:
            end_call(block)

    part_rows = cart_rows // dp_size
    me = lax.axis_index("dp")
    for step, ref in enumerate(cart_outs):
        target = target_of(me, step, "dp", dp_size)
        at = pl.ds(pl.multiple_of(target * part_rows, part_rows), part_rows)
        ref[0] = (dk_ref[at, :] * scale).astype(ref.dtype)
        ref[1] = dv_ref[at, :].astype(ref.dtype)
    own = dk_ref[cart_rows:all_keys, :] * scale, dv_ref[cart_rows:all_keys, :]
    own_tokens = tokens // heads_size
    columns = width * head_dim
    me = lax.axis_index("heads")
    for place, (step, ref) in enumerate(zip(near_steps + far_steps, dq_outs)):
        target = target_of(me, step, "heads", heads_size)
        at = pl.ds(pl.multiple_of(target * own_tokens, own_tokens), own_tokens)
        if last and place < kept:
            for index in range(held):
                ref[:, index * columns : (index + 1) * columns] = dq_before[index * kept + place][...]
            ref[:, held * columns :] = dq_ref[at, :]
        else:
            ref[...] = dq_ref[at, :]
    if not last:
        self_ref[0], self_ref[1] = own
        return
    count = tokens * kv_local
    for kind in range(2):
        for index, before in enumerate(self_before):
            wide_ref[pl.ds(index, tokens, stride=kv_local), :] = before[kind]
        wide_ref[pl.ds(kv_index, tokens, stride=kv_local), :] = own[kind]
        self_ref[kind * count : (kind + 1) * count, :] = wide_ref[0:count, :].astype(bf16)


def sum_kernel(*refs):
    part_refs, out_ref = refs[:-1], refs[-1]
    total = part_refs[0][...]
    for ref in part_refs[1:]:
        total = total + ref[...].astype(f32)
    out_ref[...] = total


def cart_kernel(kv_local, *refs):
    done_refs, part_refs, out_ref = refs[: kv_local - 1], refs[kv_local - 1 : -1], refs[-1]
    part_rows = part_refs[0].shape[1]
    for kind in range(2):
        total = part_refs[0][kind]
        for ref in part_refs[1:]:
            total = total + ref[kind].astype(f32)
        for kv_index, part in enumerate((*[ref[kind] for ref in done_refs], total)):
            out_ref[pl.ds(kind * kv_local + kv_index, part_rows, stride=2 * kv_local), :] = part


def place_kernel(heads_size, kv_local, *refs):
    part_refs, out_ref, sems = refs[:-2], refs[-2], refs[-1]
    near_steps, far_steps = split_steps(heads_size)
    columns = out_ref.shape[1] // (heads_size * kv_local)
    me = lax.axis_index("heads")
    places = [(step, 0) for step in near_steps]
    places += [(step, kv_index) for kv_index in range(kv_local) for step in far_steps]
    copies = []
    for index, ((step, kv_index), ref) in enumerate(zip(places, part_refs)):
        source = source_of(me, step, "heads", heads_size)
        at = pl.multiple_of((source * kv_local + kv_index) * columns, columns)
        copies.append(pltpu.make_async_copy(ref, out_ref.at[:, pl.ds(at, ref.shape[1])], sems.at[index]))
    for copy in copies:
        copy.start()
    for copy in copies:
        copy.wait()


def paired(axis, size):
    return axis == "heads" and size & (size - 1) == 0


def target_of(me, step, axis, size):
    return me ^ step if paired(axis, size) else (me + step) % size


def source_of(me, step, axis, size):
    return me ^ step if paired(axis, size) else (me + size - step) % size


def shift(values, axis, size, step):
    if step == 0:
        return values
    return lax.ppermute(values, axis, [(source, target_of(source, step, axis, size)) for source in range(size)])


def split_steps(heads_size):
    early = [step for step in range(heads_size) if step in early_steps]
    return [step for step in range(heads_size) if step not in early], early


def on_device(dp_size, heads_size, queries, out_grad, self_keys, self_values, cart_keys, cart_values, segment_ids):
    tokens, heads_local, head_dim = queries.shape
    kv_local = self_keys.shape[1]
    cart_rows = cart_keys.shape[0]
    width = heads_local // kv_local
    block_tokens = 64
    chunk = 256
    fine = 128
    sub = 16
    all_keys = cart_rows + tokens
    rows = block_tokens * width
    part_rows = cart_rows // dp_size
    own_tokens = tokens // heads_size
    flat = [array.reshape(-1, head_dim) for array in (queries, out_grad, self_keys, self_values, cart_keys, cart_values)]
    macs = tokens * width * all_keys * head_dim * 5
    blocks = tokens // block_tokens
    columns = width * head_dim
    count = tokens * kv_local
    near_steps, far_steps = split_steps(heads_size)
    kept = len(near_steps)
    anywhere = pl.BlockSpec(memory_space=pl.ANY)
    cart_list, kept_list, far_list, self_list, received = [], [], [], [], []
    for kv_index in range(kv_local):
        last = kv_index == kv_local - 1
        near = jax.ShapeDtypeStruct((own_tokens, kv_local * columns if last else columns), bf16)
        far = jax.ShapeDtypeStruct((own_tokens, columns), bf16)
        own_shape = (2 * count, head_dim) if last else (2, tokens, head_dim)
        other_shapes = [near] * kept + [far] * (heads_size - kept)
        other_shapes.append(jax.ShapeDtypeStruct(own_shape, bf16 if last else f32))
        before = kept_list + self_list
        outs = pl.pallas_call(
            functools.partial(head_kernel, dp_size, heads_size, kv_index, kv_local, width, block_tokens, chunk, fine, sub),
            out_shape=(
                *[
                    jax.ShapeDtypeStruct((2, part_rows, head_dim), bf16 if step else f32)
                    for step in range(dp_size)
                ],
                *other_shapes,
            ),
            in_specs=[pl.BlockSpec(memory_space=pltpu.HBM)] * 6
            + [pl.BlockSpec(memory_space=pltpu.VMEM)] * (1 + (len(before) if last else 0)),
            scratch_shapes=[
                pltpu.VMEM((cart_rows * kv_local, head_dim), f32),
                pltpu.VMEM((all_keys, head_dim), bf16),
                pltpu.VMEM((all_keys, head_dim), bf16),
                pltpu.VMEM((head_dim, all_keys), bf16),
                pltpu.VMEM((2, all_keys, rows), f32),
                pltpu.VMEM((2, all_keys, rows), f32),
                pltpu.VMEM((2, all_keys, rows), f32),
                pltpu.VMEM((all_keys, rows), bf16),
                pltpu.VMEM((all_keys, rows), bf16),
                pltpu.VMEM((all_keys, head_dim), f32),
                pltpu.VMEM((all_keys, head_dim), f32),
                pltpu.VMEM((rows, head_dim), f32),
                pltpu.VMEM((tokens, columns), bf16),
                *[pltpu.VMEM(array.shape, bf16) for array in flat],
                pltpu.SemaphoreType.DMA((4 + 2 * blocks,)),
            ],
            compiler_params=pltpu.CompilerParams(vmem_limit_bytes=vmem_bytes),
            cost_estimate=pl.CostEstimate(flops=4 * macs, bytes_accessed=5 * 2**20, transcendentals=tokens * width * all_keys),
            name="head_grads",
        )(*flat, segment_ids, *(before if last else []))
        cart_sends, near, far = outs[1:dp_size], outs[dp_size : dp_size + kept], outs[dp_size + kept : -1]
        if last:
            cart_sends, near, far, received = lax.optimization_barrier((cart_sends, near, far, received))
        else:
            kept_list += near
            self_list.append(outs[-1])
        cart_parts = [outs[0], *[shift(part, "dp", dp_size, step + 1) for step, part in enumerate(cart_sends)]]
        far_parts = [shift(part, "heads", heads_size, step) for step, part in zip(far_steps, far)]
        if not last:
            received.append((cart_parts, far_parts))
    for early_cart, early_far in received:
        cart_list.append(
            pl.pallas_call(
                sum_kernel,
                out_shape=jax.ShapeDtypeStruct((2, part_rows, head_dim), f32),
                compiler_params=pltpu.CompilerParams(vmem_limit_bytes=small_vmem_bytes),
                cost_estimate=pl.CostEstimate(flops=2**20, bytes_accessed=2**20, transcendentals=0),
                name="cart_sum",
            )(*early_cart)
        )
        far_list += early_far
    query_list = [shift(part, "heads", heads_size, step) for step, part in zip(near_steps, near)] + far_list + far_parts
    query_grads = pl.pallas_call(
        functools.partial(place_kernel, heads_size, kv_local),
        out_shape=jax.ShapeDtypeStruct((own_tokens, heads_size * heads_local * head_dim), bf16),
        in_specs=[anywhere] * len(query_list),
        out_specs=anywhere,
        scratch_shapes=[pltpu.SemaphoreType.DMA((len(query_list),))],
        compiler_params=pltpu.CompilerParams(vmem_limit_bytes=small_vmem_bytes),
        cost_estimate=pl.CostEstimate(flops=2**20, bytes_accessed=2 * 2**20, transcendentals=0),
        name="place_queries",
    )(*query_list)
    cart_grads = pl.pallas_call(
        functools.partial(cart_kernel, kv_local),
        out_shape=jax.ShapeDtypeStruct((part_rows * 2 * kv_local, head_dim), f32),
        compiler_params=pltpu.CompilerParams(vmem_limit_bytes=small_vmem_bytes),
        cost_estimate=pl.CostEstimate(flops=2**20, bytes_accessed=2 * 2**20, transcendentals=0),
        name="cart_grads",
    )(*cart_list, *cart_parts)
    cart_grads = cart_grads.reshape(part_rows, 2, kv_local, head_dim)
    self_grads = outs[-1].reshape(2, tokens, kv_local, head_dim)
    return (cart_grads, self_grads, query_grads)


def solution(mesh):
    in_specs = (
        P(("groups", "dp"), "heads", None),
        P(("groups", "dp"), "heads", None),
        P(("groups", "dp"), "heads", None),
        P(("groups", "dp"), "heads", None),
        P("groups", "heads", None),
        P("groups", "heads", None),
        P(("groups", "dp"), None),
    )
    out_specs = (
        P(("groups", "dp"), None, "heads", None),
        P(None, ("groups", "dp"), "heads", None),
        P(("groups", "dp", "heads"), None),
    )
    return jax.shard_map(
        functools.partial(on_device, mesh.shape["dp"], mesh.shape["heads"]),
        mesh=mesh, in_specs=in_specs, out_specs=out_specs, check_vma=False,
    )
```

```python
import functools
import math

import jax
import jax.numpy as jnp
from jax import lax
from jax.experimental import pallas as pl
from jax.experimental.pallas import tpu as pltpu
from jax.sharding import PartitionSpec as P

masked_score = -1e30
vmem_bytes = 56 * 1024 * 1024
small_vmem_bytes = 8 * 1024 * 1024
early_steps = (2,)
f32 = jnp.float32
bf16 = jnp.bfloat16


def dot_nt(left, right):
    return lax.dot_general(left, right, (((1,), (1,)), ((), ())), preferred_element_type=f32)


def dot_nn(left, right):
    return lax.dot_general(left, right, (((1,), (0,)), ((), ())), preferred_element_type=f32)


def fold_rows(values, op):
    rows, columns = values.shape
    return op(values.reshape(rows // 8, 8, columns), axis=0)


def head_kernel(dp_size, heads_size, kv_index, kv_local, width, block_tokens, chunk, fine, sub, *refs):
    last = kv_index == kv_local - 1
    q_ref, g_ref, sk_ref, sv_ref, ck_ref, cv_ref, seg_ref = refs[:7]
    refs = refs[7:]
    held = kv_index if last else 0
    near_steps, far_steps = split_steps(heads_size)
    kept = len(near_steps)
    dq_before, refs = refs[: held * kept], refs[held * kept :]
    self_before, refs = refs[:held], refs[held:]
    cart_outs, refs = refs[:dp_size], refs[dp_size:]
    dq_outs, self_ref, refs = refs[:heads_size], refs[heads_size], refs[heads_size + 1 :]
    (
        wide_ref, keys_ref, vals_ref, keys_t_ref, s_ref, w_ref, d_ref, p_ref, ds_ref, dk_ref, dv_ref, out_ref, dq_ref,
        q_in, g_in, sk_in, sv_in, ck_in, cv_in, sems,
    ) = refs
    head_dim = q_ref.shape[1]
    tokens = seg_ref.shape[1]
    cart_rows = ck_ref.shape[0] // kv_local
    all_keys = cart_rows + tokens
    rows = block_tokens * width
    scale = head_dim ** -0.5
    scale2 = scale * math.log2(math.e)
    span = block_tokens * kv_local * width
    blocks = tokens // block_tokens

    def block_copy(source, target, block, sem):
        at = slice(block * span, (block + 1) * span)
        return pltpu.make_async_copy(source.at[at, :], target.at[at, :], sems.at[sem])

    copies = {
        name: pltpu.make_async_copy(source, target, sems.at[at])
        for at, (name, source, target) in enumerate(
            [("ck", ck_ref, ck_in), ("sk", sk_ref, sk_in), ("cv", cv_ref, cv_in), ("sv", sv_ref, sv_in)]
        )
    }
    for block in range(blocks):
        copies["q", block] = block_copy(q_ref, q_in, block, 4 + block)
        copies["g", block] = block_copy(g_ref, g_in, block, 4 + blocks + block)
    order = ["ck", "sk", ("q", 0), "cv", "sv", ("g", 0)]
    order += [(kind, block) for block in range(1, blocks) for kind in ("q", "g")]
    for name in order:
        copies[name].start()

    def pick(name, ref, dst, at):
        copies[name].wait()
        count = ref.shape[0] // kv_local
        if kv_local == 1:
            dst[at : at + count, :] = ref[...]
        else:
            wide_ref[0 : ref.shape[0], :] = ref[...].astype(f32)
            dst[at : at + count, :] = wide_ref[pl.ds(kv_index, count, stride=kv_local), :].astype(bf16)

    def rows_of(name, ref, block):
        copies[name, block].wait()
        wide = ref[block * span : (block + 1) * span, :]
        if kv_local == 1:
            return wide
        wide = wide.astype(f32).reshape(block_tokens, kv_local, width, head_dim)
        return wide[:, kv_index].reshape(rows, head_dim).astype(bf16)

    first_count = jnp.sum((seg_ref[...] == 0).astype(f32), axis=1, keepdims=True).astype(jnp.int32)

    def limit(block):
        return -(-(block + 1) * block_tokens // fine) * fine

    def pieces(block):
        cart = [(start, chunk) for start in range(0, cart_rows, chunk)]
        return cart + [(cart_rows, limit(block))]

    queries, grads, peaks, stats = {}, {}, {}, {}
    acc = {}

    def spread(values):
        return jnp.concatenate([values] * (sub // 8), axis=0)

    def subs(start, size):
        return [slice(at, at + sub) for at in range(start, start + size, sub)]

    def open_scores(block):
        queries[block] = rows_of("q", q_in, block)
        token = (lax.broadcasted_iota(jnp.int32, (1, rows), 1) + block * rows) // width
        begin = jnp.where(token >= first_count, first_count, 0)
        acc["peak"] = jnp.full((8, rows), masked_score, f32)
        acc["token"], acc["begin"] = token, begin

    def step_scores(block, start, size):
        s_ref[block % 2, start : start + size, :] = dot_nt(keys_ref[start : start + size, :], queries[block])
        for at in subs(start, size):
            score = s_ref[block % 2, at, :]
            if start >= cart_rows:
                key_at = lax.broadcasted_iota(jnp.int32, (sub, rows), 0) + (at.start - cart_rows)
                score = jnp.where((key_at >= acc["begin"]) & (key_at <= acc["token"]), score, masked_score)
                s_ref[block % 2, at, :] = score
            acc["peak"] = jnp.maximum(acc["peak"], fold_rows(score, jnp.max))

    def close_scores(block):
        peaks[block] = jnp.broadcast_to(jnp.max(acc["peak"], axis=0, keepdims=True), (8, rows))

    def open_weights(block):
        grads[block] = rows_of("g", g_in, block)
        acc["total"] = jnp.zeros((8, rows), f32)
        acc["center"] = jnp.zeros((8, rows), f32)

    def step_weights(block, start, size):
        d_ref[block % 2, start : start + size, :] = dot_nt(vals_ref[start : start + size, :], grads[block])
        for at in subs(start, size):
            weight = jnp.exp2((s_ref[block % 2, at, :] - spread(peaks[block])) * scale2)
            w_ref[block % 2, at, :] = weight
            acc["total"] = acc["total"] + fold_rows(weight, jnp.sum)
            acc["center"] = acc["center"] + fold_rows(weight * d_ref[block % 2, at, :], jnp.sum)

    def close_weights(block):
        share = 1.0 / jnp.sum(acc["total"], axis=0, keepdims=True)
        center = jnp.sum(acc["center"], axis=0, keepdims=True) * share
        stats[block] = jnp.broadcast_to(share, (8, rows)), jnp.broadcast_to(center, (8, rows))

    def open_grads(block):
        pass

    def step_grads(block, start, size):
        slot = block % 2
        share, center = stats[block]
        for at in subs(start, size):
            prob = w_ref[slot, at, :] * spread(share)
            p_ref[slot, at, :] = prob.astype(bf16)
            ds_ref[slot, at, :] = (prob * (d_ref[slot, at, :] - spread(center))).astype(bf16)
        at = slice(start, start + size)
        old = size if start < cart_rows else (limit(block - 1) if block else 0)
        old = old if block else 0
        for ref, left, right in ((dv_ref, p_ref, grads[block]), (dk_ref, ds_ref, queries[block])):
            part = dot_nn(left[slot, at, :], right)
            if old:
                ref[start : start + old, :] += part[:old]
            if old < size:
                ref[start + old : start + size, :] = part[old:]

    def close_grads(block):
        seen = cart_rows + limit(block)
        dq_t = dot_nn(keys_t_ref[:, 0:seen], ds_ref[block % 2, 0:seen, :])
        out_ref[...] = (dq_t * scale).T
        for head in range(width):
            dq_ref[block * block_tokens : (block + 1) * block_tokens, head * head_dim : (head + 1) * head_dim] = (
                out_ref[pl.ds(head, block_tokens, stride=width), :].astype(bf16)
            )

    pick("ck", ck_in, keys_ref, 0)
    pick("sk", sk_in, keys_ref, cart_rows)
    stages = (
        (2, open_grads, step_grads, close_grads),
        (1, open_weights, step_weights, close_weights),
        (0, open_scores, step_scores, close_scores),
    )
    for turn in range(blocks + 2):
        live = [(turn - lag, *calls) for lag, *calls in stages if 0 <= turn - lag < blocks]
        if turn == 1:
            pick("cv", cv_in, vals_ref, 0)
            pick("sv", sv_in, vals_ref, cart_rows)
            keys_t_ref[...] = keys_ref[...].astype(f32).T.astype(bf16)
        for block, begin_call, _, _ in live:
            begin_call(block)
        for index in range(len(pieces(0))):
            for block, _, step_call, _ in live:
                step_call(block, *pieces(block)[index])
        for block, _, _, end_call in live:
            end_call(block)

    part_rows = cart_rows // dp_size
    me = lax.axis_index("dp")
    for step, ref in enumerate(cart_outs):
        target = target_of(me, step, "dp", dp_size)
        at = pl.ds(pl.multiple_of(target * part_rows, part_rows), part_rows)
        ref[0] = (dk_ref[at, :] * scale).astype(ref.dtype)
        ref[1] = dv_ref[at, :].astype(ref.dtype)
    own = dk_ref[cart_rows:all_keys, :] * scale, dv_ref[cart_rows:all_keys, :]
    own_tokens = tokens // heads_size
    columns = width * head_dim
    me = lax.axis_index("heads")
    for place, (step, ref) in enumerate(zip(near_steps + far_steps, dq_outs)):
        target = target_of(me, step, "heads", heads_size)
        at = pl.ds(pl.multiple_of(target * own_tokens, own_tokens), own_tokens)
        if last and place < kept:
            for index in range(held):
                ref[:, index * columns : (index + 1) * columns] = dq_before[index * kept + place][...]
            ref[:, held * columns :] = dq_ref[at, :]
        else:
            ref[...] = dq_ref[at, :]
    if not last:
        self_ref[0], self_ref[1] = own
        return
    count = tokens * kv_local
    for kind in range(2):
        for index, before in enumerate(self_before):
            wide_ref[pl.ds(index, tokens, stride=kv_local), :] = before[kind]
        wide_ref[pl.ds(kv_index, tokens, stride=kv_local), :] = own[kind]
        self_ref[kind * count : (kind + 1) * count, :] = wide_ref[0:count, :].astype(bf16)


def sum_kernel(*refs):
    part_refs, out_ref = refs[:-1], refs[-1]
    total = part_refs[0][...]
    for ref in part_refs[1:]:
        total = total + ref[...].astype(f32)
    out_ref[...] = total


def cart_kernel(kv_local, *refs):
    done_refs, part_refs, out_ref = refs[: kv_local - 1], refs[kv_local - 1 : -1], refs[-1]
    part_rows = part_refs[0].shape[1]
    for kind in range(2):
        total = part_refs[0][kind]
        for ref in part_refs[1:]:
            total = total + ref[kind].astype(f32)
        for kv_index, part in enumerate((*[ref[kind] for ref in done_refs], total)):
            out_ref[pl.ds(kind * kv_local + kv_index, part_rows, stride=2 * kv_local), :] = part


def place_kernel(heads_size, kv_local, *refs):
    part_refs, out_ref, sems = refs[:-2], refs[-2], refs[-1]
    near_steps, far_steps = split_steps(heads_size)
    columns = out_ref.shape[1] // (heads_size * kv_local)
    me = lax.axis_index("heads")
    places = [(step, 0) for step in near_steps]
    places += [(step, kv_index) for kv_index in range(kv_local) for step in far_steps]
    copies = []
    for index, ((step, kv_index), ref) in enumerate(zip(places, part_refs)):
        source = source_of(me, step, "heads", heads_size)
        at = pl.multiple_of((source * kv_local + kv_index) * columns, columns)
        copies.append(pltpu.make_async_copy(ref, out_ref.at[:, pl.ds(at, ref.shape[1])], sems.at[index]))
    for copy in copies:
        copy.start()
    for copy in copies:
        copy.wait()


def paired(axis, size):
    return axis == "heads" and size & (size - 1) == 0


def target_of(me, step, axis, size):
    return me ^ step if paired(axis, size) else (me + step) % size


def source_of(me, step, axis, size):
    return me ^ step if paired(axis, size) else (me + size - step) % size


def shift(values, axis, size, step):
    if step == 0:
        return values
    return lax.ppermute(values, axis, [(source, target_of(source, step, axis, size)) for source in range(size)])


def split_steps(heads_size):
    early = [step for step in range(heads_size) if step in early_steps]
    return [step for step in range(heads_size) if step not in early], early


def on_device(dp_size, heads_size, queries, out_grad, self_keys, self_values, cart_keys, cart_values, segment_ids):
    tokens, heads_local, head_dim = queries.shape
    kv_local = self_keys.shape[1]
    cart_rows = cart_keys.shape[0]
    width = heads_local // kv_local
    block_tokens = 64
    chunk = 512
    fine = 128
    sub = 16
    all_keys = cart_rows + tokens
    rows = block_tokens * width
    part_rows = cart_rows // dp_size
    own_tokens = tokens // heads_size
    flat = [array.reshape(-1, head_dim) for array in (queries, out_grad, self_keys, self_values, cart_keys, cart_values)]
    macs = tokens * width * all_keys * head_dim * 5
    blocks = tokens // block_tokens
    columns = width * head_dim
    count = tokens * kv_local
    near_steps, far_steps = split_steps(heads_size)
    kept = len(near_steps)
    anywhere = pl.BlockSpec(memory_space=pl.ANY)
    cart_list, kept_list, far_list, self_list, received = [], [], [], [], []
    for kv_index in range(kv_local):
        last = kv_index == kv_local - 1
        near = jax.ShapeDtypeStruct((own_tokens, kv_local * columns if last else columns), bf16)
        far = jax.ShapeDtypeStruct((own_tokens, columns), bf16)
        own_shape = (2 * count, head_dim) if last else (2, tokens, head_dim)
        other_shapes = [near] * kept + [far] * (heads_size - kept)
        other_shapes.append(jax.ShapeDtypeStruct(own_shape, bf16 if last else f32))
        before = kept_list + self_list
        outs = pl.pallas_call(
            functools.partial(head_kernel, dp_size, heads_size, kv_index, kv_local, width, block_tokens, chunk, fine, sub),
            out_shape=(
                *[
                    jax.ShapeDtypeStruct((2, part_rows, head_dim), bf16 if step else f32)
                    for step in range(dp_size)
                ],
                *other_shapes,
            ),
            in_specs=[pl.BlockSpec(memory_space=pltpu.HBM)] * 6
            + [pl.BlockSpec(memory_space=pltpu.VMEM)] * (1 + (len(before) if last else 0)),
            scratch_shapes=[
                pltpu.VMEM((cart_rows * kv_local, head_dim), f32),
                pltpu.VMEM((all_keys, head_dim), bf16),
                pltpu.VMEM((all_keys, head_dim), bf16),
                pltpu.VMEM((head_dim, all_keys), bf16),
                pltpu.VMEM((2, all_keys, rows), f32),
                pltpu.VMEM((2, all_keys, rows), f32),
                pltpu.VMEM((2, all_keys, rows), f32),
                pltpu.VMEM((2, all_keys, rows), bf16),
                pltpu.VMEM((2, all_keys, rows), bf16),
                pltpu.VMEM((all_keys, head_dim), f32),
                pltpu.VMEM((all_keys, head_dim), f32),
                pltpu.VMEM((rows, head_dim), f32),
                pltpu.VMEM((tokens, columns), bf16),
                *[pltpu.VMEM(array.shape, bf16) for array in flat],
                pltpu.SemaphoreType.DMA((4 + 2 * blocks,)),
            ],
            compiler_params=pltpu.CompilerParams(vmem_limit_bytes=vmem_bytes),
            cost_estimate=pl.CostEstimate(flops=4 * macs, bytes_accessed=5 * 2**20, transcendentals=tokens * width * all_keys),
            name="head_grads",
        )(*flat, segment_ids, *(before if last else []))
        cart_sends, near, far = outs[1:dp_size], outs[dp_size : dp_size + kept], outs[dp_size + kept : -1]
        if last:
            cart_sends, near, far, received = lax.optimization_barrier((cart_sends, near, far, received))
        else:
            kept_list += near
            self_list.append(outs[-1])
        cart_parts = [outs[0], *[shift(part, "dp", dp_size, step + 1) for step, part in enumerate(cart_sends)]]
        far_parts = [shift(part, "heads", heads_size, step) for step, part in zip(far_steps, far)]
        if not last:
            received.append((cart_parts, far_parts))
    for early_cart, early_far in received:
        cart_list.append(
            pl.pallas_call(
                sum_kernel,
                out_shape=jax.ShapeDtypeStruct((2, part_rows, head_dim), f32),
                compiler_params=pltpu.CompilerParams(vmem_limit_bytes=small_vmem_bytes),
                cost_estimate=pl.CostEstimate(flops=2**20, bytes_accessed=2**20, transcendentals=0),
                name="cart_sum",
            )(*early_cart)
        )
        far_list += early_far
    query_list = [shift(part, "heads", heads_size, step) for step, part in zip(near_steps, near)] + far_list + far_parts
    query_grads = pl.pallas_call(
        functools.partial(place_kernel, heads_size, kv_local),
        out_shape=jax.ShapeDtypeStruct((own_tokens, heads_size * heads_local * head_dim), bf16),
        in_specs=[anywhere] * len(query_list),
        out_specs=anywhere,
        scratch_shapes=[pltpu.SemaphoreType.DMA((len(query_list),))],
        compiler_params=pltpu.CompilerParams(vmem_limit_bytes=small_vmem_bytes),
        cost_estimate=pl.CostEstimate(flops=2**20, bytes_accessed=2 * 2**20, transcendentals=0),
        name="place_queries",
    )(*query_list)
    cart_grads = pl.pallas_call(
        functools.partial(cart_kernel, kv_local),
        out_shape=jax.ShapeDtypeStruct((part_rows * 2 * kv_local, head_dim), f32),
        compiler_params=pltpu.CompilerParams(vmem_limit_bytes=small_vmem_bytes),
        cost_estimate=pl.CostEstimate(flops=2**20, bytes_accessed=2 * 2**20, transcendentals=0),
        name="cart_grads",
    )(*cart_list, *cart_parts)
    cart_grads = cart_grads.reshape(part_rows, 2, kv_local, head_dim)
    self_grads = outs[-1].reshape(2, tokens, kv_local, head_dim)
    return (cart_grads, self_grads, query_grads)


def solution(mesh):
    in_specs = (
        P(("groups", "dp"), "heads", None),
        P(("groups", "dp"), "heads", None),
        P(("groups", "dp"), "heads", None),
        P(("groups", "dp"), "heads", None),
        P("groups", "heads", None),
        P("groups", "heads", None),
        P(("groups", "dp"), None),
    )
    out_specs = (
        P(("groups", "dp"), None, "heads", None),
        P(None, ("groups", "dp"), "heads", None),
        P(("groups", "dp", "heads"), None),
    )
    return jax.shard_map(
        functools.partial(on_device, mesh.shape["dp"], mesh.shape["heads"]),
        mesh=mesh, in_specs=in_specs, out_specs=out_specs, check_vma=False,
    )
```

```python
import functools
import math

import jax
import jax.numpy as jnp
from jax import lax
from jax.experimental import pallas as pl
from jax.experimental.pallas import tpu as pltpu
from jax.sharding import PartitionSpec as P

masked_score = -1e30
vmem_bytes = 56 * 1024 * 1024
small_vmem_bytes = 8 * 1024 * 1024
early_steps = (2,)
f32 = jnp.float32
bf16 = jnp.bfloat16


def dot_nt(left, right):
    return lax.dot_general(left, right, (((1,), (1,)), ((), ())), preferred_element_type=f32)


def dot_nn(left, right):
    return lax.dot_general(left, right, (((1,), (0,)), ((), ())), preferred_element_type=f32)


def fold_rows(values, op):
    rows, columns = values.shape
    return op(values.reshape(rows // 8, 8, columns), axis=0)


def head_kernel(dp_size, heads_size, kv_index, kv_local, width, block_tokens, chunk, fine, sub, *refs):
    last = kv_index == kv_local - 1
    q_ref, g_ref, sk_ref, sv_ref, ck_ref, cv_ref, seg_ref = refs[:7]
    refs = refs[7:]
    held = kv_index if last else 0
    near_steps, far_steps = split_steps(heads_size)
    kept = len(near_steps)
    dq_before, refs = refs[: held * kept], refs[held * kept :]
    self_before, refs = refs[:held], refs[held:]
    (keep_ref, send_ref), refs = refs[:2], refs[2:]
    dq_outs, self_ref, refs = refs[:heads_size], refs[heads_size], refs[heads_size + 1 :]
    (
        wide_ref, keys_ref, vals_ref, keys_t_ref, s_ref, w_ref, d_ref, p_ref, ds_ref, dk_ref, dv_ref, out_ref, dq_ref,
        q_in, g_in, sk_in, sv_in, ck_in, cv_in, sems,
    ) = refs
    head_dim = q_ref.shape[1]
    tokens = seg_ref.shape[1]
    cart_rows = ck_ref.shape[0] // kv_local
    all_keys = cart_rows + tokens
    rows = block_tokens * width
    scale = head_dim ** -0.5
    scale2 = scale * math.log2(math.e)
    span = block_tokens * kv_local * width
    blocks = tokens // block_tokens

    def block_copy(source, target, block, sem):
        at = slice(block * span, (block + 1) * span)
        return pltpu.make_async_copy(source.at[at, :], target.at[at, :], sems.at[sem])

    copies = {
        name: pltpu.make_async_copy(source, target, sems.at[at])
        for at, (name, source, target) in enumerate(
            [("ck", ck_ref, ck_in), ("sk", sk_ref, sk_in), ("cv", cv_ref, cv_in), ("sv", sv_ref, sv_in)]
        )
    }
    for block in range(blocks):
        copies["q", block] = block_copy(q_ref, q_in, block, 4 + block)
        copies["g", block] = block_copy(g_ref, g_in, block, 4 + blocks + block)
    order = ["ck", "sk", ("q", 0), "cv", "sv", ("g", 0)]
    order += [(kind, block) for block in range(1, blocks) for kind in ("q", "g")]
    for name in order:
        copies[name].start()

    def pick(name, ref, dst, at):
        copies[name].wait()
        count = ref.shape[0] // kv_local
        if kv_local == 1:
            dst[at : at + count, :] = ref[...]
        else:
            wide_ref[0 : ref.shape[0], :] = ref[...].astype(f32)
            dst[at : at + count, :] = wide_ref[pl.ds(kv_index, count, stride=kv_local), :].astype(bf16)

    def rows_of(name, ref, block):
        copies[name, block].wait()
        wide = ref[block * span : (block + 1) * span, :]
        if kv_local == 1:
            return wide
        wide = wide.astype(f32).reshape(block_tokens, kv_local, width, head_dim)
        return wide[:, kv_index].reshape(rows, head_dim).astype(bf16)

    first_count = jnp.sum((seg_ref[...] == 0).astype(f32), axis=1, keepdims=True).astype(jnp.int32)

    def limit(block):
        return -(-(block + 1) * block_tokens // fine) * fine

    def pieces(block):
        cart = [(start, chunk) for start in range(0, cart_rows, chunk)]
        return cart + [(cart_rows, limit(block))]

    queries, grads, peaks, stats = {}, {}, {}, {}
    acc = {}

    def spread(values):
        return jnp.concatenate([values] * (sub // 8), axis=0)

    def subs(start, size):
        return [slice(at, at + sub) for at in range(start, start + size, sub)]

    def open_scores(block):
        queries[block] = rows_of("q", q_in, block)
        token = (lax.broadcasted_iota(jnp.int32, (1, rows), 1) + block * rows) // width
        begin = jnp.where(token >= first_count, first_count, 0)
        acc["peak"] = jnp.full((8, rows), masked_score, f32)
        acc["token"], acc["begin"] = token, begin

    def step_scores(block, start, size):
        s_ref[block % 2, start : start + size, :] = dot_nt(keys_ref[start : start + size, :], queries[block])
        for at in subs(start, size):
            score = s_ref[block % 2, at, :]
            if start >= cart_rows:
                key_at = lax.broadcasted_iota(jnp.int32, (sub, rows), 0) + (at.start - cart_rows)
                score = jnp.where((key_at >= acc["begin"]) & (key_at <= acc["token"]), score, masked_score)
                s_ref[block % 2, at, :] = score
            acc["peak"] = jnp.maximum(acc["peak"], fold_rows(score, jnp.max))

    def close_scores(block):
        peaks[block] = jnp.broadcast_to(jnp.max(acc["peak"], axis=0, keepdims=True), (8, rows))

    def open_weights(block):
        grads[block] = rows_of("g", g_in, block)
        acc["total"] = jnp.zeros((8, rows), f32)
        acc["center"] = jnp.zeros((8, rows), f32)

    def step_weights(block, start, size):
        d_ref[block % 2, start : start + size, :] = dot_nt(vals_ref[start : start + size, :], grads[block])
        for at in subs(start, size):
            weight = jnp.exp2((s_ref[block % 2, at, :] - spread(peaks[block])) * scale2)
            w_ref[block % 2, at, :] = weight
            acc["total"] = acc["total"] + fold_rows(weight, jnp.sum)
            acc["center"] = acc["center"] + fold_rows(weight * d_ref[block % 2, at, :], jnp.sum)

    def close_weights(block):
        share = 1.0 / jnp.sum(acc["total"], axis=0, keepdims=True)
        center = jnp.sum(acc["center"], axis=0, keepdims=True) * share
        stats[block] = jnp.broadcast_to(share, (8, rows)), jnp.broadcast_to(center, (8, rows))

    def open_grads(block):
        pass

    def step_grads(block, start, size):
        slot = block % 2
        share, center = stats[block]
        for at in subs(start, size):
            prob = w_ref[slot, at, :] * spread(share)
            p_ref[slot, at, :] = prob.astype(bf16)
            ds_ref[slot, at, :] = (prob * (d_ref[slot, at, :] - spread(center))).astype(bf16)
        at = slice(start, start + size)
        old = size if start < cart_rows else (limit(block - 1) if block else 0)
        old = old if block else 0
        for ref, left, right in ((dv_ref, p_ref, grads[block]), (dk_ref, ds_ref, queries[block])):
            part = dot_nn(left[slot, at, :], right)
            if old:
                ref[start : start + old, :] += part[:old]
            if old < size:
                ref[start + old : start + size, :] = part[old:]

    def close_grads(block):
        seen = cart_rows + limit(block)
        dq_t = dot_nn(keys_t_ref[:, 0:seen], ds_ref[block % 2, 0:seen, :])
        out_ref[...] = (dq_t * scale).T
        for head in range(width):
            dq_ref[block * block_tokens : (block + 1) * block_tokens, head * head_dim : (head + 1) * head_dim] = (
                out_ref[pl.ds(head, block_tokens, stride=width), :].astype(bf16)
            )

    pick("ck", ck_in, keys_ref, 0)
    pick("sk", sk_in, keys_ref, cart_rows)
    stages = (
        (2, open_grads, step_grads, close_grads),
        (1, open_weights, step_weights, close_weights),
        (0, open_scores, step_scores, close_scores),
    )
    for turn in range(blocks + 2):
        live = [(turn - lag, *calls) for lag, *calls in stages if 0 <= turn - lag < blocks]
        if turn == 1:
            pick("cv", cv_in, vals_ref, 0)
            pick("sv", sv_in, vals_ref, cart_rows)
            keys_t_ref[...] = keys_ref[...].astype(f32).T.astype(bf16)
        for block, begin_call, _, _ in live:
            begin_call(block)
        for index in range(len(pieces(0))):
            for block, _, step_call, _ in live:
                step_call(block, *pieces(block)[index])
        for block, _, _, end_call in live:
            end_call(block)

    part_rows = cart_rows // dp_size
    me = lax.axis_index("dp")
    for step in range(dp_size):
        at = pl.ds(pl.multiple_of((me ^ step) * part_rows, part_rows), part_rows)
        ref = send_ref if step % 2 else keep_ref
        ref[step // 2, 0] = (dk_ref[at, :] * scale).astype(ref.dtype)
        ref[step // 2, 1] = dv_ref[at, :].astype(ref.dtype)
    own = dk_ref[cart_rows:all_keys, :] * scale, dv_ref[cart_rows:all_keys, :]
    own_tokens = tokens // heads_size
    columns = width * head_dim
    me = lax.axis_index("heads")
    for place, (step, ref) in enumerate(zip(near_steps + far_steps, dq_outs)):
        target = me ^ step
        at = pl.ds(pl.multiple_of(target * own_tokens, own_tokens), own_tokens)
        if last and place < kept:
            for index in range(held):
                ref[:, index * columns : (index + 1) * columns] = dq_before[index * kept + place][...]
            ref[:, held * columns :] = dq_ref[at, :]
        else:
            ref[...] = dq_ref[at, :]
    if not last:
        self_ref[0], self_ref[1] = own
        return
    count = tokens * kv_local
    for kind in range(2):
        for index, before in enumerate(self_before):
            wide_ref[pl.ds(index, tokens, stride=kv_local), :] = before[kind]
        wide_ref[pl.ds(kv_index, tokens, stride=kv_local), :] = own[kind]
        self_ref[kind * count : (kind + 1) * count, :] = wide_ref[0:count, :].astype(bf16)


def fold_kernel(part_ref, got_ref, keep_ref, send_ref):
    for index in range(part_ref.shape[0]):
        total = part_ref[index] + got_ref[index].astype(f32)
        ref = send_ref if index % 2 else keep_ref
        ref[index // 2] = total.astype(ref.dtype)


def cart_kernel(kv_local, *refs):
    part_refs, got_refs, out_ref = refs[:kv_local], refs[kv_local:-1], refs[-1]
    part_rows = part_refs[0].shape[2]
    for kv_index in range(kv_local):
        for kind in range(2):
            total = part_refs[kv_index][0, kind] + got_refs[kv_index][0, kind].astype(f32)
            out_ref[pl.ds(kind * kv_local + kv_index, part_rows, stride=2 * kv_local), :] = total


def place_kernel(heads_size, kv_local, *refs):
    part_refs, out_ref, sems = refs[:-2], refs[-2], refs[-1]
    near_steps, far_steps = split_steps(heads_size)
    columns = out_ref.shape[1] // (heads_size * kv_local)
    me = lax.axis_index("heads")
    places = [(step, 0) for step in near_steps]
    places += [(step, kv_index) for kv_index in range(kv_local) for step in far_steps]
    copies = []
    for index, ((step, kv_index), ref) in enumerate(zip(places, part_refs)):
        source = me ^ step
        at = pl.multiple_of((source * kv_local + kv_index) * columns, columns)
        copies.append(pltpu.make_async_copy(ref, out_ref.at[:, pl.ds(at, ref.shape[1])], sems.at[index]))
    for copy in copies:
        copy.start()
    for copy in copies:
        copy.wait()


def swap(values, axis, size, step):
    if step == 0:
        return values
    return lax.ppermute(values, axis, [(source, source ^ step) for source in range(size)])


def fold(part, got):
    half = part.shape[0] // 2
    return pl.pallas_call(
        fold_kernel,
        out_shape=(
            jax.ShapeDtypeStruct((half, *part.shape[1:]), f32),
            jax.ShapeDtypeStruct((half, *part.shape[1:]), bf16),
        ),
        compiler_params=pltpu.CompilerParams(vmem_limit_bytes=small_vmem_bytes),
        cost_estimate=pl.CostEstimate(flops=2**20, bytes_accessed=2**20, transcendentals=0),
        name="cart_fold",
    )(part, got)


def split_steps(heads_size):
    early = [step for step in range(heads_size) if step in early_steps]
    return [step for step in range(heads_size) if step not in early], early


def on_device(dp_size, heads_size, queries, out_grad, self_keys, self_values, cart_keys, cart_values, segment_ids):
    tokens, heads_local, head_dim = queries.shape
    kv_local = self_keys.shape[1]
    cart_rows = cart_keys.shape[0]
    width = heads_local // kv_local
    block_tokens = 64
    chunk = 512
    fine = 128
    sub = 16
    all_keys = cart_rows + tokens
    rows = block_tokens * width
    part_rows = cart_rows // dp_size
    own_tokens = tokens // heads_size
    flat = [array.reshape(-1, head_dim) for array in (queries, out_grad, self_keys, self_values, cart_keys, cart_values)]
    macs = tokens * width * all_keys * head_dim * 5
    blocks = tokens // block_tokens
    columns = width * head_dim
    count = tokens * kv_local
    near_steps, far_steps = split_steps(heads_size)
    kept = len(near_steps)
    anywhere = pl.BlockSpec(memory_space=pl.ANY)
    cart_list, kept_list, far_list, self_list, received = [], [], [], [], []
    for kv_index in range(kv_local):
        last = kv_index == kv_local - 1
        near = jax.ShapeDtypeStruct((own_tokens, kv_local * columns if last else columns), bf16)
        far = jax.ShapeDtypeStruct((own_tokens, columns), bf16)
        own_shape = (2 * count, head_dim) if last else (2, tokens, head_dim)
        other_shapes = [near] * kept + [far] * (heads_size - kept)
        other_shapes.append(jax.ShapeDtypeStruct(own_shape, bf16 if last else f32))
        before = kept_list + self_list
        outs = pl.pallas_call(
            functools.partial(head_kernel, dp_size, heads_size, kv_index, kv_local, width, block_tokens, chunk, fine, sub),
            out_shape=(
                jax.ShapeDtypeStruct((dp_size // 2, 2, part_rows, head_dim), f32),
                jax.ShapeDtypeStruct((dp_size // 2, 2, part_rows, head_dim), bf16),
                *other_shapes,
            ),
            in_specs=[pl.BlockSpec(memory_space=pltpu.HBM)] * 6
            + [pl.BlockSpec(memory_space=pltpu.VMEM)] * (1 + (len(before) if last else 0)),
            scratch_shapes=[
                pltpu.VMEM((cart_rows * kv_local, head_dim), f32),
                pltpu.VMEM((all_keys, head_dim), bf16),
                pltpu.VMEM((all_keys, head_dim), bf16),
                pltpu.VMEM((head_dim, all_keys), bf16),
                pltpu.VMEM((2, all_keys, rows), f32),
                pltpu.VMEM((2, all_keys, rows), f32),
                pltpu.VMEM((2, all_keys, rows), f32),
                pltpu.VMEM((2, all_keys, rows), bf16),
                pltpu.VMEM((2, all_keys, rows), bf16),
                pltpu.VMEM((all_keys, head_dim), f32),
                pltpu.VMEM((all_keys, head_dim), f32),
                pltpu.VMEM((rows, head_dim), f32),
                pltpu.VMEM((tokens, columns), bf16),
                *[pltpu.VMEM(array.shape, bf16) for array in flat],
                pltpu.SemaphoreType.DMA((4 + 2 * blocks,)),
            ],
            compiler_params=pltpu.CompilerParams(vmem_limit_bytes=vmem_bytes),
            cost_estimate=pl.CostEstimate(flops=4 * macs, bytes_accessed=5 * 2**20, transcendentals=tokens * width * all_keys),
            name="head_grads",
        )(*flat, segment_ids, *(before if last else []))
        part, send, near, far = outs[0], outs[1], outs[2 : 2 + kept], outs[2 + kept : -1]
        if last:
            part, send, near, far, received = lax.optimization_barrier((part, send, near, far, received))
        else:
            kept_list += near
            self_list.append(outs[-1])
        received.append((part, swap(send, "dp", dp_size, 1)))
        far_parts = [swap(block, "heads", heads_size, step) for step, block in zip(far_steps, far)]
        if not last:
            received[-1] += tuple(far_parts)
    far_list = [block for _, _, *blocks_far in received for block in blocks_far]
    for part, got, *_ in received:
        step = 2
        while step < dp_size:
            part, send = fold(part, got)
            got = swap(send, "dp", dp_size, step)
            step *= 2
        cart_list.append((part, got))
    query_list = [swap(block, "heads", heads_size, step) for step, block in zip(near_steps, near)] + far_list + far_parts
    query_grads = pl.pallas_call(
        functools.partial(place_kernel, heads_size, kv_local),
        out_shape=jax.ShapeDtypeStruct((own_tokens, heads_size * heads_local * head_dim), bf16),
        in_specs=[anywhere] * len(query_list),
        out_specs=anywhere,
        scratch_shapes=[pltpu.SemaphoreType.DMA((len(query_list),))],
        compiler_params=pltpu.CompilerParams(vmem_limit_bytes=small_vmem_bytes),
        cost_estimate=pl.CostEstimate(flops=2**20, bytes_accessed=2 * 2**20, transcendentals=0),
        name="place_queries",
    )(*query_list)
    cart_grads = pl.pallas_call(
        functools.partial(cart_kernel, kv_local),
        out_shape=jax.ShapeDtypeStruct((part_rows * 2 * kv_local, head_dim), f32),
        compiler_params=pltpu.CompilerParams(vmem_limit_bytes=small_vmem_bytes),
        cost_estimate=pl.CostEstimate(flops=2**20, bytes_accessed=2 * 2**20, transcendentals=0),
        name="cart_grads",
    )(*[part for part, _ in cart_list], *[got for _, got in cart_list])
    cart_grads = cart_grads.reshape(part_rows, 2, kv_local, head_dim)
    self_grads = outs[-1].reshape(2, tokens, kv_local, head_dim)
    return (cart_grads, self_grads, query_grads)


def solution(mesh):
    in_specs = (
        P(("groups", "dp"), "heads", None),
        P(("groups", "dp"), "heads", None),
        P(("groups", "dp"), "heads", None),
        P(("groups", "dp"), "heads", None),
        P("groups", "heads", None),
        P("groups", "heads", None),
        P(("groups", "dp"), None),
    )
    out_specs = (
        P(("groups", "dp"), None, "heads", None),
        P(None, ("groups", "dp"), "heads", None),
        P(("groups", "dp", "heads"), None),
    )
    return jax.shard_map(
        functools.partial(on_device, mesh.shape["dp"], mesh.shape["heads"]),
        mesh=mesh, in_specs=in_specs, out_specs=out_specs, check_vma=False,
    )
```

```python
import functools
import math

import jax
import jax.numpy as jnp
from jax import lax
from jax.experimental import pallas as pl
from jax.experimental.pallas import tpu as pltpu
from jax.sharding import PartitionSpec as P

masked_score = -1e30
vmem_bytes = 56 * 1024 * 1024
small_vmem_bytes = 8 * 1024 * 1024
early_steps = ()
f32 = jnp.float32
bf16 = jnp.bfloat16


def dot_nt(left, right):
    return lax.dot_general(left, right, (((1,), (1,)), ((), ())), preferred_element_type=f32)


def dot_nn(left, right):
    return lax.dot_general(left, right, (((1,), (0,)), ((), ())), preferred_element_type=f32)


def fold_rows(values, op):
    rows, columns = values.shape
    return op(values.reshape(rows // 8, 8, columns), axis=0)


def head_kernel(dp_size, heads_size, kv_index, kv_local, width, block_tokens, chunk, fine, sub, *refs):
    last = kv_index == kv_local - 1
    q_ref, g_ref, sk_ref, sv_ref, ck_ref, cv_ref, seg_ref = refs[:7]
    refs = refs[7:]
    held = kv_index if last else 0
    near_steps, far_steps = split_steps(heads_size)
    kept = len(near_steps)
    dq_before, refs = refs[: held * kept], refs[held * kept :]
    self_before, refs = refs[:held], refs[held:]
    (keep_ref, send_ref), refs = refs[:2], refs[2:]
    dq_outs, self_ref, refs = refs[:heads_size], refs[heads_size], refs[heads_size + 1 :]
    (
        wide_ref, keys_ref, vals_ref, keys_t_ref, s_ref, w_ref, d_ref, p_ref, ds_ref, dk_ref, dv_ref, out_ref, dq_ref,
        q_in, g_in, sk_in, sv_in, ck_in, cv_in, sems,
    ) = refs
    head_dim = q_ref.shape[1]
    tokens = seg_ref.shape[1]
    cart_rows = ck_ref.shape[0] // kv_local
    all_keys = cart_rows + tokens
    rows = block_tokens * width
    scale = head_dim ** -0.5
    scale2 = scale * math.log2(math.e)
    span = block_tokens * kv_local * width
    blocks = tokens // block_tokens

    def block_copy(source, target, block, sem):
        at = slice(block * span, (block + 1) * span)
        return pltpu.make_async_copy(source.at[at, :], target.at[at, :], sems.at[sem])

    copies = {
        name: pltpu.make_async_copy(source, target, sems.at[at])
        for at, (name, source, target) in enumerate(
            [("ck", ck_ref, ck_in), ("sk", sk_ref, sk_in), ("cv", cv_ref, cv_in), ("sv", sv_ref, sv_in)]
        )
    }
    for block in range(blocks):
        copies["q", block] = block_copy(q_ref, q_in, block, 4 + block)
        copies["g", block] = block_copy(g_ref, g_in, block, 4 + blocks + block)
    order = ["ck", "sk", ("q", 0), "cv", "sv", ("g", 0)]
    order += [(kind, block) for block in range(1, blocks) for kind in ("q", "g")]
    for name in order:
        copies[name].start()

    def pick(name, ref, dst, at):
        copies[name].wait()
        count = ref.shape[0] // kv_local
        if kv_local == 1:
            dst[at : at + count, :] = ref[...]
        else:
            wide_ref[0 : ref.shape[0], :] = ref[...].astype(f32)
            dst[at : at + count, :] = wide_ref[pl.ds(kv_index, count, stride=kv_local), :].astype(bf16)

    def rows_of(name, ref, block):
        copies[name, block].wait()
        wide = ref[block * span : (block + 1) * span, :]
        if kv_local == 1:
            return wide
        wide = wide.astype(f32).reshape(block_tokens, kv_local, width, head_dim)
        return wide[:, kv_index].reshape(rows, head_dim).astype(bf16)

    first_count = jnp.sum((seg_ref[...] == 0).astype(f32), axis=1, keepdims=True).astype(jnp.int32)

    def limit(block):
        return -(-(block + 1) * block_tokens // fine) * fine

    def pieces(block):
        cart = [(start, chunk) for start in range(0, cart_rows, chunk)]
        return cart + [(cart_rows, limit(block))]

    queries, grads, peaks, stats = {}, {}, {}, {}
    acc = {}

    def spread(values):
        return jnp.concatenate([values] * (sub // 8), axis=0)

    def subs(start, size):
        return [slice(at, at + sub) for at in range(start, start + size, sub)]

    def open_scores(block):
        queries[block] = rows_of("q", q_in, block)
        token = (lax.broadcasted_iota(jnp.int32, (1, rows), 1) + block * rows) // width
        begin = jnp.where(token >= first_count, first_count, 0)
        acc["peak"] = jnp.full((8, rows), masked_score, f32)
        acc["token"], acc["begin"] = token, begin

    def step_scores(block, start, size):
        s_ref[block % 2, start : start + size, :] = dot_nt(keys_ref[start : start + size, :], queries[block])
        for at in subs(start, size):
            score = s_ref[block % 2, at, :]
            if start >= cart_rows:
                key_at = lax.broadcasted_iota(jnp.int32, (sub, rows), 0) + (at.start - cart_rows)
                score = jnp.where((key_at >= acc["begin"]) & (key_at <= acc["token"]), score, masked_score)
                s_ref[block % 2, at, :] = score
            acc["peak"] = jnp.maximum(acc["peak"], fold_rows(score, jnp.max))

    def close_scores(block):
        peaks[block] = jnp.broadcast_to(jnp.max(acc["peak"], axis=0, keepdims=True), (8, rows))

    def open_weights(block):
        grads[block] = rows_of("g", g_in, block)
        acc["total"] = jnp.zeros((8, rows), f32)
        acc["center"] = jnp.zeros((8, rows), f32)

    def step_weights(block, start, size):
        d_ref[block % 2, start : start + size, :] = dot_nt(vals_ref[start : start + size, :], grads[block])
        for at in subs(start, size):
            weight = jnp.exp2((s_ref[block % 2, at, :] - spread(peaks[block])) * scale2)
            w_ref[block % 2, at, :] = weight
            acc["total"] = acc["total"] + fold_rows(weight, jnp.sum)
            acc["center"] = acc["center"] + fold_rows(weight * d_ref[block % 2, at, :], jnp.sum)

    def close_weights(block):
        share = 1.0 / jnp.sum(acc["total"], axis=0, keepdims=True)
        center = jnp.sum(acc["center"], axis=0, keepdims=True) * share
        stats[block] = jnp.broadcast_to(share, (8, rows)), jnp.broadcast_to(center, (8, rows))

    def open_grads(block):
        pass

    def step_grads(block, start, size):
        slot = block % 2
        share, center = stats[block]
        for at in subs(start, size):
            prob = w_ref[slot, at, :] * spread(share)
            p_ref[slot, at, :] = prob.astype(bf16)
            ds_ref[slot, at, :] = (prob * (d_ref[slot, at, :] - spread(center))).astype(bf16)
        at = slice(start, start + size)
        old = size if start < cart_rows else (limit(block - 1) if block else 0)
        old = old if block else 0
        for ref, left, right in ((dv_ref, p_ref, grads[block]), (dk_ref, ds_ref, queries[block])):
            part = dot_nn(left[slot, at, :], right)
            if old:
                ref[start : start + old, :] += part[:old]
            if old < size:
                ref[start + old : start + size, :] = part[old:]

    def close_grads(block):
        seen = cart_rows + limit(block)
        dq_t = dot_nn(keys_t_ref[:, 0:seen], ds_ref[block % 2, 0:seen, :])
        out_ref[...] = (dq_t * scale).T
        for head in range(width):
            dq_ref[block * block_tokens : (block + 1) * block_tokens, head * head_dim : (head + 1) * head_dim] = (
                out_ref[pl.ds(head, block_tokens, stride=width), :].astype(bf16)
            )

    pick("ck", ck_in, keys_ref, 0)
    pick("sk", sk_in, keys_ref, cart_rows)
    stages = (
        (2, open_grads, step_grads, close_grads),
        (1, open_weights, step_weights, close_weights),
        (0, open_scores, step_scores, close_scores),
    )
    for turn in range(blocks + 2):
        live = [(turn - lag, *calls) for lag, *calls in stages if 0 <= turn - lag < blocks]
        if turn == 1:
            pick("cv", cv_in, vals_ref, 0)
            pick("sv", sv_in, vals_ref, cart_rows)
            keys_t_ref[...] = keys_ref[...].astype(f32).T.astype(bf16)
        for block, begin_call, _, _ in live:
            begin_call(block)
        for index in range(len(pieces(0))):
            for block, _, step_call, _ in live:
                step_call(block, *pieces(block)[index])
        for block, _, _, end_call in live:
            end_call(block)

    part_rows = cart_rows // dp_size
    me = lax.axis_index("dp")
    half = dp_size // 2
    for index, share in enumerate(share_order(dp_size, last)):
        at = pl.ds(pl.multiple_of((me ^ share) * part_rows, part_rows), part_rows)
        ref = send_ref if index >= half else keep_ref
        ref[index % half, 0] = (dk_ref[at, :] * scale).astype(ref.dtype)
        ref[index % half, 1] = dv_ref[at, :].astype(ref.dtype)
    own = dk_ref[cart_rows:all_keys, :] * scale, dv_ref[cart_rows:all_keys, :]
    own_tokens = tokens // heads_size
    columns = width * head_dim
    me = lax.axis_index("heads")
    for place, (step, ref) in enumerate(zip(near_steps + far_steps, dq_outs)):
        target = me ^ step
        at = pl.ds(pl.multiple_of(target * own_tokens, own_tokens), own_tokens)
        if last and place < kept:
            for index in range(held):
                ref[:, index * columns : (index + 1) * columns] = dq_before[index * kept + place][...]
            ref[:, held * columns :] = dq_ref[at, :]
        else:
            ref[...] = dq_ref[at, :]
    if not last:
        self_ref[0], self_ref[1] = own
        return
    count = tokens * kv_local
    for kind in range(2):
        for index, before in enumerate(self_before):
            wide_ref[pl.ds(index, tokens, stride=kv_local), :] = before[kind]
        wide_ref[pl.ds(kv_index, tokens, stride=kv_local), :] = own[kind]
        self_ref[kind * count : (kind + 1) * count, :] = wide_ref[0:count, :].astype(bf16)


def fold_kernel(part_ref, got_ref, keep_ref, send_ref):
    half = keep_ref.shape[0]
    for index in range(2 * half):
        total = part_ref[index] + got_ref[index].astype(f32)
        ref = send_ref if index >= half else keep_ref
        ref[index % half] = total.astype(ref.dtype)


def cart_kernel(kv_local, *refs):
    part_refs, got_refs, out_ref = refs[:kv_local], refs[kv_local:-1], refs[-1]
    part_rows = part_refs[0].shape[2]
    for kv_index in range(kv_local):
        for kind in range(2):
            total = part_refs[kv_index][0, kind] + got_refs[kv_index][0, kind].astype(f32)
            out_ref[pl.ds(kind * kv_local + kv_index, part_rows, stride=2 * kv_local), :] = total


def place_kernel(heads_size, kv_local, *refs):
    part_refs, out_ref, sems = refs[:-2], refs[-2], refs[-1]
    near_steps, far_steps = split_steps(heads_size)
    columns = out_ref.shape[1] // (heads_size * kv_local)
    me = lax.axis_index("heads")
    places = [(step, 0) for step in near_steps]
    places += [(step, kv_index) for kv_index in range(kv_local) for step in far_steps]
    copies = []
    for index, ((step, kv_index), ref) in enumerate(zip(places, part_refs)):
        source = me ^ step
        at = pl.multiple_of((source * kv_local + kv_index) * columns, columns)
        copies.append(pltpu.make_async_copy(ref, out_ref.at[:, pl.ds(at, ref.shape[1])], sems.at[index]))
    for copy in copies:
        copy.start()
    for copy in copies:
        copy.wait()


def swap(values, axis, size, step):
    if step == 0:
        return values
    return lax.ppermute(values, axis, [(source, source ^ step) for source in range(size)])


def fold(part, got):
    half = part.shape[0] // 2
    return pl.pallas_call(
        fold_kernel,
        out_shape=(
            jax.ShapeDtypeStruct((half, *part.shape[1:]), f32),
            jax.ShapeDtypeStruct((half, *part.shape[1:]), bf16),
        ),
        compiler_params=pltpu.CompilerParams(vmem_limit_bytes=small_vmem_bytes),
        cost_estimate=pl.CostEstimate(flops=2**20, bytes_accessed=2**20, transcendentals=0),
        name="cart_fold",
    )(part, got)


def split_steps(heads_size):
    early = [step for step in range(heads_size) if step in early_steps]
    late = [0, *range(2, heads_size), 1]
    return [step for step in late if step < heads_size and step not in early], early


def swap_order(dp_size, last):
    bits = [1 << bit for bit in range(dp_size.bit_length() - 1)]
    return bits if last else bits[::-1]


def share_order(dp_size, last):
    shares = [0]
    for bit in reversed(swap_order(dp_size, last)):
        shares = shares + [share ^ bit for share in shares]
    return shares


def on_device(dp_size, heads_size, queries, out_grad, self_keys, self_values, cart_keys, cart_values, segment_ids):
    tokens, heads_local, head_dim = queries.shape
    kv_local = self_keys.shape[1]
    cart_rows = cart_keys.shape[0]
    width = heads_local // kv_local
    block_tokens = 64
    chunk = 512
    fine = 128
    sub = 16
    all_keys = cart_rows + tokens
    rows = block_tokens * width
    part_rows = cart_rows // dp_size
    own_tokens = tokens // heads_size
    flat = [array.reshape(-1, head_dim) for array in (queries, out_grad, self_keys, self_values, cart_keys, cart_values)]
    macs = tokens * width * all_keys * head_dim * 5
    blocks = tokens // block_tokens
    columns = width * head_dim
    count = tokens * kv_local
    near_steps, far_steps = split_steps(heads_size)
    kept = len(near_steps)
    anywhere = pl.BlockSpec(memory_space=pl.ANY)
    kept_list, self_list, received = [], [], []
    for kv_index in range(kv_local):
        last = kv_index == kv_local - 1
        near = jax.ShapeDtypeStruct((own_tokens, kv_local * columns if last else columns), bf16)
        far = jax.ShapeDtypeStruct((own_tokens, columns), bf16)
        own_shape = (2 * count, head_dim) if last else (2, tokens, head_dim)
        other_shapes = [near] * kept + [far] * (heads_size - kept)
        other_shapes.append(jax.ShapeDtypeStruct(own_shape, bf16 if last else f32))
        before = kept_list + self_list
        outs = pl.pallas_call(
            functools.partial(head_kernel, dp_size, heads_size, kv_index, kv_local, width, block_tokens, chunk, fine, sub),
            out_shape=(
                jax.ShapeDtypeStruct((dp_size // 2, 2, part_rows, head_dim), f32),
                jax.ShapeDtypeStruct((dp_size // 2, 2, part_rows, head_dim), bf16),
                *other_shapes,
            ),
            in_specs=[pl.BlockSpec(memory_space=pltpu.HBM)] * 6
            + [pl.BlockSpec(memory_space=pltpu.VMEM)] * (1 + (len(before) if last else 0)),
            scratch_shapes=[
                pltpu.VMEM((cart_rows * kv_local, head_dim), f32),
                pltpu.VMEM((all_keys, head_dim), bf16),
                pltpu.VMEM((all_keys, head_dim), bf16),
                pltpu.VMEM((head_dim, all_keys), bf16),
                pltpu.VMEM((2, all_keys, rows), f32),
                pltpu.VMEM((2, all_keys, rows), f32),
                pltpu.VMEM((2, all_keys, rows), f32),
                pltpu.VMEM((2, all_keys, rows), bf16),
                pltpu.VMEM((2, all_keys, rows), bf16),
                pltpu.VMEM((all_keys, head_dim), f32),
                pltpu.VMEM((all_keys, head_dim), f32),
                pltpu.VMEM((rows, head_dim), f32),
                pltpu.VMEM((tokens, columns), bf16),
                *[pltpu.VMEM(array.shape, bf16) for array in flat],
                pltpu.SemaphoreType.DMA((4 + 2 * blocks,)),
            ],
            compiler_params=pltpu.CompilerParams(vmem_limit_bytes=vmem_bytes),
            cost_estimate=pl.CostEstimate(flops=4 * macs, bytes_accessed=5 * 2**20, transcendentals=tokens * width * all_keys),
            name="head_grads",
        )(*flat, segment_ids, *(before if last else []))
        part, send, near, far = outs[0], outs[1], outs[2 : 2 + kept], outs[2 + kept : -1]
        if last:
            part, send, near, far, received = lax.optimization_barrier((part, send, near, far, received))
        else:
            kept_list += near
            self_list.append(outs[-1])
        received.append((part, swap(send, "dp", dp_size, swap_order(dp_size, last)[0])))
        far_parts = [swap(block, "heads", heads_size, step) for step, block in zip(far_steps, far)]
        if not last:
            received[-1] += tuple(far_parts)
    far_list = [block for _, _, *blocks_far in received for block in blocks_far]
    state = [(part, got) for part, got, *_ in received]
    for level in range(1, dp_size.bit_length() - 1):
        state = [fold(part, got) for part, got in state]
        kept_parts, sends = zip(*state)
        sends = lax.optimization_barrier(sends)
        state = [
            (part, swap(send, "dp", dp_size, swap_order(dp_size, index == kv_local - 1)[level]))
            for index, (part, send) in reversed(list(enumerate(zip(kept_parts, sends))))
        ][::-1]
    cart_list = state
    query_list = [swap(block, "heads", heads_size, step) for step, block in zip(near_steps, near)] + far_list + far_parts
    query_grads = pl.pallas_call(
        functools.partial(place_kernel, heads_size, kv_local),
        out_shape=jax.ShapeDtypeStruct((own_tokens, heads_size * heads_local * head_dim), bf16),
        in_specs=[anywhere] * len(query_list),
        out_specs=anywhere,
        scratch_shapes=[pltpu.SemaphoreType.DMA((len(query_list),))],
        compiler_params=pltpu.CompilerParams(vmem_limit_bytes=small_vmem_bytes),
        cost_estimate=pl.CostEstimate(flops=2**20, bytes_accessed=2 * 2**20, transcendentals=0),
        name="place_queries",
    )(*query_list)
    cart_grads = pl.pallas_call(
        functools.partial(cart_kernel, kv_local),
        out_shape=jax.ShapeDtypeStruct((part_rows * 2 * kv_local, head_dim), f32),
        compiler_params=pltpu.CompilerParams(vmem_limit_bytes=small_vmem_bytes),
        cost_estimate=pl.CostEstimate(flops=2**20, bytes_accessed=2 * 2**20, transcendentals=0),
        name="cart_grads",
    )(*[part for part, _ in cart_list], *[got for _, got in cart_list])
    cart_grads = cart_grads.reshape(part_rows, 2, kv_local, head_dim)
    self_grads = outs[-1].reshape(2, tokens, kv_local, head_dim)
    return (cart_grads, self_grads, query_grads)


def solution(mesh):
    in_specs = (
        P(("groups", "dp"), "heads", None),
        P(("groups", "dp"), "heads", None),
        P(("groups", "dp"), "heads", None),
        P(("groups", "dp"), "heads", None),
        P("groups", "heads", None),
        P("groups", "heads", None),
        P(("groups", "dp"), None),
    )
    out_specs = (
        P(("groups", "dp"), None, "heads", None),
        P(None, ("groups", "dp"), "heads", None),
        P(("groups", "dp", "heads"), None),
    )
    return jax.shard_map(
        functools.partial(on_device, mesh.shape["dp"], mesh.shape["heads"]),
        mesh=mesh, in_specs=in_specs, out_specs=out_specs, check_vma=False,
    )
```

```python
import functools
import math

import jax
import jax.numpy as jnp
from jax import lax
from jax.experimental import pallas as pl
from jax.experimental.pallas import tpu as pltpu
from jax.sharding import PartitionSpec as P

masked_score = -1e30
vmem_bytes = 46 * 1024 * 1024
small_vmem_bytes = 8 * 1024 * 1024
early_steps = (2,)
f32 = jnp.float32
bf16 = jnp.bfloat16


def dot_nt(left, right):
    return lax.dot_general(left, right, (((1,), (1,)), ((), ())), preferred_element_type=f32)


def dot_nn(left, right):
    return lax.dot_general(left, right, (((1,), (0,)), ((), ())), preferred_element_type=f32)


def fold_rows(values, op):
    rows, columns = values.shape
    return op(values.reshape(rows // 8, 8, columns), axis=0)


def head_kernel(dp_size, heads_size, kv_index, kv_local, width, block_tokens, chunk, fine, sub, *refs):
    last = kv_index == kv_local - 1
    q_ref, g_ref, sk_ref, sv_ref, ck_ref, cv_ref, seg_ref = refs[:7]
    refs = refs[7:]
    held = kv_index if last else 0
    near_steps, far_steps = split_steps(heads_size)
    kept = len(near_steps)
    dq_before, refs = refs[: held * kept], refs[held * kept :]
    self_before, refs = refs[:held], refs[held:]
    (keep_ref, send_ref), refs = refs[:2], refs[2:]
    dq_outs, self_ref, refs = refs[:heads_size], refs[heads_size], refs[heads_size + 1 :]
    (
        wide_ref, keys_ref, vals_ref, keys_t_ref, s_ref, w_ref, d_ref, p_ref, ds_ref, dk_ref, dv_ref, out_ref, dq_ref,
        q_in, g_in, sk_in, sv_in, ck_in, cv_in, seg_in, sems,
    ) = refs
    head_dim = q_ref.shape[1]
    tokens = seg_ref.shape[1]
    cart_rows = ck_ref.shape[0] // kv_local
    all_keys = cart_rows + tokens
    rows = block_tokens * width
    scale = head_dim ** -0.5
    scale2 = scale * math.log2(math.e)
    span = block_tokens * kv_local * width
    blocks = tokens // block_tokens

    def block_copy(source, target, block, sem):
        at = slice(block * span, (block + 1) * span)
        return pltpu.make_async_copy(source.at[at, :], target.at[at, :], sems.at[sem])

    copies = {
        name: pltpu.make_async_copy(source, target, sems.at[at])
        for at, (name, source, target) in enumerate(
            [("ck", ck_ref, ck_in), ("sk", sk_ref, sk_in), ("cv", cv_ref, cv_in), ("sv", sv_ref, sv_in)]
        )
    }
    for block in range(blocks):
        copies["q", block] = block_copy(q_ref, q_in, block, 4 + block)
        copies["g", block] = block_copy(g_ref, g_in, block, 4 + blocks + block)
    copies["seg"] = pltpu.make_async_copy(seg_ref, seg_in, sems.at[4 + 2 * blocks])
    order = ["ck", "sk", ("q", 0), "seg", "cv", "sv", ("g", 0)]
    order += [(kind, block) for block in range(1, blocks) for kind in ("q", "g")]
    for name in order:
        copies[name].start()

    def pick(name, ref, dst, at):
        copies[name].wait()
        count = ref.shape[0] // kv_local
        if kv_local == 1:
            dst[at : at + count, :] = ref[...]
        else:
            wide_ref[0 : ref.shape[0], :] = ref[...].astype(f32)
            dst[at : at + count, :] = wide_ref[pl.ds(kv_index, count, stride=kv_local), :].astype(bf16)

    def rows_of(name, ref, block):
        copies[name, block].wait()
        wide = ref[block * span : (block + 1) * span, :]
        if kv_local == 1:
            return wide
        wide = wide.astype(f32).reshape(block_tokens, kv_local, width, head_dim)
        return wide[:, kv_index].reshape(rows, head_dim).astype(bf16)

    copies["seg"].wait()
    first_count = jnp.sum((seg_in[...] == 0).astype(f32), axis=1, keepdims=True).astype(jnp.int32)

    def limit(block):
        return -(-(block + 1) * block_tokens // fine) * fine

    def pieces(block):
        cart = [(start, chunk) for start in range(0, cart_rows, chunk)]
        return cart + [(cart_rows, limit(block))]

    queries, grads, peaks, stats = {}, {}, {}, {}
    acc = {}

    def spread(values):
        return jnp.concatenate([values] * (sub // 8), axis=0)

    def subs(start, size):
        return [slice(at, at + sub) for at in range(start, start + size, sub)]

    def open_scores(block):
        queries[block] = rows_of("q", q_in, block)
        token = (lax.broadcasted_iota(jnp.int32, (1, rows), 1) + block * rows) // width
        begin = jnp.where(token >= first_count, first_count, 0)
        acc["peak"] = jnp.full((8, rows), masked_score, f32)
        acc["token"], acc["begin"] = token, begin

    def step_scores(block, start, size):
        s_ref[block % 2, start : start + size, :] = dot_nt(keys_ref[start : start + size, :], queries[block])
        for at in subs(start, size):
            score = s_ref[block % 2, at, :]
            if start >= cart_rows:
                key_at = lax.broadcasted_iota(jnp.int32, (sub, rows), 0) + (at.start - cart_rows)
                score = jnp.where((key_at >= acc["begin"]) & (key_at <= acc["token"]), score, masked_score)
                s_ref[block % 2, at, :] = score
            acc["peak"] = jnp.maximum(acc["peak"], fold_rows(score, jnp.max))

    def close_scores(block):
        peaks[block] = jnp.broadcast_to(jnp.max(acc["peak"], axis=0, keepdims=True), (8, rows))

    def open_weights(block):
        grads[block] = rows_of("g", g_in, block)
        acc["total"] = jnp.zeros((8, rows), f32)
        acc["center"] = jnp.zeros((8, rows), f32)

    def step_weights(block, start, size):
        d_ref[block % 2, start : start + size, :] = dot_nt(vals_ref[start : start + size, :], grads[block])
        for at in subs(start, size):
            weight = jnp.exp2((s_ref[block % 2, at, :] - spread(peaks[block])) * scale2)
            w_ref[block % 2, at, :] = weight
            acc["total"] = acc["total"] + fold_rows(weight, jnp.sum)
            acc["center"] = acc["center"] + fold_rows(weight * d_ref[block % 2, at, :], jnp.sum)

    def close_weights(block):
        share = 1.0 / jnp.sum(acc["total"], axis=0, keepdims=True)
        center = jnp.sum(acc["center"], axis=0, keepdims=True) * share
        stats[block] = jnp.broadcast_to(share, (8, rows)), jnp.broadcast_to(center, (8, rows))

    def open_grads(block):
        pass

    def step_grads(block, start, size):
        slot = block % 2
        share, center = stats[block]
        for at in subs(start, size):
            prob = w_ref[slot, at, :] * spread(share)
            p_ref[slot, at, :] = prob.astype(bf16)
            ds_ref[slot, at, :] = (prob * (d_ref[slot, at, :] - spread(center))).astype(bf16)
        at = slice(start, start + size)
        old = size if start < cart_rows else (limit(block - 1) if block else 0)
        old = old if block else 0
        for ref, left, right in ((dv_ref, p_ref, grads[block]), (dk_ref, ds_ref, queries[block])):
            part = dot_nn(left[slot, at, :], right)
            if old:
                ref[start : start + old, :] += part[:old]
            if old < size:
                ref[start + old : start + size, :] = part[old:]

    def close_grads(block):
        seen = cart_rows + limit(block)
        dq_t = dot_nn(keys_t_ref[:, 0:seen], ds_ref[block % 2, 0:seen, :])
        out_ref[...] = (dq_t * scale).T
        for head in range(width):
            dq_ref[block * block_tokens : (block + 1) * block_tokens, head * head_dim : (head + 1) * head_dim] = (
                out_ref[pl.ds(head, block_tokens, stride=width), :].astype(bf16)
            )

    pick("ck", ck_in, keys_ref, 0)
    pick("sk", sk_in, keys_ref, cart_rows)
    stages = (
        (2, open_grads, step_grads, close_grads),
        (1, open_weights, step_weights, close_weights),
        (0, open_scores, step_scores, close_scores),
    )
    for turn in range(blocks + 2):
        live = [(turn - lag, *calls) for lag, *calls in stages if 0 <= turn - lag < blocks]
        if turn == 1:
            pick("cv", cv_in, vals_ref, 0)
            pick("sv", sv_in, vals_ref, cart_rows)
            keys_t_ref[...] = keys_ref[...].astype(f32).T.astype(bf16)
        for block, begin_call, _, _ in live:
            begin_call(block)
        for index in range(len(pieces(0))):
            for block, _, step_call, _ in live:
                step_call(block, *pieces(block)[index])
        for block, _, _, end_call in live:
            end_call(block)

    part_rows = cart_rows // dp_size
    me = lax.axis_index("dp")
    for step in range(dp_size):
        at = pl.ds(pl.multiple_of((me ^ step) * part_rows, part_rows), part_rows)
        ref = send_ref if step % 2 else keep_ref
        ref[step // 2, 0] = (dk_ref[at, :] * scale).astype(ref.dtype)
        ref[step // 2, 1] = dv_ref[at, :].astype(ref.dtype)
    own = dk_ref[cart_rows:all_keys, :] * scale, dv_ref[cart_rows:all_keys, :]
    own_tokens = tokens // heads_size
    columns = width * head_dim
    me = lax.axis_index("heads")
    for place, (step, ref) in enumerate(zip(near_steps + far_steps, dq_outs)):
        target = me ^ step
        at = pl.ds(pl.multiple_of(target * own_tokens, own_tokens), own_tokens)
        if last and place < kept:
            for index in range(held):
                ref[:, index * columns : (index + 1) * columns] = dq_before[index * kept + place][...]
            ref[:, held * columns :] = dq_ref[at, :]
        else:
            ref[...] = dq_ref[at, :]
    if not last:
        self_ref[0], self_ref[1] = own
        return
    count = tokens * kv_local
    for kind in range(2):
        for index, before in enumerate(self_before):
            wide_ref[pl.ds(index, tokens, stride=kv_local), :] = before[kind]
        wide_ref[pl.ds(kv_index, tokens, stride=kv_local), :] = own[kind]
        self_ref[kind * count : (kind + 1) * count, :] = wide_ref[0:count, :].astype(bf16)


def fold_kernel(part_ref, got_ref, keep_ref, send_ref):
    for index in range(part_ref.shape[0]):
        total = part_ref[index] + got_ref[index].astype(f32)
        ref = send_ref if index % 2 else keep_ref
        ref[index // 2] = total.astype(ref.dtype)


def cart_kernel(kv_local, *refs):
    part_refs, got_refs, out_ref = refs[:kv_local], refs[kv_local:-1], refs[-1]
    part_rows = part_refs[0].shape[2]
    for kv_index in range(kv_local):
        for kind in range(2):
            total = part_refs[kv_index][0, kind] + got_refs[kv_index][0, kind].astype(f32)
            out_ref[pl.ds(kind * kv_local + kv_index, part_rows, stride=2 * kv_local), :] = total


def place_kernel(heads_size, kv_local, *refs):
    part_refs, out_ref, sems = refs[:-2], refs[-2], refs[-1]
    near_steps, far_steps = split_steps(heads_size)
    columns = out_ref.shape[1] // (heads_size * kv_local)
    me = lax.axis_index("heads")
    places = [(step, 0) for step in near_steps]
    places += [(step, kv_index) for kv_index in range(kv_local) for step in far_steps]
    copies = []
    for index, ((step, kv_index), ref) in enumerate(zip(places, part_refs)):
        source = me ^ step
        at = pl.multiple_of((source * kv_local + kv_index) * columns, columns)
        copies.append(pltpu.make_async_copy(ref, out_ref.at[:, pl.ds(at, ref.shape[1])], sems.at[index]))
    for copy in copies:
        copy.start()
    for copy in copies:
        copy.wait()


def swap(values, axis, size, step):
    if step == 0:
        return values
    return lax.ppermute(values, axis, [(source, source ^ step) for source in range(size)])


def fold(part, got):
    half = part.shape[0] // 2
    return pl.pallas_call(
        fold_kernel,
        out_shape=(
            jax.ShapeDtypeStruct((half, *part.shape[1:]), f32),
            jax.ShapeDtypeStruct((half, *part.shape[1:]), bf16),
        ),
        compiler_params=pltpu.CompilerParams(vmem_limit_bytes=small_vmem_bytes),
        cost_estimate=pl.CostEstimate(flops=2**20, bytes_accessed=2**20, transcendentals=0),
        name="cart_fold",
    )(part, got)


def split_steps(heads_size):
    early = [step for step in range(heads_size) if step in early_steps]
    return [step for step in range(heads_size) if step not in early], early


def on_device(dp_size, heads_size, queries, out_grad, self_keys, self_values, cart_keys, cart_values, segment_ids):
    tokens, heads_local, head_dim = queries.shape
    kv_local = self_keys.shape[1]
    cart_rows = cart_keys.shape[0]
    width = heads_local // kv_local
    block_tokens = 64
    chunk = 512
    fine = 128
    sub = 16
    all_keys = cart_rows + tokens
    rows = block_tokens * width
    part_rows = cart_rows // dp_size
    own_tokens = tokens // heads_size
    flat = [pltpu.with_memory_space_constraint(array.reshape(-1, head_dim), pltpu.HBM) for array in (queries, out_grad, self_keys, self_values, cart_keys, cart_values)]
    segments = pltpu.with_memory_space_constraint(segment_ids, pltpu.HBM)
    macs = tokens * width * all_keys * head_dim * 5
    blocks = tokens // block_tokens
    columns = width * head_dim
    count = tokens * kv_local
    near_steps, far_steps = split_steps(heads_size)
    kept = len(near_steps)
    anywhere = pl.BlockSpec(memory_space=pl.ANY)
    cart_list, kept_list, far_list, self_list, received = [], [], [], [], []
    for kv_index in range(kv_local):
        last = kv_index == kv_local - 1
        near = jax.ShapeDtypeStruct((own_tokens, kv_local * columns if last else columns), bf16)
        far = jax.ShapeDtypeStruct((own_tokens, columns), bf16)
        own_shape = (2 * count, head_dim) if last else (2, tokens, head_dim)
        other_shapes = [near] * kept + [far] * (heads_size - kept)
        other_shapes.append(jax.ShapeDtypeStruct(own_shape, bf16 if last else f32))
        before = kept_list + self_list
        outs = pl.pallas_call(
            functools.partial(head_kernel, dp_size, heads_size, kv_index, kv_local, width, block_tokens, chunk, fine, sub),
            out_shape=(
                jax.ShapeDtypeStruct((dp_size // 2, 2, part_rows, head_dim), f32),
                jax.ShapeDtypeStruct((dp_size // 2, 2, part_rows, head_dim), bf16),
                *other_shapes,
            ),
            in_specs=[pl.BlockSpec(memory_space=pltpu.HBM)] * 7
            + [pl.BlockSpec(memory_space=pltpu.VMEM)] * (len(before) if last else 0),
            scratch_shapes=[
                pltpu.VMEM((cart_rows * kv_local, head_dim), f32),
                pltpu.VMEM((all_keys, head_dim), bf16),
                pltpu.VMEM((all_keys, head_dim), bf16),
                pltpu.VMEM((head_dim, all_keys), bf16),
                pltpu.VMEM((2, all_keys, rows), f32),
                pltpu.VMEM((2, all_keys, rows), f32),
                pltpu.VMEM((2, all_keys, rows), f32),
                pltpu.VMEM((2, all_keys, rows), bf16),
                pltpu.VMEM((2, all_keys, rows), bf16),
                pltpu.VMEM((all_keys, head_dim), f32),
                pltpu.VMEM((all_keys, head_dim), f32),
                pltpu.VMEM((rows, head_dim), f32),
                pltpu.VMEM((tokens, columns), bf16),
                *[pltpu.VMEM(array.shape, bf16) for array in flat],
                pltpu.VMEM(segment_ids.shape, jnp.int32),
                pltpu.SemaphoreType.DMA((5 + 2 * blocks,)),
            ],
            compiler_params=pltpu.CompilerParams(vmem_limit_bytes=vmem_bytes),
            cost_estimate=pl.CostEstimate(flops=4 * macs, bytes_accessed=5 * 2**20, transcendentals=tokens * width * all_keys),
            name="head_grads",
        )(*flat, segments, *(before if last else []))
        part, send, near, far = outs[0], outs[1], outs[2 : 2 + kept], outs[2 + kept : -1]
        if last:
            part, send, near, far, received = lax.optimization_barrier((part, send, near, far, received))
        else:
            kept_list += near
            self_list.append(outs[-1])
        received.append((part, swap(send, "dp", dp_size, 1)))
        far_parts = [swap(block, "heads", heads_size, step) for step, block in zip(far_steps, far)]
        if not last:
            received[-1] += tuple(far_parts)
    far_list = [block for _, _, *blocks_far in received for block in blocks_far]
    for part, got, *_ in received:
        step = 2
        while step < dp_size:
            part, send = fold(part, got)
            got = swap(send, "dp", dp_size, step)
            step *= 2
        cart_list.append((part, got))
    query_list = [swap(block, "heads", heads_size, step) for step, block in zip(near_steps, near)] + far_list + far_parts
    query_grads = pl.pallas_call(
        functools.partial(place_kernel, heads_size, kv_local),
        out_shape=jax.ShapeDtypeStruct((own_tokens, heads_size * heads_local * head_dim), bf16),
        in_specs=[anywhere] * len(query_list),
        out_specs=anywhere,
        scratch_shapes=[pltpu.SemaphoreType.DMA((len(query_list),))],
        compiler_params=pltpu.CompilerParams(vmem_limit_bytes=small_vmem_bytes),
        cost_estimate=pl.CostEstimate(flops=2**20, bytes_accessed=2 * 2**20, transcendentals=0),
        name="place_queries",
    )(*query_list)
    cart_grads = pl.pallas_call(
        functools.partial(cart_kernel, kv_local),
        out_shape=jax.ShapeDtypeStruct((part_rows * 2 * kv_local, head_dim), f32),
        compiler_params=pltpu.CompilerParams(vmem_limit_bytes=small_vmem_bytes),
        cost_estimate=pl.CostEstimate(flops=2**20, bytes_accessed=2 * 2**20, transcendentals=0),
        name="cart_grads",
    )(*[part for part, _ in cart_list], *[got for _, got in cart_list])
    cart_grads = cart_grads.reshape(part_rows, 2, kv_local, head_dim)
    self_grads = outs[-1].reshape(2, tokens, kv_local, head_dim)
    return (cart_grads, self_grads, query_grads)


def solution(mesh):
    in_specs = (
        P(("groups", "dp"), "heads", None),
        P(("groups", "dp"), "heads", None),
        P(("groups", "dp"), "heads", None),
        P(("groups", "dp"), "heads", None),
        P("groups", "heads", None),
        P("groups", "heads", None),
        P(("groups", "dp"), None),
    )
    out_specs = (
        P(("groups", "dp"), None, "heads", None),
        P(None, ("groups", "dp"), "heads", None),
        P(("groups", "dp", "heads"), None),
    )
    return jax.shard_map(
        functools.partial(on_device, mesh.shape["dp"], mesh.shape["heads"]),
        mesh=mesh, in_specs=in_specs, out_specs=out_specs, check_vma=False,
    )
```

```python
import functools
import math

import jax
import jax.numpy as jnp
from jax import lax
from jax.experimental import pallas as pl
from jax.experimental.pallas import tpu as pltpu
from jax.sharding import PartitionSpec as P

masked_score = -1e30
vmem_bytes = 46 * 1024 * 1024
small_vmem_bytes = 8 * 1024 * 1024
early_steps = (2,)
f32 = jnp.float32
bf16 = jnp.bfloat16


def dot_nt(left, right):
    return lax.dot_general(left, right, (((1,), (1,)), ((), ())), preferred_element_type=f32)


def dot_nn(left, right):
    return lax.dot_general(left, right, (((1,), (0,)), ((), ())), preferred_element_type=f32)


def fold_rows(values, op):
    rows, columns = values.shape
    return op(values.reshape(rows // 8, 8, columns), axis=0)


def head_kernel(dp_size, heads_size, kv_index, kv_local, width, block_tokens, chunk, fine, sub, *refs):
    last = kv_index == kv_local - 1
    first = kv_index == 0
    if first:
        (q_ref, g_ref, sk_ref, sv_ref, ck_ref, cv_ref, seg_ref), refs = refs[:7], refs[7:]
    else:
        (keys_ref, vals_ref, keys_t_ref, q_rows, g_rows, seg_in), refs = refs[:6], refs[6:]
    held = kv_index if last else 0
    near_steps, far_steps = split_steps(heads_size)
    kept = len(near_steps)
    dq_before, refs = refs[: held * kept], refs[held * kept :]
    self_before, refs = refs[:held], refs[held:]
    (keep_ref, send_ref), refs = refs[:2], refs[2:]
    dq_outs, self_ref, refs = refs[:heads_size], refs[heads_size], refs[heads_size + 1 :]
    if first:
        others = range(1, kv_local)
        next_refs = {other: refs[5 * other - 5 : 5 * other] for other in others}
        refs = refs[5 * len(others) :]
        if kv_local > 1:
            seg_out, refs = refs[0], refs[1:]
        (
            keys_ref, vals_ref, keys_t_ref, q_in, g_in, sk_in, sv_in, ck_in, cv_in, seg_in, sems,
        ), refs = refs[:11], refs[11:]
    wide_ref, s_ref, w_ref, d_ref, p_ref, ds_ref, dk_ref, dv_ref, out_ref, dq_ref = refs
    all_keys, head_dim = keys_ref.shape
    tokens = seg_in.shape[1]
    cart_rows = all_keys - tokens
    rows = block_tokens * width
    scale = head_dim ** -0.5
    scale2 = scale * math.log2(math.e)
    span = block_tokens * kv_local * width
    blocks = tokens // block_tokens

    if first:

        def block_copy(source, target, block, sem):
            at = slice(block * span, (block + 1) * span)
            return pltpu.make_async_copy(source.at[at, :], target.at[at, :], sems.at[sem])

        copies = {
            name: pltpu.make_async_copy(source, target, sems.at[at])
            for at, (name, source, target) in enumerate(
                [("ck", ck_ref, ck_in), ("sk", sk_ref, sk_in), ("cv", cv_ref, cv_in), ("sv", sv_ref, sv_in)]
            )
        }
        for block in range(blocks):
            copies["q", block] = block_copy(q_ref, q_in, block, 4 + block)
            copies["g", block] = block_copy(g_ref, g_in, block, 4 + blocks + block)
        copies["seg"] = pltpu.make_async_copy(seg_ref, seg_in, sems.at[4 + 2 * blocks])
        order = ["ck", "sk", ("q", 0), "seg", "cv", "sv", ("g", 0)]
        order += [(kind, block) for block in range(1, blocks) for kind in ("q", "g")]
        for name in order:
            copies[name].start()

    def pick(name, ref, dst, at):
        copies[name].wait()
        count = ref.shape[0] // kv_local
        if kv_local == 1:
            dst[at : at + count, :] = ref[...]
        else:
            wide_ref[0 : ref.shape[0], :] = ref[...].astype(f32)
            dst[at : at + count, :] = wide_ref[pl.ds(0, count, stride=kv_local), :].astype(bf16)
            for other in others:
                next_ref = next_refs[other][0 if dst is keys_ref else 1]
                next_ref[at : at + count, :] = wide_ref[pl.ds(other, count, stride=kv_local), :].astype(bf16)

    def rows_of(name, block):
        at = slice(block * rows, (block + 1) * rows)
        if not first:
            return (q_rows if name == "q" else g_rows)[at, :]
        copies[name, block].wait()
        wide = (q_in if name == "q" else g_in)[block * span : (block + 1) * span, :]
        if kv_local == 1:
            return wide
        wide = wide.astype(f32).reshape(block_tokens, kv_local, width, head_dim)
        for other in others:
            next_refs[other][3 if name == "q" else 4][at, :] = wide[:, other].reshape(rows, head_dim).astype(bf16)
        return wide[:, 0].reshape(rows, head_dim).astype(bf16)

    if first:
        copies["seg"].wait()
        if kv_local > 1:
            seg_out[...] = seg_in[...]
    first_count = jnp.sum((seg_in[...] == 0).astype(f32), axis=1, keepdims=True).astype(jnp.int32)

    def limit(block):
        return -(-(block + 1) * block_tokens // fine) * fine

    def pieces(block):
        cart = [(start, chunk) for start in range(0, cart_rows, chunk)]
        return cart + [(cart_rows, limit(block))]

    queries, grads, peaks, stats = {}, {}, {}, {}
    acc = {}

    def spread(values):
        return jnp.concatenate([values] * (sub // 8), axis=0)

    def subs(start, size):
        return [slice(at, at + sub) for at in range(start, start + size, sub)]

    def open_scores(block):
        queries[block] = rows_of("q", block)
        token = (lax.broadcasted_iota(jnp.int32, (1, rows), 1) + block * rows) // width
        begin = jnp.where(token >= first_count, first_count, 0)
        acc["peak"] = jnp.full((8, rows), masked_score, f32)
        acc["token"], acc["begin"] = token, begin

    def step_scores(block, start, size):
        s_ref[block % 2, start : start + size, :] = dot_nt(keys_ref[start : start + size, :], queries[block])
        for at in subs(start, size):
            score = s_ref[block % 2, at, :]
            if start >= cart_rows:
                key_at = lax.broadcasted_iota(jnp.int32, (sub, rows), 0) + (at.start - cart_rows)
                score = jnp.where((key_at >= acc["begin"]) & (key_at <= acc["token"]), score, masked_score)
                s_ref[block % 2, at, :] = score
            acc["peak"] = jnp.maximum(acc["peak"], fold_rows(score, jnp.max))

    def close_scores(block):
        peaks[block] = jnp.broadcast_to(jnp.max(acc["peak"], axis=0, keepdims=True), (8, rows))

    def open_weights(block):
        grads[block] = rows_of("g", block)
        acc["total"] = jnp.zeros((8, rows), f32)
        acc["center"] = jnp.zeros((8, rows), f32)

    def step_weights(block, start, size):
        d_ref[block % 2, start : start + size, :] = dot_nt(vals_ref[start : start + size, :], grads[block])
        for at in subs(start, size):
            weight = jnp.exp2((s_ref[block % 2, at, :] - spread(peaks[block])) * scale2)
            w_ref[block % 2, at, :] = weight
            acc["total"] = acc["total"] + fold_rows(weight, jnp.sum)
            acc["center"] = acc["center"] + fold_rows(weight * d_ref[block % 2, at, :], jnp.sum)

    def close_weights(block):
        share = 1.0 / jnp.sum(acc["total"], axis=0, keepdims=True)
        center = jnp.sum(acc["center"], axis=0, keepdims=True) * share
        stats[block] = jnp.broadcast_to(share, (8, rows)), jnp.broadcast_to(center, (8, rows))

    def open_grads(block):
        pass

    def step_grads(block, start, size):
        slot = block % 2
        share, center = stats[block]
        for at in subs(start, size):
            prob = w_ref[slot, at, :] * spread(share)
            p_ref[slot, at, :] = prob.astype(bf16)
            ds_ref[slot, at, :] = (prob * (d_ref[slot, at, :] - spread(center))).astype(bf16)
        at = slice(start, start + size)
        old = size if start < cart_rows else (limit(block - 1) if block else 0)
        old = old if block else 0
        for ref, left, right in ((dv_ref, p_ref, grads[block]), (dk_ref, ds_ref, queries[block])):
            part = dot_nn(left[slot, at, :], right)
            if old:
                ref[start : start + old, :] += part[:old]
            if old < size:
                ref[start + old : start + size, :] = part[old:]

    def close_grads(block):
        seen = cart_rows + limit(block)
        dq_t = dot_nn(keys_t_ref[:, 0:seen], ds_ref[block % 2, 0:seen, :])
        out_ref[...] = (dq_t * scale).T
        for head in range(width):
            dq_ref[block * block_tokens : (block + 1) * block_tokens, head * head_dim : (head + 1) * head_dim] = (
                out_ref[pl.ds(head, block_tokens, stride=width), :].astype(bf16)
            )

    if first:
        pick("ck", ck_in, keys_ref, 0)
        pick("sk", sk_in, keys_ref, cart_rows)
    stages = (
        (2, open_grads, step_grads, close_grads),
        (1, open_weights, step_weights, close_weights),
        (0, open_scores, step_scores, close_scores),
    )
    for turn in range(blocks + 2):
        live = [(turn - lag, *calls) for lag, *calls in stages if 0 <= turn - lag < blocks]
        if turn == 1 and first:
            pick("cv", cv_in, vals_ref, 0)
            pick("sv", sv_in, vals_ref, cart_rows)
            keys_t_ref[...] = keys_ref[...].astype(f32).T.astype(bf16)
            for other in others:
                next_refs[other][2][...] = next_refs[other][0][...].astype(f32).T.astype(bf16)
        for block, begin_call, _, _ in live:
            begin_call(block)
        for index in range(len(pieces(0))):
            for block, _, step_call, _ in live:
                step_call(block, *pieces(block)[index])
        for block, _, _, end_call in live:
            end_call(block)

    part_rows = cart_rows // dp_size
    me = lax.axis_index("dp")
    for step in range(dp_size):
        at = pl.ds(pl.multiple_of((me ^ step) * part_rows, part_rows), part_rows)
        ref = send_ref if step % 2 else keep_ref
        ref[step // 2, 0] = (dk_ref[at, :] * scale).astype(ref.dtype)
        ref[step // 2, 1] = dv_ref[at, :].astype(ref.dtype)
    own = dk_ref[cart_rows:all_keys, :] * scale, dv_ref[cart_rows:all_keys, :]
    own_tokens = tokens // heads_size
    columns = width * head_dim
    me = lax.axis_index("heads")
    for place, (step, ref) in enumerate(zip(near_steps + far_steps, dq_outs)):
        target = me ^ step
        at = pl.ds(pl.multiple_of(target * own_tokens, own_tokens), own_tokens)
        if last and place < kept:
            for index in range(held):
                ref[:, index * columns : (index + 1) * columns] = dq_before[index * kept + place][...]
            ref[:, held * columns :] = dq_ref[at, :]
        else:
            ref[...] = dq_ref[at, :]
    if not last:
        self_ref[0], self_ref[1] = own
        return
    count = tokens * kv_local
    for kind in range(2):
        for index, before in enumerate(self_before):
            wide_ref[pl.ds(index, tokens, stride=kv_local), :] = before[kind]
        wide_ref[pl.ds(kv_index, tokens, stride=kv_local), :] = own[kind]
        self_ref[kind * count : (kind + 1) * count, :] = wide_ref[0:count, :].astype(bf16)


def fold_kernel(part_ref, got_ref, keep_ref, send_ref):
    for index in range(part_ref.shape[0]):
        total = part_ref[index] + got_ref[index].astype(f32)
        ref = send_ref if index % 2 else keep_ref
        ref[index // 2] = total.astype(ref.dtype)


def cart_kernel(kv_local, *refs):
    part_refs, got_refs, out_ref = refs[:kv_local], refs[kv_local:-1], refs[-1]
    part_rows = part_refs[0].shape[2]
    for kv_index in range(kv_local):
        for kind in range(2):
            total = part_refs[kv_index][0, kind] + got_refs[kv_index][0, kind].astype(f32)
            out_ref[pl.ds(kind * kv_local + kv_index, part_rows, stride=2 * kv_local), :] = total


def place_kernel(heads_size, kv_local, *refs):
    part_refs, out_ref, sems = refs[:-2], refs[-2], refs[-1]
    near_steps, far_steps = split_steps(heads_size)
    columns = out_ref.shape[1] // (heads_size * kv_local)
    me = lax.axis_index("heads")
    places = [(step, 0) for step in near_steps]
    places += [(step, kv_index) for kv_index in range(kv_local) for step in far_steps]
    copies = []
    for index, ((step, kv_index), ref) in enumerate(zip(places, part_refs)):
        source = me ^ step
        at = pl.multiple_of((source * kv_local + kv_index) * columns, columns)
        copies.append(pltpu.make_async_copy(ref, out_ref.at[:, pl.ds(at, ref.shape[1])], sems.at[index]))
    for copy in copies:
        copy.start()
    for copy in copies:
        copy.wait()


def swap(values, axis, size, step):
    if step == 0:
        return values
    return lax.ppermute(values, axis, [(source, source ^ step) for source in range(size)])


def fold(part, got):
    half = part.shape[0] // 2
    return pl.pallas_call(
        fold_kernel,
        out_shape=(
            jax.ShapeDtypeStruct((half, *part.shape[1:]), f32),
            jax.ShapeDtypeStruct((half, *part.shape[1:]), bf16),
        ),
        compiler_params=pltpu.CompilerParams(vmem_limit_bytes=small_vmem_bytes),
        cost_estimate=pl.CostEstimate(flops=2**20, bytes_accessed=2**20, transcendentals=0),
        name="cart_fold",
    )(part, got)


def split_steps(heads_size):
    early = [step for step in range(heads_size) if step in early_steps]
    return [step for step in range(heads_size) if step not in early], early


def on_device(dp_size, heads_size, queries, out_grad, self_keys, self_values, cart_keys, cart_values, segment_ids):
    tokens, heads_local, head_dim = queries.shape
    kv_local = self_keys.shape[1]
    cart_rows = cart_keys.shape[0]
    width = heads_local // kv_local
    block_tokens = 64
    chunk = 512
    fine = 128
    sub = 16
    all_keys = cart_rows + tokens
    rows = block_tokens * width
    part_rows = cart_rows // dp_size
    own_tokens = tokens // heads_size
    flat = [pltpu.with_memory_space_constraint(array.reshape(-1, head_dim), pltpu.HBM) for array in (queries, out_grad, self_keys, self_values, cart_keys, cart_values)]
    segments = pltpu.with_memory_space_constraint(segment_ids, pltpu.HBM)
    macs = tokens * width * all_keys * head_dim * 5
    blocks = tokens // block_tokens
    columns = width * head_dim
    count = tokens * kv_local
    near_steps, far_steps = split_steps(heads_size)
    kept = len(near_steps)
    anywhere = pl.BlockSpec(memory_space=pl.ANY)
    cart_list, kept_list, far_list, self_list, received = [], [], [], [], []
    for kv_index in range(kv_local):
        last = kv_index == kv_local - 1
        near = jax.ShapeDtypeStruct((own_tokens, kv_local * columns if last else columns), bf16)
        far = jax.ShapeDtypeStruct((own_tokens, columns), bf16)
        own_shape = (2 * count, head_dim) if last else (2, tokens, head_dim)
        other_shapes = [near] * kept + [far] * (heads_size - kept)
        other_shapes.append(jax.ShapeDtypeStruct(own_shape, bf16 if last else f32))
        next_shapes, first_scratch = [], []
        if kv_index == 0:
            key_like = jax.ShapeDtypeStruct((all_keys, head_dim), bf16)
            turned = jax.ShapeDtypeStruct((head_dim, all_keys), bf16)
            row_like = jax.ShapeDtypeStruct((tokens * width, head_dim), bf16)
            next_shapes = [key_like, key_like, turned, row_like, row_like] * (kv_local - 1)
            if kv_local > 1:
                next_shapes.append(jax.ShapeDtypeStruct(segment_ids.shape, jnp.int32))
            inputs = [*flat, segments]
            first_scratch = [
                pltpu.VMEM((all_keys, head_dim), bf16),
                pltpu.VMEM((all_keys, head_dim), bf16),
                pltpu.VMEM((head_dim, all_keys), bf16),
                *[pltpu.VMEM(array.shape, bf16) for array in flat],
                pltpu.VMEM(segment_ids.shape, jnp.int32),
                pltpu.SemaphoreType.DMA((5 + 2 * blocks,)),
            ]
        else:
            inputs = [*prepared[5 * kv_index - 5 : 5 * kv_index], prepared[-1]]
        before = kept_list + self_list if last else []
        outs = pl.pallas_call(
            functools.partial(head_kernel, dp_size, heads_size, kv_index, kv_local, width, block_tokens, chunk, fine, sub),
            out_shape=(
                jax.ShapeDtypeStruct((dp_size // 2, 2, part_rows, head_dim), f32),
                jax.ShapeDtypeStruct((dp_size // 2, 2, part_rows, head_dim), bf16),
                *other_shapes,
                *next_shapes,
            ),
            in_specs=[pl.BlockSpec(memory_space=pltpu.VMEM if kv_index else pltpu.HBM)] * len(inputs)
            + [pl.BlockSpec(memory_space=pltpu.VMEM)] * len(before),
            scratch_shapes=[
                *first_scratch,
                pltpu.VMEM((cart_rows * kv_local, head_dim), f32),
                pltpu.VMEM((2, all_keys, rows), f32),
                pltpu.VMEM((2, all_keys, rows), f32),
                pltpu.VMEM((2, all_keys, rows), f32),
                pltpu.VMEM((2, all_keys, rows), bf16),
                pltpu.VMEM((2, all_keys, rows), bf16),
                pltpu.VMEM((all_keys, head_dim), f32),
                pltpu.VMEM((all_keys, head_dim), f32),
                pltpu.VMEM((rows, head_dim), f32),
                pltpu.VMEM((tokens, columns), bf16),
            ],
            compiler_params=pltpu.CompilerParams(vmem_limit_bytes=vmem_bytes),
            cost_estimate=pl.CostEstimate(flops=4 * macs, bytes_accessed=5 * 2**20, transcendentals=tokens * width * all_keys),
            name="head_grads",
        )(*inputs, *before)
        if kv_index == 0:
            prepared = outs[len(outs) - len(next_shapes) :]
        outs = outs[: len(outs) - len(next_shapes)]
        part, send, near, far = outs[0], outs[1], outs[2 : 2 + kept], outs[2 + kept : -1]
        if last:
            part, send, near, far, received = lax.optimization_barrier((part, send, near, far, received))
        else:
            kept_list += near
            self_list.append(outs[-1])
        received.append((part, swap(send, "dp", dp_size, 1)))
        far_parts = [swap(block, "heads", heads_size, step) for step, block in zip(far_steps, far)]
        if not last:
            received[-1] += tuple(far_parts)
    far_list = [block for _, _, *blocks_far in received for block in blocks_far]
    for part, got, *_ in received:
        step = 2
        while step < dp_size:
            part, send = fold(part, got)
            got = swap(send, "dp", dp_size, step)
            step *= 2
        cart_list.append((part, got))
    query_list = [swap(block, "heads", heads_size, step) for step, block in zip(near_steps, near)] + far_list + far_parts
    query_grads = pl.pallas_call(
        functools.partial(place_kernel, heads_size, kv_local),
        out_shape=jax.ShapeDtypeStruct((own_tokens, heads_size * heads_local * head_dim), bf16),
        in_specs=[anywhere] * len(query_list),
        out_specs=anywhere,
        scratch_shapes=[pltpu.SemaphoreType.DMA((len(query_list),))],
        compiler_params=pltpu.CompilerParams(vmem_limit_bytes=small_vmem_bytes),
        cost_estimate=pl.CostEstimate(flops=2**20, bytes_accessed=2 * 2**20, transcendentals=0),
        name="place_queries",
    )(*query_list)
    cart_grads = pl.pallas_call(
        functools.partial(cart_kernel, kv_local),
        out_shape=jax.ShapeDtypeStruct((part_rows * 2 * kv_local, head_dim), f32),
        compiler_params=pltpu.CompilerParams(vmem_limit_bytes=small_vmem_bytes),
        cost_estimate=pl.CostEstimate(flops=2**20, bytes_accessed=2 * 2**20, transcendentals=0),
        name="cart_grads",
    )(*[part for part, _ in cart_list], *[got for _, got in cart_list])
    cart_grads = cart_grads.reshape(part_rows, 2, kv_local, head_dim)
    self_grads = outs[-1].reshape(2, tokens, kv_local, head_dim)
    return (cart_grads, self_grads, query_grads)


def solution(mesh):
    in_specs = (
        P(("groups", "dp"), "heads", None),
        P(("groups", "dp"), "heads", None),
        P(("groups", "dp"), "heads", None),
        P(("groups", "dp"), "heads", None),
        P("groups", "heads", None),
        P("groups", "heads", None),
        P(("groups", "dp"), None),
    )
    out_specs = (
        P(("groups", "dp"), None, "heads", None),
        P(None, ("groups", "dp"), "heads", None),
        P(("groups", "dp", "heads"), None),
    )
    return jax.shard_map(
        functools.partial(on_device, mesh.shape["dp"], mesh.shape["heads"]),
        mesh=mesh, in_specs=in_specs, out_specs=out_specs, check_vma=False,
    )
```

```python
import functools
import math

import jax
import jax.numpy as jnp
from jax import lax
from jax.experimental import pallas as pl
from jax.experimental.pallas import tpu as pltpu
from jax.sharding import PartitionSpec as P

masked_score = -1e30
vmem_bytes = 46 * 1024 * 1024
small_vmem_bytes = 8 * 1024 * 1024
early_steps = ()
f32 = jnp.float32
bf16 = jnp.bfloat16


def dot_nt(left, right):
    return lax.dot_general(left, right, (((1,), (1,)), ((), ())), preferred_element_type=f32)


def dot_nn(left, right):
    return lax.dot_general(left, right, (((1,), (0,)), ((), ())), preferred_element_type=f32)


def fold_rows(values, op):
    rows, columns = values.shape
    return op(values.reshape(rows // 8, 8, columns), axis=0)


def head_kernel(dp_size, heads_size, kv_index, kv_local, width, block_tokens, chunk, fine, sub, *refs):
    last = kv_index == kv_local - 1
    first = kv_index == 0
    if first:
        (q_ref, g_ref, sk_ref, sv_ref, ck_ref, cv_ref, seg_ref), refs = refs[:7], refs[7:]
    else:
        (keys_ref, vals_ref, keys_t_ref, q_rows, g_rows, seg_in), refs = refs[:6], refs[6:]
    held = kv_index if last else 0
    near_steps, far_steps = split_steps(heads_size)
    kept = len(near_steps)
    dq_before, refs = refs[: held * kept], refs[held * kept :]
    self_before, refs = refs[:held], refs[held:]
    (keep_ref, send_ref), refs = refs[:2], refs[2:]
    dq_outs, self_ref, refs = refs[:heads_size], refs[heads_size], refs[heads_size + 1 :]
    if first:
        others = range(1, kv_local)
        next_refs = {other: refs[5 * other - 5 : 5 * other] for other in others}
        refs = refs[5 * len(others) :]
        if kv_local > 1:
            seg_out, refs = refs[0], refs[1:]
        (
            keys_ref, vals_ref, keys_t_ref, q_in, g_in, sk_in, sv_in, ck_in, cv_in, seg_in, sems,
        ), refs = refs[:11], refs[11:]
    wide_ref, s_ref, w_ref, d_ref, p_ref, ds_ref, dk_ref, dv_ref, out_ref, dq_ref = refs
    all_keys, head_dim = keys_ref.shape
    tokens = seg_in.shape[1]
    cart_rows = all_keys - tokens
    rows = block_tokens * width
    scale = head_dim ** -0.5
    scale2 = scale * math.log2(math.e)
    span = block_tokens * kv_local * width
    blocks = tokens // block_tokens

    if first:

        def block_copy(source, target, block, sem):
            at = slice(block * span, (block + 1) * span)
            return pltpu.make_async_copy(source.at[at, :], target.at[at, :], sems.at[sem])

        copies = {
            name: pltpu.make_async_copy(source, target, sems.at[at])
            for at, (name, source, target) in enumerate(
                [("ck", ck_ref, ck_in), ("sk", sk_ref, sk_in), ("cv", cv_ref, cv_in), ("sv", sv_ref, sv_in)]
            )
        }
        for block in range(blocks):
            copies["q", block] = block_copy(q_ref, q_in, block, 4 + block)
            copies["g", block] = block_copy(g_ref, g_in, block, 4 + blocks + block)
        copies["seg"] = pltpu.make_async_copy(seg_ref, seg_in, sems.at[4 + 2 * blocks])
        order = ["ck", "sk", ("q", 0), "seg", "cv", "sv", ("g", 0)]
        order += [(kind, block) for block in range(1, blocks) for kind in ("q", "g")]
        for name in order:
            copies[name].start()

    def pick(name, ref, dst, at):
        copies[name].wait()
        count = ref.shape[0] // kv_local
        if kv_local == 1:
            dst[at : at + count, :] = ref[...]
        else:
            wide_ref[0 : ref.shape[0], :] = ref[...].astype(f32)
            dst[at : at + count, :] = wide_ref[pl.ds(0, count, stride=kv_local), :].astype(bf16)
            for other in others:
                next_ref = next_refs[other][0 if dst is keys_ref else 1]
                next_ref[at : at + count, :] = wide_ref[pl.ds(other, count, stride=kv_local), :].astype(bf16)

    def rows_of(name, block):
        at = slice(block * rows, (block + 1) * rows)
        if not first:
            return (q_rows if name == "q" else g_rows)[at, :]
        copies[name, block].wait()
        wide = (q_in if name == "q" else g_in)[block * span : (block + 1) * span, :]
        if kv_local == 1:
            return wide
        wide = wide.astype(f32).reshape(block_tokens, kv_local, width, head_dim)
        for other in others:
            next_refs[other][3 if name == "q" else 4][at, :] = wide[:, other].reshape(rows, head_dim).astype(bf16)
        return wide[:, 0].reshape(rows, head_dim).astype(bf16)

    if first:
        copies["seg"].wait()
        if kv_local > 1:
            seg_out[...] = seg_in[...]
    first_count = jnp.sum((seg_in[...] == 0).astype(f32), axis=1, keepdims=True).astype(jnp.int32)

    def limit(block):
        return -(-(block + 1) * block_tokens // fine) * fine

    def pieces(block):
        cart = [(start, chunk) for start in range(0, cart_rows, chunk)]
        return cart + [(cart_rows, limit(block))]

    queries, grads, peaks, stats = {}, {}, {}, {}
    acc = {}

    def spread(values):
        return jnp.concatenate([values] * (sub // 8), axis=0)

    def subs(start, size):
        return [slice(at, at + sub) for at in range(start, start + size, sub)]

    def open_scores(block):
        queries[block] = rows_of("q", block)
        token = (lax.broadcasted_iota(jnp.int32, (1, rows), 1) + block * rows) // width
        begin = jnp.where(token >= first_count, first_count, 0)
        acc["peak"] = jnp.full((8, rows), masked_score, f32)
        acc["token"], acc["begin"] = token, begin

    def step_scores(block, start, size):
        s_ref[block % 2, start : start + size, :] = dot_nt(keys_ref[start : start + size, :], queries[block])
        for at in subs(start, size):
            score = s_ref[block % 2, at, :]
            if start >= cart_rows:
                key_at = lax.broadcasted_iota(jnp.int32, (sub, rows), 0) + (at.start - cart_rows)
                score = jnp.where((key_at >= acc["begin"]) & (key_at <= acc["token"]), score, masked_score)
                s_ref[block % 2, at, :] = score
            acc["peak"] = jnp.maximum(acc["peak"], fold_rows(score, jnp.max))

    def close_scores(block):
        peaks[block] = jnp.broadcast_to(jnp.max(acc["peak"], axis=0, keepdims=True), (8, rows))

    def open_weights(block):
        grads[block] = rows_of("g", block)
        acc["total"] = jnp.zeros((8, rows), f32)
        acc["center"] = jnp.zeros((8, rows), f32)

    def step_weights(block, start, size):
        d_ref[block % 2, start : start + size, :] = dot_nt(vals_ref[start : start + size, :], grads[block])
        for at in subs(start, size):
            weight = jnp.exp2((s_ref[block % 2, at, :] - spread(peaks[block])) * scale2)
            w_ref[block % 2, at, :] = weight
            acc["total"] = acc["total"] + fold_rows(weight, jnp.sum)
            acc["center"] = acc["center"] + fold_rows(weight * d_ref[block % 2, at, :], jnp.sum)

    def close_weights(block):
        share = 1.0 / jnp.sum(acc["total"], axis=0, keepdims=True)
        center = jnp.sum(acc["center"], axis=0, keepdims=True) * share
        stats[block] = jnp.broadcast_to(share, (8, rows)), jnp.broadcast_to(center, (8, rows))

    def open_grads(block):
        pass

    def step_grads(block, start, size):
        slot = block % 2
        share, center = stats[block]
        for at in subs(start, size):
            prob = w_ref[slot, at, :] * spread(share)
            p_ref[slot, at, :] = prob.astype(bf16)
            ds_ref[slot, at, :] = (prob * (d_ref[slot, at, :] - spread(center))).astype(bf16)
        at = slice(start, start + size)
        old = size if start < cart_rows else (limit(block - 1) if block else 0)
        old = old if block else 0
        for ref, left, right in ((dv_ref, p_ref, grads[block]), (dk_ref, ds_ref, queries[block])):
            part = dot_nn(left[slot, at, :], right)
            if old:
                ref[start : start + old, :] += part[:old]
            if old < size:
                ref[start + old : start + size, :] = part[old:]

    def close_grads(block):
        seen = cart_rows + limit(block)
        dq_t = dot_nn(keys_t_ref[:, 0:seen], ds_ref[block % 2, 0:seen, :])
        out_ref[...] = (dq_t * scale).T
        for head in range(width):
            dq_ref[block * block_tokens : (block + 1) * block_tokens, head * head_dim : (head + 1) * head_dim] = (
                out_ref[pl.ds(head, block_tokens, stride=width), :].astype(bf16)
            )

    if first:
        pick("ck", ck_in, keys_ref, 0)
        pick("sk", sk_in, keys_ref, cart_rows)
    stages = (
        (2, open_grads, step_grads, close_grads),
        (1, open_weights, step_weights, close_weights),
        (0, open_scores, step_scores, close_scores),
    )
    for turn in range(blocks + 2):
        live = [(turn - lag, *calls) for lag, *calls in stages if 0 <= turn - lag < blocks]
        if turn == 1 and first:
            pick("cv", cv_in, vals_ref, 0)
            pick("sv", sv_in, vals_ref, cart_rows)
            keys_t_ref[...] = keys_ref[...].astype(f32).T.astype(bf16)
            for other in others:
                next_refs[other][2][...] = next_refs[other][0][...].astype(f32).T.astype(bf16)
        for block, begin_call, _, _ in live:
            begin_call(block)
        for index in range(len(pieces(0))):
            for block, _, step_call, _ in live:
                step_call(block, *pieces(block)[index])
        for block, _, _, end_call in live:
            end_call(block)

    part_rows = cart_rows // dp_size
    me = lax.axis_index("dp")
    half = dp_size // 2
    for index, share in enumerate(share_order(dp_size, last)):
        at = pl.ds(pl.multiple_of((me ^ share) * part_rows, part_rows), part_rows)
        ref = send_ref if index >= half else keep_ref
        ref[index % half, 0] = (dk_ref[at, :] * scale).astype(ref.dtype)
        ref[index % half, 1] = dv_ref[at, :].astype(ref.dtype)
    own = dk_ref[cart_rows:all_keys, :] * scale, dv_ref[cart_rows:all_keys, :]
    own_tokens = tokens // heads_size
    columns = width * head_dim
    me = lax.axis_index("heads")
    for place, (step, ref) in enumerate(zip(near_steps + far_steps, dq_outs)):
        target = me ^ step
        at = pl.ds(pl.multiple_of(target * own_tokens, own_tokens), own_tokens)
        if last and place < kept:
            for index in range(held):
                ref[:, index * columns : (index + 1) * columns] = dq_before[index * kept + place][...]
            ref[:, held * columns :] = dq_ref[at, :]
        else:
            ref[...] = dq_ref[at, :]
    if not last:
        self_ref[0], self_ref[1] = own
        return
    count = tokens * kv_local
    for kind in range(2):
        for index, before in enumerate(self_before):
            wide_ref[pl.ds(index, tokens, stride=kv_local), :] = before[kind]
        wide_ref[pl.ds(kv_index, tokens, stride=kv_local), :] = own[kind]
        self_ref[kind * count : (kind + 1) * count, :] = wide_ref[0:count, :].astype(bf16)


def fold_kernel(part_ref, got_ref, keep_ref, send_ref):
    half = keep_ref.shape[0]
    for index in range(2 * half):
        total = part_ref[index] + got_ref[index].astype(f32)
        ref = send_ref if index >= half else keep_ref
        ref[index % half] = total.astype(ref.dtype)


def cart_kernel(kv_local, *refs):
    part_refs, got_refs, out_ref = refs[:kv_local], refs[kv_local:-1], refs[-1]
    part_rows = part_refs[0].shape[2]
    for kv_index in range(kv_local):
        for kind in range(2):
            total = part_refs[kv_index][0, kind] + got_refs[kv_index][0, kind].astype(f32)
            out_ref[pl.ds(kind * kv_local + kv_index, part_rows, stride=2 * kv_local), :] = total


def place_kernel(heads_size, kv_local, *refs):
    part_refs, out_ref, sems = refs[:-2], refs[-2], refs[-1]
    near_steps, far_steps = split_steps(heads_size)
    columns = out_ref.shape[1] // (heads_size * kv_local)
    me = lax.axis_index("heads")
    places = [(step, 0) for step in near_steps]
    places += [(step, kv_index) for kv_index in range(kv_local) for step in far_steps]
    copies = []
    for index, ((step, kv_index), ref) in enumerate(zip(places, part_refs)):
        source = me ^ step
        at = pl.multiple_of((source * kv_local + kv_index) * columns, columns)
        copies.append(pltpu.make_async_copy(ref, out_ref.at[:, pl.ds(at, ref.shape[1])], sems.at[index]))
    for copy in copies:
        copy.start()
    for copy in copies:
        copy.wait()


def swap(values, axis, size, step):
    if step == 0:
        return values
    return lax.ppermute(values, axis, [(source, source ^ step) for source in range(size)])


def fold(part, got):
    half = part.shape[0] // 2
    return pl.pallas_call(
        fold_kernel,
        out_shape=(
            jax.ShapeDtypeStruct((half, *part.shape[1:]), f32),
            jax.ShapeDtypeStruct((half, *part.shape[1:]), bf16),
        ),
        compiler_params=pltpu.CompilerParams(vmem_limit_bytes=small_vmem_bytes),
        cost_estimate=pl.CostEstimate(flops=2**20, bytes_accessed=2**20, transcendentals=0),
        name="cart_fold",
    )(part, got)


def split_steps(heads_size):
    early = [step for step in range(heads_size) if step in early_steps]
    late = [0, *range(2, heads_size), 1]
    return [step for step in late if step < heads_size and step not in early], early


def swap_order(dp_size, last):
    bits = [1 << bit for bit in range(dp_size.bit_length() - 1)]
    return bits if last else bits[::-1]


def share_order(dp_size, last):
    shares = [0]
    for bit in reversed(swap_order(dp_size, last)):
        shares = shares + [share ^ bit for share in shares]
    return shares


def on_device(dp_size, heads_size, queries, out_grad, self_keys, self_values, cart_keys, cart_values, segment_ids):
    tokens, heads_local, head_dim = queries.shape
    kv_local = self_keys.shape[1]
    cart_rows = cart_keys.shape[0]
    width = heads_local // kv_local
    block_tokens = 64
    chunk = 512
    fine = 128
    sub = 16
    all_keys = cart_rows + tokens
    rows = block_tokens * width
    part_rows = cart_rows // dp_size
    own_tokens = tokens // heads_size
    flat = [pltpu.with_memory_space_constraint(array.reshape(-1, head_dim), pltpu.HBM) for array in (queries, out_grad, self_keys, self_values, cart_keys, cart_values)]
    segments = pltpu.with_memory_space_constraint(segment_ids, pltpu.HBM)
    macs = tokens * width * all_keys * head_dim * 5
    blocks = tokens // block_tokens
    columns = width * head_dim
    count = tokens * kv_local
    near_steps, far_steps = split_steps(heads_size)
    kept = len(near_steps)
    anywhere = pl.BlockSpec(memory_space=pl.ANY)
    cart_list, kept_list, far_list, self_list, received = [], [], [], [], []
    for kv_index in range(kv_local):
        last = kv_index == kv_local - 1
        near = jax.ShapeDtypeStruct((own_tokens, kv_local * columns if last else columns), bf16)
        far = jax.ShapeDtypeStruct((own_tokens, columns), bf16)
        own_shape = (2 * count, head_dim) if last else (2, tokens, head_dim)
        other_shapes = [near] * kept + [far] * (heads_size - kept)
        other_shapes.append(jax.ShapeDtypeStruct(own_shape, bf16 if last else f32))
        next_shapes, first_scratch = [], []
        if kv_index == 0:
            key_like = jax.ShapeDtypeStruct((all_keys, head_dim), bf16)
            turned = jax.ShapeDtypeStruct((head_dim, all_keys), bf16)
            row_like = jax.ShapeDtypeStruct((tokens * width, head_dim), bf16)
            next_shapes = [key_like, key_like, turned, row_like, row_like] * (kv_local - 1)
            if kv_local > 1:
                next_shapes.append(jax.ShapeDtypeStruct(segment_ids.shape, jnp.int32))
            inputs = [*flat, segments]
            first_scratch = [
                pltpu.VMEM((all_keys, head_dim), bf16),
                pltpu.VMEM((all_keys, head_dim), bf16),
                pltpu.VMEM((head_dim, all_keys), bf16),
                *[pltpu.VMEM(array.shape, bf16) for array in flat],
                pltpu.VMEM(segment_ids.shape, jnp.int32),
                pltpu.SemaphoreType.DMA((5 + 2 * blocks,)),
            ]
        else:
            inputs = [*prepared[5 * kv_index - 5 : 5 * kv_index], prepared[-1]]
        before = kept_list + self_list if last else []
        outs = pl.pallas_call(
            functools.partial(head_kernel, dp_size, heads_size, kv_index, kv_local, width, block_tokens, chunk, fine, sub),
            out_shape=(
                jax.ShapeDtypeStruct((dp_size // 2, 2, part_rows, head_dim), f32),
                jax.ShapeDtypeStruct((dp_size // 2, 2, part_rows, head_dim), bf16),
                *other_shapes,
                *next_shapes,
            ),
            in_specs=[pl.BlockSpec(memory_space=pltpu.VMEM if kv_index else pltpu.HBM)] * len(inputs)
            + [pl.BlockSpec(memory_space=pltpu.VMEM)] * len(before),
            scratch_shapes=[
                *first_scratch,
                pltpu.VMEM((cart_rows * kv_local, head_dim), f32),
                pltpu.VMEM((2, all_keys, rows), f32),
                pltpu.VMEM((2, all_keys, rows), f32),
                pltpu.VMEM((2, all_keys, rows), f32),
                pltpu.VMEM((2, all_keys, rows), bf16),
                pltpu.VMEM((2, all_keys, rows), bf16),
                pltpu.VMEM((all_keys, head_dim), f32),
                pltpu.VMEM((all_keys, head_dim), f32),
                pltpu.VMEM((rows, head_dim), f32),
                pltpu.VMEM((tokens, columns), bf16),
            ],
            compiler_params=pltpu.CompilerParams(vmem_limit_bytes=vmem_bytes),
            cost_estimate=pl.CostEstimate(flops=4 * macs, bytes_accessed=5 * 2**20, transcendentals=tokens * width * all_keys),
            name="head_grads",
        )(*inputs, *before)
        if kv_index == 0:
            prepared = outs[len(outs) - len(next_shapes) :]
        outs = outs[: len(outs) - len(next_shapes)]
        part, send, near, far = outs[0], outs[1], outs[2 : 2 + kept], outs[2 + kept : -1]
        if last:
            held_back, received = lax.optimization_barrier((near[-1], received))
            near = [*near[:-1], held_back]
        else:
            kept_list += near
            self_list.append(outs[-1])
        received.append((part, swap(send, "dp", dp_size, swap_order(dp_size, last)[0])))
        far_parts = [swap(block, "heads", heads_size, step) for step, block in zip(far_steps, far)]
        if not last:
            received[-1] += tuple(far_parts)
    far_list = [block for _, _, *blocks_far in received for block in blocks_far]
    cart_list = []
    for index, (part, got, *_) in enumerate(received):
        for step in swap_order(dp_size, index == kv_local - 1)[1:]:
            part, send = fold(part, got)
            got = swap(send, "dp", dp_size, step)
        cart_list.append((part, got))
    query_list = [swap(block, "heads", heads_size, step) for step, block in zip(near_steps, near)] + far_list + far_parts
    query_grads = pl.pallas_call(
        functools.partial(place_kernel, heads_size, kv_local),
        out_shape=jax.ShapeDtypeStruct((own_tokens, heads_size * heads_local * head_dim), bf16),
        in_specs=[anywhere] * len(query_list),
        out_specs=anywhere,
        scratch_shapes=[pltpu.SemaphoreType.DMA((len(query_list),))],
        compiler_params=pltpu.CompilerParams(vmem_limit_bytes=small_vmem_bytes),
        cost_estimate=pl.CostEstimate(flops=2**20, bytes_accessed=2 * 2**20, transcendentals=0),
        name="place_queries",
    )(*query_list)
    cart_grads = pl.pallas_call(
        functools.partial(cart_kernel, kv_local),
        out_shape=jax.ShapeDtypeStruct((part_rows * 2 * kv_local, head_dim), f32),
        compiler_params=pltpu.CompilerParams(vmem_limit_bytes=small_vmem_bytes),
        cost_estimate=pl.CostEstimate(flops=2**20, bytes_accessed=2 * 2**20, transcendentals=0),
        name="cart_grads",
    )(*[part for part, _ in cart_list], *[got for _, got in cart_list])
    cart_grads = cart_grads.reshape(part_rows, 2, kv_local, head_dim)
    self_grads = outs[-1].reshape(2, tokens, kv_local, head_dim)
    return (cart_grads, self_grads, query_grads)


def solution(mesh):
    in_specs = (
        P(("groups", "dp"), "heads", None),
        P(("groups", "dp"), "heads", None),
        P(("groups", "dp"), "heads", None),
        P(("groups", "dp"), "heads", None),
        P("groups", "heads", None),
        P("groups", "heads", None),
        P(("groups", "dp"), None),
    )
    out_specs = (
        P(("groups", "dp"), None, "heads", None),
        P(None, ("groups", "dp"), "heads", None),
        P(("groups", "dp", "heads"), None),
    )
    return jax.shard_map(
        functools.partial(on_device, mesh.shape["dp"], mesh.shape["heads"]),
        mesh=mesh, in_specs=in_specs, out_specs=out_specs, check_vma=False,
    )
```

```python
import functools
import math

import jax
import jax.numpy as jnp
from jax import lax
from jax.experimental import pallas as pl
from jax.experimental.pallas import tpu as pltpu
from jax.sharding import PartitionSpec as P

masked_score = -1e30
vmem_bytes = 46 * 1024 * 1024
small_vmem_bytes = 8 * 1024 * 1024
early_steps = ()
f32 = jnp.float32
bf16 = jnp.bfloat16


def dot_nt(left, right):
    return lax.dot_general(left, right, (((1,), (1,)), ((), ())), preferred_element_type=f32)


def dot_nn(left, right):
    return lax.dot_general(left, right, (((1,), (0,)), ((), ())), preferred_element_type=f32)


def fold_rows(values, op):
    rows, columns = values.shape
    return op(values.reshape(rows // 8, 8, columns), axis=0)


def head_kernel(dp_size, heads_size, kv_index, kv_local, width, block_tokens, chunk, fine, sub, *refs):
    last = kv_index == kv_local - 1
    first = kv_index == 0
    if first:
        (q_ref, g_ref, sk_ref, sv_ref, ck_ref, cv_ref, seg_ref), refs = refs[:7], refs[7:]
    else:
        (keys_ref, vals_ref, keys_t_ref, q_rows, g_rows, seg_in), refs = refs[:6], refs[6:]
    held = kv_index if last else 0
    near_steps, far_steps = split_steps(heads_size)
    kept = len(near_steps)
    dq_before, refs = refs[: held * kept], refs[held * kept :]
    self_before, refs = refs[:held], refs[held:]
    (keep_ref, send_ref), refs = refs[:2], refs[2:]
    dq_outs, self_ref, refs = refs[:heads_size], refs[heads_size], refs[heads_size + 1 :]
    if first:
        others = range(1, kv_local)
        next_refs = {other: refs[5 * other - 5 : 5 * other] for other in others}
        refs = refs[5 * len(others) :]
        if kv_local > 1:
            seg_out, refs = refs[0], refs[1:]
        (
            keys_ref, vals_ref, keys_t_ref, q_in, g_in, sk_in, sv_in, ck_in, cv_in, seg_in, sems,
        ), refs = refs[:11], refs[11:]
    wide_ref, s_ref, w_ref, d_ref, p_ref, ds_ref, dk_ref, dv_ref, out_ref, dq_ref = refs
    all_keys, head_dim = keys_ref.shape
    tokens = seg_in.shape[1]
    cart_rows = all_keys - tokens
    rows = block_tokens * width
    scale = head_dim ** -0.5
    scale2 = scale * math.log2(math.e)
    span = block_tokens * kv_local * width
    blocks = tokens // block_tokens

    if first:

        def block_copy(source, target, block, sem):
            at = slice(block * span, (block + 1) * span)
            return pltpu.make_async_copy(source.at[at, :], target.at[at, :], sems.at[sem])

        copies = {
            name: pltpu.make_async_copy(source, target, sems.at[at])
            for at, (name, source, target) in enumerate(
                [("ck", ck_ref, ck_in), ("sk", sk_ref, sk_in), ("cv", cv_ref, cv_in), ("sv", sv_ref, sv_in)]
            )
        }
        for block in range(blocks):
            copies["q", block] = block_copy(q_ref, q_in, block, 4 + block)
            copies["g", block] = block_copy(g_ref, g_in, block, 4 + blocks + block)
        copies["seg"] = pltpu.make_async_copy(seg_ref, seg_in, sems.at[4 + 2 * blocks])
        order = ["ck", "sk", ("q", 0), "seg", "cv", "sv", ("g", 0)]
        order += [(kind, block) for block in range(1, blocks) for kind in ("q", "g")]
        for name in order:
            copies[name].start()

    def pick(name, ref, dst, at):
        copies[name].wait()
        count = ref.shape[0] // kv_local
        if kv_local == 1:
            dst[at : at + count, :] = ref[...]
        else:
            wide_ref[0 : ref.shape[0], :] = ref[...].astype(f32)
            dst[at : at + count, :] = wide_ref[pl.ds(0, count, stride=kv_local), :].astype(bf16)
            for other in others:
                next_ref = next_refs[other][0 if dst is keys_ref else 1]
                next_ref[at : at + count, :] = wide_ref[pl.ds(other, count, stride=kv_local), :].astype(bf16)

    def rows_of(name, block):
        at = slice(block * rows, (block + 1) * rows)
        if not first:
            return (q_rows if name == "q" else g_rows)[at, :]
        copies[name, block].wait()
        wide = (q_in if name == "q" else g_in)[block * span : (block + 1) * span, :]
        if kv_local == 1:
            return wide
        wide = wide.astype(f32).reshape(block_tokens, kv_local, width, head_dim)
        for other in others:
            next_refs[other][3 if name == "q" else 4][at, :] = wide[:, other].reshape(rows, head_dim).astype(bf16)
        return wide[:, 0].reshape(rows, head_dim).astype(bf16)

    if first:
        copies["seg"].wait()
        if kv_local > 1:
            seg_out[...] = seg_in[...]
    first_count = jnp.sum((seg_in[...] == 0).astype(f32), axis=1, keepdims=True).astype(jnp.int32)

    def limit(block):
        return -(-(block + 1) * block_tokens // fine) * fine

    def pieces(block):
        cart = [(start, chunk) for start in range(0, cart_rows, chunk)]
        return cart + [(cart_rows, limit(block))]

    queries, grads, peaks, stats = {}, {}, {}, {}
    acc = {}

    def spread(values):
        return jnp.concatenate([values] * (sub // 8), axis=0)

    def subs(start, size):
        return [slice(at, at + sub) for at in range(start, start + size, sub)]

    def open_scores(block):
        queries[block] = rows_of("q", block)
        token = (lax.broadcasted_iota(jnp.int32, (1, rows), 1) + block * rows) // width
        begin = jnp.where(token >= first_count, first_count, 0)
        acc["peak"] = jnp.full((8, rows), masked_score, f32)
        acc["token"], acc["begin"] = token, begin

    def step_scores(block, start, size):
        s_ref[block % 2, start : start + size, :] = dot_nt(keys_ref[start : start + size, :], queries[block])
        for at in subs(start, size):
            score = s_ref[block % 2, at, :]
            if start >= cart_rows:
                key_at = lax.broadcasted_iota(jnp.int32, (sub, rows), 0) + (at.start - cart_rows)
                score = jnp.where((key_at >= acc["begin"]) & (key_at <= acc["token"]), score, masked_score)
                s_ref[block % 2, at, :] = score
            acc["peak"] = jnp.maximum(acc["peak"], fold_rows(score, jnp.max))

    def close_scores(block):
        peaks[block] = jnp.broadcast_to(jnp.max(acc["peak"], axis=0, keepdims=True), (8, rows))

    def open_weights(block):
        grads[block] = rows_of("g", block)
        acc["total"] = jnp.zeros((8, rows), f32)
        acc["center"] = jnp.zeros((8, rows), f32)

    def step_weights(block, start, size):
        d_ref[block % 2, start : start + size, :] = dot_nt(vals_ref[start : start + size, :], grads[block])
        for at in subs(start, size):
            weight = jnp.exp2((s_ref[block % 2, at, :] - spread(peaks[block])) * scale2)
            w_ref[block % 2, at, :] = weight
            acc["total"] = acc["total"] + fold_rows(weight, jnp.sum)
            acc["center"] = acc["center"] + fold_rows(weight * d_ref[block % 2, at, :], jnp.sum)

    def close_weights(block):
        share = 1.0 / jnp.sum(acc["total"], axis=0, keepdims=True)
        center = jnp.sum(acc["center"], axis=0, keepdims=True) * share
        stats[block] = jnp.broadcast_to(share, (8, rows)), jnp.broadcast_to(center, (8, rows))

    def open_grads(block):
        pass

    def step_grads(block, start, size):
        slot = block % 2
        share, center = stats[block]
        for at in subs(start, size):
            prob = w_ref[slot, at, :] * spread(share)
            p_ref[slot, at, :] = prob.astype(bf16)
            ds_ref[slot, at, :] = (prob * (d_ref[slot, at, :] - spread(center))).astype(bf16)
        at = slice(start, start + size)
        old = size if start < cart_rows else (limit(block - 1) if block else 0)
        old = old if block else 0
        for ref, left, right in ((dv_ref, p_ref, grads[block]), (dk_ref, ds_ref, queries[block])):
            part = dot_nn(left[slot, at, :], right)
            if old:
                ref[start : start + old, :] += part[:old]
            if old < size:
                ref[start + old : start + size, :] = part[old:]

    def close_grads(block):
        seen = cart_rows + limit(block)
        dq_t = dot_nn(keys_t_ref[:, 0:seen], ds_ref[block % 2, 0:seen, :])
        out_ref[...] = (dq_t * scale).T
        for head in range(width):
            dq_ref[block * block_tokens : (block + 1) * block_tokens, head * head_dim : (head + 1) * head_dim] = (
                out_ref[pl.ds(head, block_tokens, stride=width), :].astype(bf16)
            )

    if first:
        pick("ck", ck_in, keys_ref, 0)
        pick("sk", sk_in, keys_ref, cart_rows)
    stages = (
        (2, open_grads, step_grads, close_grads),
        (1, open_weights, step_weights, close_weights),
        (0, open_scores, step_scores, close_scores),
    )
    for turn in range(blocks + 2):
        live = [(turn - lag, *calls) for lag, *calls in stages if 0 <= turn - lag < blocks]
        if turn == 1 and first:
            pick("cv", cv_in, vals_ref, 0)
            pick("sv", sv_in, vals_ref, cart_rows)
            keys_t_ref[...] = keys_ref[...].astype(f32).T.astype(bf16)
            for other in others:
                next_refs[other][2][...] = next_refs[other][0][...].astype(f32).T.astype(bf16)
        for block, begin_call, _, _ in live:
            begin_call(block)
        for index in range(len(pieces(0))):
            for block, _, step_call, _ in live:
                step_call(block, *pieces(block)[index])
        for block, _, _, end_call in live:
            end_call(block)

    part_rows = cart_rows // dp_size
    me = lax.axis_index("dp")
    for step in range(dp_size):
        at = pl.ds(pl.multiple_of((me ^ step) * part_rows, part_rows), part_rows)
        ref = send_ref if step % 2 else keep_ref
        ref[step // 2, 0] = (dk_ref[at, :] * scale).astype(ref.dtype)
        ref[step // 2, 1] = dv_ref[at, :].astype(ref.dtype)
    own = dk_ref[cart_rows:all_keys, :] * scale, dv_ref[cart_rows:all_keys, :]
    own_tokens = tokens // heads_size
    columns = width * head_dim
    me = lax.axis_index("heads")
    for place, (step, ref) in enumerate(zip(near_steps + far_steps, dq_outs)):
        target = me ^ step
        at = pl.ds(pl.multiple_of(target * own_tokens, own_tokens), own_tokens)
        if last and place < kept:
            for index in range(held):
                ref[:, index * columns : (index + 1) * columns] = dq_before[index * kept + place][...]
            ref[:, held * columns :] = dq_ref[at, :]
        else:
            ref[...] = dq_ref[at, :]
    if not last:
        self_ref[0], self_ref[1] = own
        return
    count = tokens * kv_local
    for kind in range(2):
        for index, before in enumerate(self_before):
            wide_ref[pl.ds(index, tokens, stride=kv_local), :] = before[kind]
        wide_ref[pl.ds(kv_index, tokens, stride=kv_local), :] = own[kind]
        self_ref[kind * count : (kind + 1) * count, :] = wide_ref[0:count, :].astype(bf16)


def fold_kernel(part_ref, got_ref, keep_ref, send_ref):
    for index in range(part_ref.shape[0]):
        total = part_ref[index] + got_ref[index].astype(f32)
        ref = send_ref if index % 2 else keep_ref
        ref[index // 2] = total.astype(ref.dtype)


def cart_kernel(kv_local, *refs):
    part_refs, got_refs, out_ref = refs[:kv_local], refs[kv_local:-1], refs[-1]
    part_rows = part_refs[0].shape[2]
    for kv_index in range(kv_local):
        for kind in range(2):
            total = part_refs[kv_index][0, kind] + got_refs[kv_index][0, kind].astype(f32)
            out_ref[pl.ds(kind * kv_local + kv_index, part_rows, stride=2 * kv_local), :] = total


def place_kernel(heads_size, kv_local, *refs):
    part_refs, out_ref, sems = refs[:-2], refs[-2], refs[-1]
    near_steps, far_steps = split_steps(heads_size)
    columns = out_ref.shape[1] // (heads_size * kv_local)
    me = lax.axis_index("heads")
    places = [(step, 0) for step in near_steps]
    places += [(step, kv_index) for kv_index in range(kv_local) for step in far_steps]
    copies = []
    for index, ((step, kv_index), ref) in enumerate(zip(places, part_refs)):
        source = me ^ step
        at = pl.multiple_of((source * kv_local + kv_index) * columns, columns)
        copies.append(pltpu.make_async_copy(ref, out_ref.at[:, pl.ds(at, ref.shape[1])], sems.at[index]))
    for copy in copies:
        copy.start()
    for copy in copies:
        copy.wait()


def swap(values, axis, size, step):
    if step == 0:
        return values
    return lax.ppermute(values, axis, [(source, source ^ step) for source in range(size)])


def fold(part, got):
    half = part.shape[0] // 2
    return pl.pallas_call(
        fold_kernel,
        out_shape=(
            jax.ShapeDtypeStruct((half, *part.shape[1:]), f32),
            jax.ShapeDtypeStruct((half, *part.shape[1:]), bf16),
        ),
        compiler_params=pltpu.CompilerParams(vmem_limit_bytes=small_vmem_bytes),
        cost_estimate=pl.CostEstimate(flops=2**20, bytes_accessed=2**20, transcendentals=0),
        name="cart_fold",
    )(part, got)


def split_steps(heads_size):
    early = [step for step in range(heads_size) if step in early_steps]
    late = [0, *range(2, heads_size), 1]
    return [step for step in late if step < heads_size and step not in early], early


def on_device(dp_size, heads_size, queries, out_grad, self_keys, self_values, cart_keys, cart_values, segment_ids):
    tokens, heads_local, head_dim = queries.shape
    kv_local = self_keys.shape[1]
    cart_rows = cart_keys.shape[0]
    width = heads_local // kv_local
    block_tokens = 64
    chunk = 512
    fine = 128
    sub = 16
    all_keys = cart_rows + tokens
    rows = block_tokens * width
    part_rows = cart_rows // dp_size
    own_tokens = tokens // heads_size
    flat = [pltpu.with_memory_space_constraint(array.reshape(-1, head_dim), pltpu.HBM) for array in (queries, out_grad, self_keys, self_values, cart_keys, cart_values)]
    segments = pltpu.with_memory_space_constraint(segment_ids, pltpu.HBM)
    macs = tokens * width * all_keys * head_dim * 5
    blocks = tokens // block_tokens
    columns = width * head_dim
    count = tokens * kv_local
    near_steps, far_steps = split_steps(heads_size)
    kept = len(near_steps)
    anywhere = pl.BlockSpec(memory_space=pl.ANY)
    cart_list, kept_list, far_list, self_list, received = [], [], [], [], []
    for kv_index in range(kv_local):
        last = kv_index == kv_local - 1
        near = jax.ShapeDtypeStruct((own_tokens, kv_local * columns if last else columns), bf16)
        far = jax.ShapeDtypeStruct((own_tokens, columns), bf16)
        own_shape = (2 * count, head_dim) if last else (2, tokens, head_dim)
        other_shapes = [near] * kept + [far] * (heads_size - kept)
        other_shapes.append(jax.ShapeDtypeStruct(own_shape, bf16 if last else f32))
        next_shapes, first_scratch = [], []
        if kv_index == 0:
            key_like = jax.ShapeDtypeStruct((all_keys, head_dim), bf16)
            turned = jax.ShapeDtypeStruct((head_dim, all_keys), bf16)
            row_like = jax.ShapeDtypeStruct((tokens * width, head_dim), bf16)
            next_shapes = [key_like, key_like, turned, row_like, row_like] * (kv_local - 1)
            if kv_local > 1:
                next_shapes.append(jax.ShapeDtypeStruct(segment_ids.shape, jnp.int32))
            inputs = [*flat, segments]
            first_scratch = [
                pltpu.VMEM((all_keys, head_dim), bf16),
                pltpu.VMEM((all_keys, head_dim), bf16),
                pltpu.VMEM((head_dim, all_keys), bf16),
                *[pltpu.VMEM(array.shape, bf16) for array in flat],
                pltpu.VMEM(segment_ids.shape, jnp.int32),
                pltpu.SemaphoreType.DMA((5 + 2 * blocks,)),
            ]
        else:
            inputs = [*prepared[5 * kv_index - 5 : 5 * kv_index], prepared[-1]]
        before = kept_list + self_list if last else []
        outs = pl.pallas_call(
            functools.partial(head_kernel, dp_size, heads_size, kv_index, kv_local, width, block_tokens, chunk, fine, sub),
            out_shape=(
                jax.ShapeDtypeStruct((dp_size // 2, 2, part_rows, head_dim), f32),
                jax.ShapeDtypeStruct((dp_size // 2, 2, part_rows, head_dim), bf16),
                *other_shapes,
                *next_shapes,
            ),
            in_specs=[pl.BlockSpec(memory_space=pltpu.VMEM if kv_index else pltpu.HBM)] * len(inputs)
            + [pl.BlockSpec(memory_space=pltpu.VMEM)] * len(before),
            scratch_shapes=[
                *first_scratch,
                pltpu.VMEM((cart_rows * kv_local, head_dim), f32),
                pltpu.VMEM((2, all_keys, rows), f32),
                pltpu.VMEM((2, all_keys, rows), f32),
                pltpu.VMEM((2, all_keys, rows), f32),
                pltpu.VMEM((2, all_keys, rows), bf16),
                pltpu.VMEM((2, all_keys, rows), bf16),
                pltpu.VMEM((all_keys, head_dim), f32),
                pltpu.VMEM((all_keys, head_dim), f32),
                pltpu.VMEM((rows, head_dim), f32),
                pltpu.VMEM((tokens, columns), bf16),
            ],
            compiler_params=pltpu.CompilerParams(vmem_limit_bytes=vmem_bytes),
            cost_estimate=pl.CostEstimate(flops=4 * macs, bytes_accessed=5 * 2**20, transcendentals=tokens * width * all_keys),
            name="head_grads",
        )(*inputs, *before)
        if kv_index == 0:
            prepared = outs[len(outs) - len(next_shapes) :]
        outs = outs[: len(outs) - len(next_shapes)]
        part, send, near, far = outs[0], outs[1], outs[2 : 2 + kept], outs[2 + kept : -1]
        if last:
            part, send, near, far, received = lax.optimization_barrier((part, send, near, far, received))
        else:
            kept_list += near
            self_list.append(outs[-1])
        received.append((part, swap(send, "dp", dp_size, 1)))
        far_parts = [swap(block, "heads", heads_size, step) for step, block in zip(far_steps, far)]
        if not last:
            received[-1] += tuple(far_parts)
    far_list = [block for _, _, *blocks_far in received for block in blocks_far]
    for part, got, *_ in received:
        step = 2
        while step < dp_size:
            part, send = fold(part, got)
            got = swap(send, "dp", dp_size, step)
            step *= 2
        cart_list.append((part, got))
    query_list = [swap(block, "heads", heads_size, step) for step, block in zip(near_steps, near)] + far_list + far_parts
    query_grads = pl.pallas_call(
        functools.partial(place_kernel, heads_size, kv_local),
        out_shape=jax.ShapeDtypeStruct((own_tokens, heads_size * heads_local * head_dim), bf16),
        in_specs=[anywhere] * len(query_list),
        out_specs=anywhere,
        scratch_shapes=[pltpu.SemaphoreType.DMA((len(query_list),))],
        compiler_params=pltpu.CompilerParams(vmem_limit_bytes=small_vmem_bytes),
        cost_estimate=pl.CostEstimate(flops=2**20, bytes_accessed=2 * 2**20, transcendentals=0),
        name="place_queries",
    )(*query_list)
    cart_grads = pl.pallas_call(
        functools.partial(cart_kernel, kv_local),
        out_shape=jax.ShapeDtypeStruct((part_rows * 2 * kv_local, head_dim), f32),
        compiler_params=pltpu.CompilerParams(vmem_limit_bytes=small_vmem_bytes),
        cost_estimate=pl.CostEstimate(flops=2**20, bytes_accessed=2 * 2**20, transcendentals=0),
        name="cart_grads",
    )(*[part for part, _ in cart_list], *[got for _, got in cart_list])
    cart_grads = cart_grads.reshape(part_rows, 2, kv_local, head_dim)
    self_grads = outs[-1].reshape(2, tokens, kv_local, head_dim)
    return (cart_grads, self_grads, query_grads)


def solution(mesh):
    in_specs = (
        P(("groups", "dp"), "heads", None),
        P(("groups", "dp"), "heads", None),
        P(("groups", "dp"), "heads", None),
        P(("groups", "dp"), "heads", None),
        P("groups", "heads", None),
        P("groups", "heads", None),
        P(("groups", "dp"), None),
    )
    out_specs = (
        P(("groups", "dp"), None, "heads", None),
        P(None, ("groups", "dp"), "heads", None),
        P(("groups", "dp", "heads"), None),
    )
    return jax.shard_map(
        functools.partial(on_device, mesh.shape["dp"], mesh.shape["heads"]),
        mesh=mesh, in_specs=in_specs, out_specs=out_specs, check_vma=False,
    )
```

```python
import functools
import math

import jax
import jax.numpy as jnp
from jax import lax
from jax.experimental import pallas as pl
from jax.experimental.pallas import tpu as pltpu
from jax.sharding import PartitionSpec as P

masked_score = -1e30
vmem_bytes = 46 * 1024 * 1024
small_vmem_bytes = 8 * 1024 * 1024
early_steps = ()
f32 = jnp.float32
bf16 = jnp.bfloat16


def dot_nt(left, right):
    return lax.dot_general(left, right, (((1,), (1,)), ((), ())), preferred_element_type=f32)


def dot_nn(left, right):
    return lax.dot_general(left, right, (((1,), (0,)), ((), ())), preferred_element_type=f32)


def fold_rows(values, op):
    rows, columns = values.shape
    return op(values.reshape(rows // 8, 8, columns), axis=0)


def head_kernel(dp_size, heads_size, kv_index, kv_local, width, block_tokens, chunk, fine, sub, *refs):
    last = kv_index == kv_local - 1
    first = kv_index == 0
    if first:
        (q_ref, g_ref, sk_ref, sv_ref, ck_ref, cv_ref, seg_ref), refs = refs[:7], refs[7:]
    else:
        (keys_ref, vals_ref, keys_t_ref, q_rows, g_rows, seg_in), refs = refs[:6], refs[6:]
    held = kv_index if last else 0
    near_steps, far_steps = split_steps(heads_size)
    kept = len(near_steps)
    dq_before, refs = refs[: held * kept], refs[held * kept :]
    self_before, refs = refs[:held], refs[held:]
    (keep_ref, send_ref), refs = refs[:2], refs[2:]
    dq_outs, self_ref, refs = refs[:heads_size], refs[heads_size], refs[heads_size + 1 :]
    if first:
        others = range(1, kv_local)
        next_refs = {other: refs[5 * other - 5 : 5 * other] for other in others}
        refs = refs[5 * len(others) :]
        if kv_local > 1:
            seg_out, refs = refs[0], refs[1:]
        (
            keys_ref, vals_ref, keys_t_ref, q_in, g_in, sk_in, sv_in, ck_in, cv_in, seg_in, sems,
        ), refs = refs[:11], refs[11:]
    wide_ref, s_ref, w_ref, d_ref, p_ref, ds_ref, dk_ref, dv_ref, out_ref, dq_ref = refs
    all_keys, head_dim = keys_ref.shape
    tokens = seg_in.shape[1]
    cart_rows = all_keys - tokens
    rows = block_tokens * width
    scale = head_dim ** -0.5
    scale2 = scale * math.log2(math.e)
    span = block_tokens * kv_local * width
    blocks = tokens // block_tokens

    if first:

        def block_copy(source, target, block, sem):
            at = slice(block * span, (block + 1) * span)
            return pltpu.make_async_copy(source.at[at, :], target.at[at, :], sems.at[sem])

        copies = {
            name: pltpu.make_async_copy(source, target, sems.at[at])
            for at, (name, source, target) in enumerate(
                [("ck", ck_ref, ck_in), ("sk", sk_ref, sk_in), ("cv", cv_ref, cv_in), ("sv", sv_ref, sv_in)]
            )
        }
        for block in range(blocks):
            copies["q", block] = block_copy(q_ref, q_in, block, 4 + block)
            copies["g", block] = block_copy(g_ref, g_in, block, 4 + blocks + block)
        copies["seg"] = pltpu.make_async_copy(seg_ref, seg_in, sems.at[4 + 2 * blocks])
        order = ["ck", "sk", ("q", 0), "seg", "cv", "sv", ("g", 0)]
        order += [(kind, block) for block in range(1, blocks) for kind in ("q", "g")]
        for name in order:
            copies[name].start()

    def pick(name, ref, dst, at):
        copies[name].wait()
        count = ref.shape[0] // kv_local
        if kv_local == 1:
            dst[at : at + count, :] = ref[...]
        else:
            wide_ref[0 : ref.shape[0], :] = ref[...].astype(f32)
            dst[at : at + count, :] = wide_ref[pl.ds(0, count, stride=kv_local), :].astype(bf16)
            for other in others:
                next_ref = next_refs[other][0 if dst is keys_ref else 1]
                next_ref[at : at + count, :] = wide_ref[pl.ds(other, count, stride=kv_local), :].astype(bf16)

    def rows_of(name, block):
        at = slice(block * rows, (block + 1) * rows)
        if not first:
            return (q_rows if name == "q" else g_rows)[at, :]
        copies[name, block].wait()
        wide = (q_in if name == "q" else g_in)[block * span : (block + 1) * span, :]
        if kv_local == 1:
            return wide
        wide = wide.astype(f32).reshape(block_tokens, kv_local, width, head_dim)
        for other in others:
            next_refs[other][3 if name == "q" else 4][at, :] = wide[:, other].reshape(rows, head_dim).astype(bf16)
        return wide[:, 0].reshape(rows, head_dim).astype(bf16)

    if first:
        copies["seg"].wait()
        if kv_local > 1:
            seg_out[...] = seg_in[...]
    first_count = jnp.sum((seg_in[...] == 0).astype(f32), axis=1, keepdims=True).astype(jnp.int32)

    def limit(block):
        return -(-(block + 1) * block_tokens // fine) * fine

    def pieces(block):
        cart = [(start, chunk) for start in range(0, cart_rows, chunk)]
        return cart + [(cart_rows, limit(block))]

    queries, grads, peaks, stats = {}, {}, {}, {}
    acc = {}

    def spread(values):
        return jnp.concatenate([values] * (sub // 8), axis=0)

    def subs(start, size):
        return [slice(at, at + sub) for at in range(start, start + size, sub)]

    def open_scores(block):
        queries[block] = rows_of("q", block)
        token = (lax.broadcasted_iota(jnp.int32, (1, rows), 1) + block * rows) // width
        begin = jnp.where(token >= first_count, first_count, 0)
        acc["peak"] = jnp.full((8, rows), masked_score, f32)
        acc["token"], acc["begin"] = token, begin

    def step_scores(block, start, size):
        s_ref[block % 2, start : start + size, :] = dot_nt(keys_ref[start : start + size, :], queries[block])
        for at in subs(start, size):
            score = s_ref[block % 2, at, :]
            if start >= cart_rows:
                key_at = lax.broadcasted_iota(jnp.int32, (sub, rows), 0) + (at.start - cart_rows)
                score = jnp.where((key_at >= acc["begin"]) & (key_at <= acc["token"]), score, masked_score)
                s_ref[block % 2, at, :] = score
            acc["peak"] = jnp.maximum(acc["peak"], fold_rows(score, jnp.max))

    def close_scores(block):
        peaks[block] = jnp.broadcast_to(jnp.max(acc["peak"], axis=0, keepdims=True), (8, rows))

    def open_weights(block):
        grads[block] = rows_of("g", block)
        acc["total"] = jnp.zeros((8, rows), f32)
        acc["center"] = jnp.zeros((8, rows), f32)

    def step_weights(block, start, size):
        d_ref[block % 2, start : start + size, :] = dot_nt(vals_ref[start : start + size, :], grads[block])
        for at in subs(start, size):
            weight = jnp.exp2((s_ref[block % 2, at, :] - spread(peaks[block])) * scale2)
            w_ref[block % 2, at, :] = weight
            acc["total"] = acc["total"] + fold_rows(weight, jnp.sum)
            acc["center"] = acc["center"] + fold_rows(weight * d_ref[block % 2, at, :], jnp.sum)

    def close_weights(block):
        share = 1.0 / jnp.sum(acc["total"], axis=0, keepdims=True)
        center = jnp.sum(acc["center"], axis=0, keepdims=True) * share
        stats[block] = jnp.broadcast_to(share, (8, rows)), jnp.broadcast_to(center, (8, rows))

    def open_grads(block):
        pass

    def step_grads(block, start, size):
        slot = block % 2
        share, center = stats[block]
        for at in subs(start, size):
            prob = w_ref[slot, at, :] * spread(share)
            p_ref[slot, at, :] = prob.astype(bf16)
            ds_ref[slot, at, :] = (prob * (d_ref[slot, at, :] - spread(center))).astype(bf16)
        at = slice(start, start + size)
        old = size if start < cart_rows else (limit(block - 1) if block else 0)
        old = old if block else 0
        for ref, left, right in ((dv_ref, p_ref, grads[block]), (dk_ref, ds_ref, queries[block])):
            part = dot_nn(left[slot, at, :], right)
            if old:
                ref[start : start + old, :] += part[:old]
            if old < size:
                ref[start + old : start + size, :] = part[old:]

    def close_grads(block):
        seen = cart_rows + limit(block)
        dq_t = dot_nn(keys_t_ref[:, 0:seen], ds_ref[block % 2, 0:seen, :])
        out_ref[...] = (dq_t * scale).T
        for head in range(width):
            dq_ref[block * block_tokens : (block + 1) * block_tokens, head * head_dim : (head + 1) * head_dim] = (
                out_ref[pl.ds(head, block_tokens, stride=width), :].astype(bf16)
            )

    if first:
        pick("ck", ck_in, keys_ref, 0)
        pick("sk", sk_in, keys_ref, cart_rows)
    stages = (
        (2, open_grads, step_grads, close_grads),
        (1, open_weights, step_weights, close_weights),
        (0, open_scores, step_scores, close_scores),
    )
    for turn in range(blocks + 2):
        live = [(turn - lag, *calls) for lag, *calls in stages if 0 <= turn - lag < blocks]
        if turn == 1 and first:
            pick("cv", cv_in, vals_ref, 0)
            pick("sv", sv_in, vals_ref, cart_rows)
            keys_t_ref[...] = keys_ref[...].astype(f32).T.astype(bf16)
            for other in others:
                next_refs[other][2][...] = next_refs[other][0][...].astype(f32).T.astype(bf16)
        for block, begin_call, _, _ in live:
            begin_call(block)
        for index in range(len(pieces(0))):
            for block, _, step_call, _ in live:
                step_call(block, *pieces(block)[index])
        for block, _, _, end_call in live:
            end_call(block)

    part_rows = cart_rows // dp_size
    me = lax.axis_index("dp")
    for step in range(dp_size):
        at = pl.ds(pl.multiple_of((me ^ step) * part_rows, part_rows), part_rows)
        ref = send_ref if step % 2 else keep_ref
        ref[step // 2, 0] = (dk_ref[at, :] * scale).astype(ref.dtype)
        ref[step // 2, 1] = dv_ref[at, :].astype(ref.dtype)
    own = dk_ref[cart_rows:all_keys, :] * scale, dv_ref[cart_rows:all_keys, :]
    own_tokens = tokens // heads_size
    columns = width * head_dim
    me = lax.axis_index("heads")
    for place, (step, ref) in enumerate(zip(near_steps + far_steps, dq_outs)):
        target = me ^ step
        at = pl.ds(pl.multiple_of(target * own_tokens, own_tokens), own_tokens)
        if last and place < kept:
            for index in range(held):
                ref[:, index * columns : (index + 1) * columns] = dq_before[index * kept + place][...]
            ref[:, held * columns :] = dq_ref[at, :]
        else:
            ref[...] = dq_ref[at, :]
    if not last:
        self_ref[0], self_ref[1] = own
        return
    count = tokens * kv_local
    for kind in range(2):
        for index, before in enumerate(self_before):
            wide_ref[pl.ds(index, tokens, stride=kv_local), :] = before[kind]
        wide_ref[pl.ds(kv_index, tokens, stride=kv_local), :] = own[kind]
        self_ref[kind * count : (kind + 1) * count, :] = wide_ref[0:count, :].astype(bf16)


def fold_kernel(part_ref, got_ref, keep_ref, send_ref):
    for index in range(part_ref.shape[0]):
        total = part_ref[index] + got_ref[index].astype(f32)
        ref = send_ref if index % 2 else keep_ref
        ref[index // 2] = total.astype(ref.dtype)


def cart_kernel(kv_local, *refs):
    part_refs, got_refs, (out_ref, *buffers, sems) = refs[:kv_local], refs[kv_local : 2 * kv_local], refs[2 * kv_local :]
    spread = 2 * kv_local
    rows = part_refs[0].shape[2] // len(buffers)
    copies = []
    for index, buffer in enumerate(buffers):
        here = slice(index * rows, (index + 1) * rows)
        for kv_index in range(kv_local):
            for kind in range(2):
                total = part_refs[kv_index][0, kind, here, :] + got_refs[kv_index][0, kind, here, :].astype(f32)
                buffer[pl.ds(kind * kv_local + kv_index, rows, stride=spread), :] = total
        at = slice(index * rows * spread, (index + 1) * rows * spread)
        copies.append(pltpu.make_async_copy(buffer, out_ref.at[at, :], sems.at[index]))
        copies[-1].start()
    for copy in copies:
        copy.wait()


def place_kernel(heads_size, kv_local, *refs):
    part_refs, out_ref, sems = refs[:-2], refs[-2], refs[-1]
    near_steps, far_steps = split_steps(heads_size)
    columns = out_ref.shape[1] // (heads_size * kv_local)
    me = lax.axis_index("heads")
    places = [(step, 0) for step in near_steps]
    places += [(step, kv_index) for kv_index in range(kv_local) for step in far_steps]
    copies = []
    for index, ((step, kv_index), ref) in enumerate(zip(places, part_refs)):
        source = me ^ step
        at = pl.multiple_of((source * kv_local + kv_index) * columns, columns)
        copies.append(pltpu.make_async_copy(ref, out_ref.at[:, pl.ds(at, ref.shape[1])], sems.at[index]))
    for copy in copies:
        copy.start()
    for copy in copies:
        copy.wait()


def swap(values, axis, size, step):
    if step == 0:
        return values
    return lax.ppermute(values, axis, [(source, source ^ step) for source in range(size)])


def fold(part, got):
    half = part.shape[0] // 2
    return pl.pallas_call(
        fold_kernel,
        out_shape=(
            jax.ShapeDtypeStruct((half, *part.shape[1:]), f32),
            jax.ShapeDtypeStruct((half, *part.shape[1:]), bf16),
        ),
        compiler_params=pltpu.CompilerParams(vmem_limit_bytes=small_vmem_bytes),
        cost_estimate=pl.CostEstimate(flops=2**20, bytes_accessed=2**20, transcendentals=0),
        name="cart_fold",
    )(part, got)


def split_steps(heads_size):
    early = [step for step in range(heads_size) if step in early_steps]
    late = [0, *range(2, heads_size), 1]
    return [step for step in late if step < heads_size and step not in early], early


def on_device(dp_size, heads_size, queries, out_grad, self_keys, self_values, cart_keys, cart_values, segment_ids):
    tokens, heads_local, head_dim = queries.shape
    kv_local = self_keys.shape[1]
    cart_rows = cart_keys.shape[0]
    width = heads_local // kv_local
    block_tokens = 64
    chunk = 512
    fine = 64
    sub = 16
    all_keys = cart_rows + tokens
    rows = block_tokens * width
    part_rows = cart_rows // dp_size
    own_tokens = tokens // heads_size
    flat = [pltpu.with_memory_space_constraint(array.reshape(-1, head_dim), pltpu.HBM) for array in (queries, out_grad, self_keys, self_values, cart_keys, cart_values)]
    segments = pltpu.with_memory_space_constraint(segment_ids, pltpu.HBM)
    macs = tokens * width * all_keys * head_dim * 5
    blocks = tokens // block_tokens
    columns = width * head_dim
    count = tokens * kv_local
    near_steps, far_steps = split_steps(heads_size)
    kept = len(near_steps)
    anywhere = pl.BlockSpec(memory_space=pl.ANY)
    cart_list, kept_list, far_list, self_list, received = [], [], [], [], []
    for kv_index in range(kv_local):
        last = kv_index == kv_local - 1
        near = jax.ShapeDtypeStruct((own_tokens, kv_local * columns if last else columns), bf16)
        far = jax.ShapeDtypeStruct((own_tokens, columns), bf16)
        own_shape = (2 * count, head_dim) if last else (2, tokens, head_dim)
        other_shapes = [near] * kept + [far] * (heads_size - kept)
        other_shapes.append(jax.ShapeDtypeStruct(own_shape, bf16 if last else f32))
        next_shapes, first_scratch = [], []
        if kv_index == 0:
            key_like = jax.ShapeDtypeStruct((all_keys, head_dim), bf16)
            turned = jax.ShapeDtypeStruct((head_dim, all_keys), bf16)
            row_like = jax.ShapeDtypeStruct((tokens * width, head_dim), bf16)
            next_shapes = [key_like, key_like, turned, row_like, row_like] * (kv_local - 1)
            if kv_local > 1:
                next_shapes.append(jax.ShapeDtypeStruct(segment_ids.shape, jnp.int32))
            inputs = [*flat, segments]
            first_scratch = [
                pltpu.VMEM((all_keys, head_dim), bf16),
                pltpu.VMEM((all_keys, head_dim), bf16),
                pltpu.VMEM((head_dim, all_keys), bf16),
                *[pltpu.VMEM(array.shape, bf16) for array in flat],
                pltpu.VMEM(segment_ids.shape, jnp.int32),
                pltpu.SemaphoreType.DMA((5 + 2 * blocks,)),
            ]
        else:
            inputs = [*prepared[5 * kv_index - 5 : 5 * kv_index], prepared[-1]]
        before = kept_list + self_list if last else []
        outs = pl.pallas_call(
            functools.partial(head_kernel, dp_size, heads_size, kv_index, kv_local, width, block_tokens, chunk, fine, sub),
            out_shape=(
                jax.ShapeDtypeStruct((dp_size // 2, 2, part_rows, head_dim), f32),
                jax.ShapeDtypeStruct((dp_size // 2, 2, part_rows, head_dim), bf16),
                *other_shapes,
                *next_shapes,
            ),
            in_specs=[pl.BlockSpec(memory_space=pltpu.VMEM if kv_index else pltpu.HBM)] * len(inputs)
            + [pl.BlockSpec(memory_space=pltpu.VMEM)] * len(before),
            scratch_shapes=[
                *first_scratch,
                pltpu.VMEM((cart_rows * kv_local, head_dim), f32),
                pltpu.VMEM((2, all_keys, rows), f32),
                pltpu.VMEM((2, all_keys, rows), f32),
                pltpu.VMEM((2, all_keys, rows), f32),
                pltpu.VMEM((2, all_keys, rows), bf16),
                pltpu.VMEM((2, all_keys, rows), bf16),
                pltpu.VMEM((all_keys, head_dim), f32),
                pltpu.VMEM((all_keys, head_dim), f32),
                pltpu.VMEM((rows, head_dim), f32),
                pltpu.VMEM((tokens, columns), bf16),
            ],
            compiler_params=pltpu.CompilerParams(vmem_limit_bytes=vmem_bytes),
            cost_estimate=pl.CostEstimate(flops=4 * macs, bytes_accessed=5 * 2**20, transcendentals=tokens * width * all_keys),
            name="head_grads",
        )(*inputs, *before)
        if kv_index == 0:
            prepared = outs[len(outs) - len(next_shapes) :]
        outs = outs[: len(outs) - len(next_shapes)]
        part, send, near, far = outs[0], outs[1], outs[2 : 2 + kept], outs[2 + kept : -1]
        if last:
            part, send, near, far, received = lax.optimization_barrier((part, send, near, far, received))
        else:
            kept_list += near
            self_list.append(outs[-1])
        received.append((part, swap(send, "dp", dp_size, 1)))
        far_parts = [swap(block, "heads", heads_size, step) for step, block in zip(far_steps, far)]
        if not last:
            received[-1] += tuple(far_parts)
    far_list = [block for _, _, *blocks_far in received for block in blocks_far]
    for part, got, *_ in received:
        step = 2
        while step < dp_size:
            part, send = fold(part, got)
            got = swap(send, "dp", dp_size, step)
            step *= 2
        cart_list.append((part, got))
    query_list = [swap(block, "heads", heads_size, step) for step, block in zip(near_steps, near)] + far_list + far_parts
    query_grads = pl.pallas_call(
        functools.partial(place_kernel, heads_size, kv_local),
        out_shape=jax.ShapeDtypeStruct((own_tokens, heads_size * heads_local * head_dim), bf16),
        in_specs=[anywhere] * len(query_list),
        out_specs=anywhere,
        scratch_shapes=[pltpu.SemaphoreType.DMA((len(query_list),))],
        compiler_params=pltpu.CompilerParams(vmem_limit_bytes=small_vmem_bytes),
        cost_estimate=pl.CostEstimate(flops=2**20, bytes_accessed=2 * 2**20, transcendentals=0),
        name="place_queries",
    )(*query_list)
    cart_grads = pl.pallas_call(
        functools.partial(cart_kernel, kv_local),
        out_shape=jax.ShapeDtypeStruct((part_rows * 2 * kv_local, head_dim), f32),
        in_specs=[pl.BlockSpec(memory_space=pltpu.VMEM)] * (2 * kv_local),
        out_specs=anywhere,
        scratch_shapes=[
            pltpu.VMEM((part_rows * kv_local, head_dim), f32),
            pltpu.VMEM((part_rows * kv_local, head_dim), f32),
            pltpu.SemaphoreType.DMA((2,)),
        ],
        compiler_params=pltpu.CompilerParams(vmem_limit_bytes=small_vmem_bytes),
        cost_estimate=pl.CostEstimate(flops=2**20, bytes_accessed=2 * 2**20, transcendentals=0),
        name="cart_grads",
    )(*[part for part, _ in cart_list], *[got for _, got in cart_list])
    cart_grads = cart_grads.reshape(part_rows, 2, kv_local, head_dim)
    self_grads = outs[-1].reshape(2, tokens, kv_local, head_dim)
    return (cart_grads, self_grads, query_grads)


def solution(mesh):
    in_specs = (
        P(("groups", "dp"), "heads", None),
        P(("groups", "dp"), "heads", None),
        P(("groups", "dp"), "heads", None),
        P(("groups", "dp"), "heads", None),
        P("groups", "heads", None),
        P("groups", "heads", None),
        P(("groups", "dp"), None),
    )
    out_specs = (
        P(("groups", "dp"), None, "heads", None),
        P(None, ("groups", "dp"), "heads", None),
        P(("groups", "dp", "heads"), None),
    )
    return jax.shard_map(
        functools.partial(on_device, mesh.shape["dp"], mesh.shape["heads"]),
        mesh=mesh, in_specs=in_specs, out_specs=out_specs, check_vma=False,
    )
```

```python
import functools
import math

import jax
import jax.numpy as jnp
from jax import lax
from jax.experimental import pallas as pl
from jax.experimental.pallas import tpu as pltpu
from jax.sharding import PartitionSpec as P

masked_score = -1e30
vmem_bytes = 46 * 1024 * 1024
small_vmem_bytes = 8 * 1024 * 1024
early_steps = ()
f32 = jnp.float32
bf16 = jnp.bfloat16


def dot_nt(left, right):
    return lax.dot_general(left, right, (((1,), (1,)), ((), ())), preferred_element_type=f32)


def dot_nn(left, right):
    return lax.dot_general(left, right, (((1,), (0,)), ((), ())), preferred_element_type=f32)


def fold_rows(values, op):
    rows, columns = values.shape
    return op(values.reshape(rows // 8, 8, columns), axis=0)


def head_kernel(dp_size, heads_size, kv_index, kv_local, width, block_tokens, chunk, fine, sub, *refs):
    last = kv_index == kv_local - 1
    first = kv_index == 0
    if first:
        (q_ref, g_ref, sk_ref, sv_ref, ck_ref, cv_ref, seg_ref), refs = refs[:7], refs[7:]
    else:
        (keys_ref, vals_ref, keys_t_ref, q_rows, g_rows, seg_in), refs = refs[:6], refs[6:]
    held = kv_index if last else 0
    near_steps, far_steps = split_steps(heads_size)
    kept = len(near_steps)
    dq_before, refs = refs[: held * kept], refs[held * kept :]
    self_before, refs = refs[:held], refs[held:]
    (keep_ref, send_ref), refs = refs[:2], refs[2:]
    dq_outs, self_ref, refs = refs[:heads_size], refs[heads_size], refs[heads_size + 1 :]
    if first:
        others = range(1, kv_local)
        next_refs = {other: refs[5 * other - 5 : 5 * other] for other in others}
        refs = refs[5 * len(others) :]
        if kv_local > 1:
            seg_out, refs = refs[0], refs[1:]
        (
            keys_ref, vals_ref, keys_t_ref, q_in, g_in, sk_in, sv_in, ck_in, cv_in, seg_in, sems,
        ), refs = refs[:11], refs[11:]
    wide_ref, s_ref, w_ref, d_ref, p_ref, ds_ref, dk_ref, dv_ref, out_ref, dq_ref = refs
    all_keys, head_dim = keys_ref.shape
    tokens = seg_in.shape[1]
    cart_rows = all_keys - tokens
    rows = block_tokens * width
    scale = head_dim ** -0.5
    scale2 = scale * math.log2(math.e)
    span = block_tokens * kv_local * width
    blocks = tokens // block_tokens

    if first:

        def block_copy(source, target, block, sem):
            at = slice(block * span, (block + 1) * span)
            return pltpu.make_async_copy(source.at[at, :], target.at[at, :], sems.at[sem])

        copies = {
            name: pltpu.make_async_copy(source, target, sems.at[at])
            for at, (name, source, target) in enumerate(
                [("ck", ck_ref, ck_in), ("sk", sk_ref, sk_in), ("cv", cv_ref, cv_in), ("sv", sv_ref, sv_in)]
            )
        }
        for block in range(blocks):
            copies["q", block] = block_copy(q_ref, q_in, block, 4 + block)
            copies["g", block] = block_copy(g_ref, g_in, block, 4 + blocks + block)
        copies["seg"] = pltpu.make_async_copy(seg_ref, seg_in, sems.at[4 + 2 * blocks])
        order = ["ck", "sk", ("q", 0), "seg", "cv", "sv", ("g", 0)]
        order += [(kind, block) for block in range(1, blocks) for kind in ("q", "g")]
        for name in order:
            copies[name].start()

    def pick(name, ref, dst, at):
        copies[name].wait()
        count = ref.shape[0] // kv_local
        if kv_local == 1:
            dst[at : at + count, :] = ref[...]
        else:
            wide_ref[0 : ref.shape[0], :] = ref[...].astype(f32)
            dst[at : at + count, :] = wide_ref[pl.ds(0, count, stride=kv_local), :].astype(bf16)
            for other in others:
                next_ref = next_refs[other][0 if dst is keys_ref else 1]
                next_ref[at : at + count, :] = wide_ref[pl.ds(other, count, stride=kv_local), :].astype(bf16)

    def rows_of(name, block):
        at = slice(block * rows, (block + 1) * rows)
        if not first:
            return (q_rows if name == "q" else g_rows)[at, :]
        copies[name, block].wait()
        wide = (q_in if name == "q" else g_in)[block * span : (block + 1) * span, :]
        if kv_local == 1:
            return wide
        wide = wide.astype(f32).reshape(block_tokens, kv_local, width, head_dim)
        for other in others:
            next_refs[other][3 if name == "q" else 4][at, :] = wide[:, other].reshape(rows, head_dim).astype(bf16)
        return wide[:, 0].reshape(rows, head_dim).astype(bf16)

    if first:
        copies["seg"].wait()
        if kv_local > 1:
            seg_out[...] = seg_in[...]
    first_count = jnp.sum((seg_in[...] == 0).astype(f32), axis=1, keepdims=True).astype(jnp.int32)

    def limit(block):
        return -(-(block + 1) * block_tokens // fine) * fine

    def pieces(block):
        cart = [(start, chunk) for start in range(0, cart_rows, chunk)]
        return cart + [(cart_rows, limit(block))]

    queries, grads, peaks, stats = {}, {}, {}, {}
    acc = {}

    def spread(values):
        return jnp.concatenate([values] * (sub // 8), axis=0)

    def subs(start, size):
        return [slice(at, at + sub) for at in range(start, start + size, sub)]

    def open_scores(block):
        queries[block] = rows_of("q", block)
        token = (lax.broadcasted_iota(jnp.int32, (1, rows), 1) + block * rows) // width
        begin = jnp.where(token >= first_count, first_count, 0)
        acc["peak"] = jnp.full((8, rows), masked_score, f32)
        acc["token"], acc["begin"] = token, begin

    def step_scores(block, start, size):
        s_ref[block % 2, start : start + size, :] = dot_nt(keys_ref[start : start + size, :], queries[block])
        for at in subs(start, size):
            score = s_ref[block % 2, at, :]
            if start >= cart_rows:
                key_at = lax.broadcasted_iota(jnp.int32, (sub, rows), 0) + (at.start - cart_rows)
                score = jnp.where((key_at >= acc["begin"]) & (key_at <= acc["token"]), score, masked_score)
                s_ref[block % 2, at, :] = score
            acc["peak"] = jnp.maximum(acc["peak"], fold_rows(score, jnp.max))

    def close_scores(block):
        peaks[block] = jnp.broadcast_to(jnp.max(acc["peak"], axis=0, keepdims=True), (8, rows))

    def open_weights(block):
        grads[block] = rows_of("g", block)
        acc["total"] = jnp.zeros((8, rows), f32)
        acc["center"] = jnp.zeros((8, rows), f32)

    def step_weights(block, start, size):
        d_ref[block % 2, start : start + size, :] = dot_nt(vals_ref[start : start + size, :], grads[block])
        for at in subs(start, size):
            weight = jnp.exp2((s_ref[block % 2, at, :] - spread(peaks[block])) * scale2)
            w_ref[block % 2, at, :] = weight
            acc["total"] = acc["total"] + fold_rows(weight, jnp.sum)
            acc["center"] = acc["center"] + fold_rows(weight * d_ref[block % 2, at, :], jnp.sum)

    def close_weights(block):
        share = 1.0 / jnp.sum(acc["total"], axis=0, keepdims=True)
        center = jnp.sum(acc["center"], axis=0, keepdims=True) * share
        stats[block] = jnp.broadcast_to(share, (8, rows)), jnp.broadcast_to(center, (8, rows))

    def open_grads(block):
        pass

    def step_grads(block, start, size):
        slot = block % 2
        share, center = stats[block]
        for at in subs(start, size):
            prob = w_ref[slot, at, :] * spread(share)
            p_ref[slot, at, :] = prob.astype(bf16)
            ds_ref[slot, at, :] = (prob * (d_ref[slot, at, :] - spread(center))).astype(bf16)
        at = slice(start, start + size)
        old = size if start < cart_rows else (limit(block - 1) if block else 0)
        old = old if block else 0
        for ref, left, right in ((dv_ref, p_ref, grads[block]), (dk_ref, ds_ref, queries[block])):
            part = dot_nn(left[slot, at, :], right)
            if old:
                ref[start : start + old, :] += part[:old]
            if old < size:
                ref[start + old : start + size, :] = part[old:]

    def close_grads(block):
        seen = cart_rows + limit(block)
        dq_t = dot_nn(keys_t_ref[:, 0:seen], ds_ref[block % 2, 0:seen, :])
        out_ref[...] = (dq_t * scale).T
        for head in range(width):
            dq_ref[block * block_tokens : (block + 1) * block_tokens, head * head_dim : (head + 1) * head_dim] = (
                out_ref[pl.ds(head, block_tokens, stride=width), :].astype(bf16)
            )

    if first:
        pick("ck", ck_in, keys_ref, 0)
        pick("sk", sk_in, keys_ref, cart_rows)
    stages = (
        (2, open_grads, step_grads, close_grads),
        (1, open_weights, step_weights, close_weights),
        (0, open_scores, step_scores, close_scores),
    )
    for turn in range(blocks + 2):
        live = [(turn - lag, *calls) for lag, *calls in stages if 0 <= turn - lag < blocks]
        if turn == 1 and first:
            pick("cv", cv_in, vals_ref, 0)
            pick("sv", sv_in, vals_ref, cart_rows)
            keys_t_ref[...] = keys_ref[...].astype(f32).T.astype(bf16)
            for other in others:
                next_refs[other][2][...] = next_refs[other][0][...].astype(f32).T.astype(bf16)
        for block, begin_call, _, _ in live:
            begin_call(block)
        for index in range(len(pieces(0))):
            for block, _, step_call, _ in live:
                step_call(block, *pieces(block)[index])
        for block, _, _, end_call in live:
            end_call(block)

    part_rows = cart_rows // dp_size
    me = lax.axis_index("dp")
    for step in range(dp_size):
        at = pl.ds(pl.multiple_of((me ^ step) * part_rows, part_rows), part_rows)
        ref = send_ref if step % 2 else keep_ref
        ref[step // 2, 0] = (dk_ref[at, :] * scale).astype(ref.dtype)
        ref[step // 2, 1] = dv_ref[at, :].astype(ref.dtype)
    own = dk_ref[cart_rows:all_keys, :] * scale, dv_ref[cart_rows:all_keys, :]
    own_tokens = tokens // heads_size
    columns = width * head_dim
    me = lax.axis_index("heads")
    for place, (step, ref) in enumerate(zip(near_steps + far_steps, dq_outs)):
        target = me ^ step
        at = pl.ds(pl.multiple_of(target * own_tokens, own_tokens), own_tokens)
        if last and place < kept:
            for index in range(held):
                ref[:, index * columns : (index + 1) * columns] = dq_before[index * kept + place][...]
            ref[:, held * columns :] = dq_ref[at, :]
        else:
            ref[...] = dq_ref[at, :]
    if not last:
        self_ref[0], self_ref[1] = own
        return
    count = tokens * kv_local
    for kind in range(2):
        for index, before in enumerate(self_before):
            wide_ref[pl.ds(index, tokens, stride=kv_local), :] = before[kind]
        wide_ref[pl.ds(kv_index, tokens, stride=kv_local), :] = own[kind]
        self_ref[kind * count : (kind + 1) * count, :] = wide_ref[0:count, :].astype(bf16)


def fold_kernel(part_ref, got_ref, keep_ref, send_ref):
    for index in range(part_ref.shape[0]):
        total = part_ref[index] + got_ref[index].astype(f32)
        ref = send_ref if index % 2 else keep_ref
        ref[index // 2] = total.astype(ref.dtype)


def cart_kernel(kv_local, *refs):
    part_refs, got_refs, out_ref = refs[:kv_local], refs[kv_local:-1], refs[-1]
    part_rows = part_refs[0].shape[2]
    for kv_index in range(kv_local):
        for kind in range(2):
            total = part_refs[kv_index][0, kind] + got_refs[kv_index][0, kind].astype(f32)
            out_ref[pl.ds(kind * kv_local + kv_index, part_rows, stride=2 * kv_local), :] = total


def place_kernel(heads_size, kv_local, *refs):
    part_refs, out_ref, sems = refs[:-2], refs[-2], refs[-1]
    near_steps, far_steps = split_steps(heads_size)
    columns = out_ref.shape[1] // (heads_size * kv_local)
    me = lax.axis_index("heads")
    places = [(step, 0) for step in near_steps]
    places += [(step, kv_index) for kv_index in range(kv_local) for step in far_steps]
    copies = []
    for index, ((step, kv_index), ref) in enumerate(zip(places, part_refs)):
        source = me ^ step
        at = pl.multiple_of((source * kv_local + kv_index) * columns, columns)
        copies.append(pltpu.make_async_copy(ref, out_ref.at[:, pl.ds(at, ref.shape[1])], sems.at[index]))
    for copy in copies:
        copy.start()
    for copy in copies:
        copy.wait()


def swap(values, axis, size, step):
    if step == 0:
        return values
    return lax.ppermute(values, axis, [(source, source ^ step) for source in range(size)])


def fold(part, got):
    half = part.shape[0] // 2
    return pl.pallas_call(
        fold_kernel,
        out_shape=(
            jax.ShapeDtypeStruct((half, *part.shape[1:]), f32),
            jax.ShapeDtypeStruct((half, *part.shape[1:]), bf16),
        ),
        compiler_params=pltpu.CompilerParams(vmem_limit_bytes=small_vmem_bytes),
        cost_estimate=pl.CostEstimate(flops=2**20, bytes_accessed=2**20, transcendentals=0),
        name="cart_fold",
    )(part, got)


def split_steps(heads_size):
    early = [step for step in range(heads_size) if step in early_steps]
    late = [0, *range(2, heads_size), 1]
    return [step for step in late if step < heads_size and step not in early], early


def on_device(dp_size, heads_size, queries, out_grad, self_keys, self_values, cart_keys, cart_values, segment_ids):
    tokens, heads_local, head_dim = queries.shape
    kv_local = self_keys.shape[1]
    cart_rows = cart_keys.shape[0]
    width = heads_local // kv_local
    block_tokens = 64
    chunk = 1024
    fine = 128
    sub = 16
    all_keys = cart_rows + tokens
    rows = block_tokens * width
    part_rows = cart_rows // dp_size
    own_tokens = tokens // heads_size
    flat = [pltpu.with_memory_space_constraint(array.reshape(-1, head_dim), pltpu.HBM) for array in (queries, out_grad, self_keys, self_values, cart_keys, cart_values)]
    segments = pltpu.with_memory_space_constraint(segment_ids, pltpu.HBM)
    macs = tokens * width * all_keys * head_dim * 5
    blocks = tokens // block_tokens
    columns = width * head_dim
    count = tokens * kv_local
    near_steps, far_steps = split_steps(heads_size)
    kept = len(near_steps)
    anywhere = pl.BlockSpec(memory_space=pl.ANY)
    cart_list, kept_list, far_list, self_list, received = [], [], [], [], []
    for kv_index in range(kv_local):
        last = kv_index == kv_local - 1
        near = jax.ShapeDtypeStruct((own_tokens, kv_local * columns if last else columns), bf16)
        far = jax.ShapeDtypeStruct((own_tokens, columns), bf16)
        own_shape = (2 * count, head_dim) if last else (2, tokens, head_dim)
        other_shapes = [near] * kept + [far] * (heads_size - kept)
        other_shapes.append(jax.ShapeDtypeStruct(own_shape, bf16 if last else f32))
        next_shapes, first_scratch = [], []
        if kv_index == 0:
            key_like = jax.ShapeDtypeStruct((all_keys, head_dim), bf16)
            turned = jax.ShapeDtypeStruct((head_dim, all_keys), bf16)
            row_like = jax.ShapeDtypeStruct((tokens * width, head_dim), bf16)
            next_shapes = [key_like, key_like, turned, row_like, row_like] * (kv_local - 1)
            if kv_local > 1:
                next_shapes.append(jax.ShapeDtypeStruct(segment_ids.shape, jnp.int32))
            inputs = [*flat, segments]
            first_scratch = [
                pltpu.VMEM((all_keys, head_dim), bf16),
                pltpu.VMEM((all_keys, head_dim), bf16),
                pltpu.VMEM((head_dim, all_keys), bf16),
                *[pltpu.VMEM(array.shape, bf16) for array in flat],
                pltpu.VMEM(segment_ids.shape, jnp.int32),
                pltpu.SemaphoreType.DMA((5 + 2 * blocks,)),
            ]
        else:
            inputs = [*prepared[5 * kv_index - 5 : 5 * kv_index], prepared[-1]]
        before = kept_list + self_list if last else []
        outs = pl.pallas_call(
            functools.partial(head_kernel, dp_size, heads_size, kv_index, kv_local, width, block_tokens, chunk, fine, sub),
            out_shape=(
                jax.ShapeDtypeStruct((dp_size // 2, 2, part_rows, head_dim), f32),
                jax.ShapeDtypeStruct((dp_size // 2, 2, part_rows, head_dim), bf16),
                *other_shapes,
                *next_shapes,
            ),
            in_specs=[pl.BlockSpec(memory_space=pltpu.VMEM if kv_index else pltpu.HBM)] * len(inputs)
            + [pl.BlockSpec(memory_space=pltpu.VMEM)] * len(before),
            scratch_shapes=[
                *first_scratch,
                pltpu.VMEM((cart_rows * kv_local, head_dim), f32),
                pltpu.VMEM((2, all_keys, rows), f32),
                pltpu.VMEM((2, all_keys, rows), f32),
                pltpu.VMEM((2, all_keys, rows), f32),
                pltpu.VMEM((2, all_keys, rows), bf16),
                pltpu.VMEM((2, all_keys, rows), bf16),
                pltpu.VMEM((all_keys, head_dim), f32),
                pltpu.VMEM((all_keys, head_dim), f32),
                pltpu.VMEM((rows, head_dim), f32),
                pltpu.VMEM((tokens, columns), bf16),
            ],
            compiler_params=pltpu.CompilerParams(vmem_limit_bytes=vmem_bytes),
            cost_estimate=pl.CostEstimate(flops=4 * macs, bytes_accessed=5 * 2**20, transcendentals=tokens * width * all_keys),
            name="head_grads",
        )(*inputs, *before)
        if kv_index == 0:
            prepared = outs[len(outs) - len(next_shapes) :]
        outs = outs[: len(outs) - len(next_shapes)]
        part, send, near, far = outs[0], outs[1], outs[2 : 2 + kept], outs[2 + kept : -1]
        if last:
            part, send, near, far, received = lax.optimization_barrier((part, send, near, far, received))
        else:
            kept_list += near
            self_list.append(outs[-1])
        received.append((part, swap(send, "dp", dp_size, 1)))
        far_parts = [swap(block, "heads", heads_size, step) for step, block in zip(far_steps, far)]
        if not last:
            received[-1] += tuple(far_parts)
    far_list = [block for _, _, *blocks_far in received for block in blocks_far]
    for part, got, *_ in received:
        step = 2
        while step < dp_size:
            part, send = fold(part, got)
            got = swap(send, "dp", dp_size, step)
            step *= 2
        cart_list.append((part, got))
    query_list = [swap(block, "heads", heads_size, step) for step, block in zip(near_steps, near)] + far_list + far_parts
    query_grads = pl.pallas_call(
        functools.partial(place_kernel, heads_size, kv_local),
        out_shape=jax.ShapeDtypeStruct((own_tokens, heads_size * heads_local * head_dim), bf16),
        in_specs=[anywhere] * len(query_list),
        out_specs=anywhere,
        scratch_shapes=[pltpu.SemaphoreType.DMA((len(query_list),))],
        compiler_params=pltpu.CompilerParams(vmem_limit_bytes=small_vmem_bytes),
        cost_estimate=pl.CostEstimate(flops=2**20, bytes_accessed=2 * 2**20, transcendentals=0),
        name="place_queries",
    )(*query_list)
    cart_grads = pl.pallas_call(
        functools.partial(cart_kernel, kv_local),
        out_shape=jax.ShapeDtypeStruct((part_rows * 2 * kv_local, head_dim), f32),
        compiler_params=pltpu.CompilerParams(vmem_limit_bytes=small_vmem_bytes),
        cost_estimate=pl.CostEstimate(flops=2**20, bytes_accessed=2 * 2**20, transcendentals=0),
        name="cart_grads",
    )(*[part for part, _ in cart_list], *[got for _, got in cart_list])
    cart_grads = cart_grads.reshape(part_rows, 2, kv_local, head_dim)
    self_grads = outs[-1].reshape(2, tokens, kv_local, head_dim)
    return (cart_grads, self_grads, query_grads)


def solution(mesh):
    in_specs = (
        P(("groups", "dp"), "heads", None),
        P(("groups", "dp"), "heads", None),
        P(("groups", "dp"), "heads", None),
        P(("groups", "dp"), "heads", None),
        P("groups", "heads", None),
        P("groups", "heads", None),
        P(("groups", "dp"), None),
    )
    out_specs = (
        P(("groups", "dp"), None, "heads", None),
        P(None, ("groups", "dp"), "heads", None),
        P(("groups", "dp", "heads"), None),
    )
    return jax.shard_map(
        functools.partial(on_device, mesh.shape["dp"], mesh.shape["heads"]),
        mesh=mesh, in_specs=in_specs, out_specs=out_specs, check_vma=False,
    )
```
